512 devices in a mesh: gx: 32 (over y, x), gy: 16 (over z, core).
Axes of the slice: x: 4, y: 8, z: 8, core: 2. Of those that a mesh axis runs over, the one named last changes fastest.
Arguments:
- pressure: float32 [5, 1024, 2048], P(None, 'gx', 'gy'), may hold values from -4 to -0.05
- newton_rhs: float32 [5, 1024, 2048], P(None, 'gx', 'gy'), may hold values from -6 to 6
- geology: int32 [5, 1024, 2048], P(None, 'gx', 'gy'), may hold values from 0 to 15
- saturated_conductivity: float32 [16], replicated, may hold values from 0.1 to 10
- genuchten_alpha: float32 [16], replicated, may hold values from 0.5 to 4
- genuchten_exponent: float32 [16], replicated, may hold values from 1.5 to 3
- land_mask: int32 [1024, 2048], P('gx', 'gy'), may hold values from 0 to 1, as said below
- ponding: float32 [1024, 2048], P('gx', 'gy'), may hold values from 0.01 to 0.3
- slope_class: int32 [1024, 2048], P('gx', 'gy'), may hold values from 0 to 7
- slope_table: float32 [8], replicated, may hold values from 0.001 to 0.05
- flow_direction: int32 [1024, 2048], P('gx', 'gy'), may hold values from 0 to 1
- soil_class: int32 [1024, 2048], P('gx', 'gy'), may hold values from 0 to 11
- soil_inverse: float32 [12, 20, 20], replicated, may hold values from -2 to 2
- soil_state: float32 [20, 1024, 2048], P(None, 'gx', 'gy'), may hold values from -6 to 6
Outputs:
- correction: float32 [5, 1024, 2048], P(None, 'gx', 'gy')
- ponding_next: float32 [1024, 2048], P('gx', 'gy')
- soil_next: float32 [20, 1024, 2048], P(None, 'gx', 'gy')
The draws below stay inside these ranges and needn't reach their ends.
Inputs may be any that keep to these rules, and one draw needn't show every extreme that they name: `land_mask`: land shares differ strongly between aligned 8 x 8 blocks of columns, from all sea to all land.
All inputs are finite; a program needn't handle non-finite values.
Results may differ from the reference program's by a relative error of at most 0.0001.
Values sent between devices are 32-bit elements; how exact they have to be, the bound alone decides.
No kernel may reach another device: no remote copies, remote signals or barrier semaphores. Data moves between devices by JAX's collectives and lax.ppermute only.
A program may use at most 64 MiB of HBM per device.

```python
import math
import jax
import jax.numpy as jnp
from jax import lax

LAYERS = 5
STATE = 20
ITERS = 3
GEOLOGY = 16
SOIL_CLASSES = 12
SLOPES = 8
NX = 1024
NY = 2048


def draw_land_mask(key, part):
    key = jax.random.fold_in(key, 11)
    level_key, cell_key = jax.random.split(key)
    level = jax.random.randint(level_key, (NX // 8, NY // 8), 0, 5)
    spread = jnp.repeat(jnp.repeat(level, 8, axis=0), 8, axis=1)
    cell = jax.random.randint(cell_key, (NX, NY), 0, 4)
    return (cell < spread).astype(jnp.int32)


def draw_soil_inverse(key, part):
    key = jax.random.fold_in(key, 23)
    noise = jax.random.normal(key, (SOIL_CLASSES, STATE, STATE), jnp.float32)
    noise = jnp.clip(noise, -3.0, 3.0)
    spread = 0.4 / STATE ** 0.5
    return 0.8 * jnp.eye(STATE, dtype=jnp.float32)[None] + spread * noise


def with_ends(result, rng, low, high):
    dims = result.shape
    place = [jax.random.randint(jax.random.fold_in(rng, axis), (), 0, dims[axis]) for axis in range(len(dims))]
    result = result.at[tuple(place)].set(low)
    longest = dims.index(max(dims))
    place[longest] = (place[longest] + 1) % dims[longest]
    return result.at[tuple(place)].set(high)


def block_levels(own_key, extent, cuts, least, largest):
    def one(dim, blocks):
        heights = jax.random.uniform(jax.random.fold_in(jax.random.fold_in(own_key, 6), dim), (blocks,), jnp.float32, least / len(cuts), largest / len(cuts))
        return jnp.repeat(jnp.exp(heights), extent[dim] // blocks).reshape((-1,) + (1,) * (len(extent) - dim - 1))

    factor_of = one(*cuts[0])
    for cut in cuts[1:]:
        factor_of = factor_of * one(*cut)
    return factor_of


def normal_values(stream_key, extent, deviation, bound, cuts=(), kind=jnp.bfloat16):
    entries = deviation * jax.random.normal(stream_key, extent, jnp.float32)
    if cuts:
        entries = entries * block_levels(stream_key, extent, cuts, -0.22, 0.18)
    return jnp.clip(entries, -bound, bound).astype(kind)


def setup_inputs(seed: int = 0) -> dict:
    streams_of = jax.random.split(jax.random.key(seed), 15)
    pressure = jnp.clip(-4.0 + 3.95 * jax.random.uniform(streams_of[0], (LAYERS, NX, NY), jnp.float32) ** block_levels(streams_of[0], (LAYERS, NX, NY), ((1, 32), (2, 16)), -0.2, 0.2), -4.0, -0.05)
    newton_rhs = normal_values(streams_of[1], (LAYERS, NX, NY), 1.0, 6.0, ((1, 32), (2, 16)), jnp.float32)
    geology = with_ends(jax.random.randint(streams_of[2], (LAYERS, NX, NY), 0, GEOLOGY), jax.random.fold_in(streams_of[2], 1), 0, GEOLOGY - 1).astype(jnp.int32)
    saturated_conductivity = jnp.clip(jnp.exp(jax.random.uniform(streams_of[3], (GEOLOGY,), jnp.float32, math.log(0.1), math.log(10.0))), 0.1, 10.0)
    genuchten_alpha = jnp.clip(jnp.exp(jax.random.uniform(streams_of[4], (GEOLOGY,), jnp.float32, math.log(0.5), math.log(4.0))), 0.5, 4.0)
    genuchten_exponent = jnp.clip(jax.random.uniform(streams_of[5], (GEOLOGY,), jnp.float32, 1.5, 3.0), 1.5, 3.0)
    land_mask = draw_land_mask(jax.random.fold_in(streams_of[14], 71), 0)
    ponding = jnp.clip(0.01 + 0.29000001 * jax.random.uniform(streams_of[7], (NX, NY), jnp.float32) ** block_levels(streams_of[7], (NX, NY), ((0, 32), (1, 16)), -0.2, 0.2), 0.01, 0.3)
    slope_class = with_ends(jax.random.randint(streams_of[8], (NX, NY), 0, SLOPES), jax.random.fold_in(streams_of[8], 1), 0, SLOPES - 1).astype(jnp.int32)
    slope_table = jnp.clip(jnp.exp(jax.random.uniform(streams_of[9], (SLOPES,), jnp.float32, math.log(0.001), math.log(0.05))), 0.001, 0.05)
    flow_direction = with_ends(jax.random.randint(streams_of[10], (NX, NY), 0, 2), jax.random.fold_in(streams_of[10], 1), 0, 1).astype(jnp.int32)
    soil_class = with_ends(jax.random.randint(streams_of[11], (NX, NY), 0, SOIL_CLASSES), jax.random.fold_in(streams_of[11], 1), 0, SOIL_CLASSES - 1).astype(jnp.int32)
    soil_inverse = draw_soil_inverse(jax.random.fold_in(streams_of[14], 71), 0)
    soil_state = normal_values(streams_of[13], (STATE, NX, NY), 1.0, 6.0, ((1, 32), (2, 16)), jnp.float32)
    return {"pressure": pressure, "newton_rhs": newton_rhs, "geology": geology, "saturated_conductivity": saturated_conductivity, "genuchten_alpha": genuchten_alpha, "genuchten_exponent": genuchten_exponent, "land_mask": land_mask, "ponding": ponding, "slope_class": slope_class, "slope_table": slope_table, "flow_direction": flow_direction, "soil_class": soil_class, "soil_inverse": soil_inverse, "soil_state": soil_state}


def lookup(table, index):
    total = jnp.zeros(index.shape, jnp.float32)
    for entry in range(table.shape[0]):
        total = jnp.where(index == entry, table[entry], total)
    return total

def harmonic(first, second):
    return 2.0 * first * second / (first + second)

def hydraulics(pressure, geology, saturated_conductivity, genuchten_alpha, genuchten_exponent):
    alpha_cell = lookup(genuchten_alpha, geology)
    exponent = lookup(genuchten_exponent, geology)
    base_cond = lookup(saturated_conductivity, geology)
    shape_m = 1.0 - 1.0 / exponent
    scaled = alpha_cell * jnp.abs(pressure)
    powered = jnp.power(scaled, exponent)
    conductivity = base_cond * jnp.power(1.0 + powered, -shape_m)
    capacity = 0.05 + 0.4 * shape_m * exponent * alpha_cell * jnp.power(scaled, exponent - 1.0) * jnp.power(1.0 + powered, -shape_m - 1.0)
    return (conductivity, capacity)

def face_terms(padded_cond):
    center = padded_cond[1:-1, 1:-1, 1:-1]
    return (harmonic(center, padded_cond[1:-1, :-2, 1:-1]), harmonic(center, padded_cond[1:-1, 2:, 1:-1]), harmonic(center, padded_cond[1:-1, 1:-1, :-2]), harmonic(center, padded_cond[1:-1, 1:-1, 2:]), harmonic(center, padded_cond[:-2, 1:-1, 1:-1]), harmonic(center, padded_cond[2:, 1:-1, 1:-1]))

def apply_operator(padded, faces, diagonal):
    field = padded[1:-1, 1:-1, 1:-1]
    beside = faces[0] * padded[1:-1, :-2, 1:-1] + faces[1] * padded[1:-1, 2:, 1:-1]
    beside = beside + faces[2] * padded[1:-1, 1:-1, :-2] + faces[3] * padded[1:-1, 1:-1, 2:]
    beside = beside + faces[4] * padded[:-2, 1:-1, 1:-1] + faces[5] * padded[2:, 1:-1, 1:-1]
    return diagonal * field - beside

def overland(ponding, slope_class, slope_table, flow_direction, land):
    outflow = jnp.sqrt(lookup(slope_table, slope_class)) / 0.03 * jnp.power(ponding, 5.0 / 3.0)
    eastward = jnp.where(flow_direction == 0, outflow, 0.0)
    southward = outflow - eastward
    inflow = jnp.pad(eastward, ((1, 0), (0, 0)))[:-1, :] + jnp.pad(southward, ((0, 0), (1, 0)))[:, :-1]
    return land * (ponding + 0.2 * (inflow - outflow))

def soil_solve(soil_state, ponding_next, top_correction, soil_class, soil_inverse, land_mask):
    forcing = soil_state.at[0].add(0.5 * ponding_next)
    forcing = forcing.at[1].add(0.5 * top_correction)
    solved = jnp.zeros_like(soil_state)
    for entry in range(soil_inverse.shape[0]):
        product = jnp.einsum('ij,jxy->ixy', soil_inverse[entry], forcing, precision=lax.Precision.HIGHEST)
        solved = jnp.where((soil_class == entry)[None], product, solved)
    return jnp.where((land_mask == 1)[None], solved, soil_state)

def reference(pressure, newton_rhs, geology, saturated_conductivity, genuchten_alpha, genuchten_exponent, land_mask, ponding, slope_class, slope_table, flow_direction, soil_class, soil_inverse, soil_state):
    land = land_mask.astype(jnp.float32)
    conductivity, capacity = hydraulics(pressure, geology, saturated_conductivity, genuchten_alpha, genuchten_exponent)
    faces = face_terms(jnp.pad(conductivity, 1))
    diagonal = capacity + 4.0 * (1.0 - land)[None] + faces[0] + faces[1] + faces[2] + faces[3] + faces[4] + faces[5]
    correction = jnp.zeros_like(newton_rhs)
    residual = newton_rhs
    direction = newton_rhs
    norm_now = jnp.sum(residual * residual)
    for step in range(ITERS):
        image = apply_operator(jnp.pad(direction, 1), faces, diagonal)
        alpha = norm_now / jnp.sum(direction * image)
        correction = correction + alpha * direction
        residual = residual - alpha * image
        norm_next = jnp.sum(residual * residual)
        direction = residual + norm_next / norm_now * direction
        norm_now = norm_next
    ponding_next = overland(ponding, slope_class, slope_table, flow_direction, land)
    soil_next = soil_solve(soil_state, ponding_next, correction[0], soil_class, soil_inverse, land_mask)
    return (correction, ponding_next, soil_next)
```

```python
import jax
import jax.numpy as jnp
from jax import lax
from jax.experimental import pallas as pl
from jax.experimental.pallas import tpu as pltpu
from jax.sharding import PartitionSpec as P


LAYERS = 5
STATE = 20
W = 3
X, Y = 32, 128
E = X + 8
FIELDS = 3 * LAYERS
G = 2 * W
SLAB = 48
F32 = jnp.float32


def two_sum(a, b):
    s = a + b
    t = s - a
    return s, (a - (s - t)) + (b - t)


def renorm(a, b):
    s = a + b
    return s, b - (s - a)


def halves(a):
    t = a * 4097.0
    hi = t - (t - a)
    return hi, a - hi


def two_prod(a, b):
    p = a * b
    (ah, al), (bh, bl) = halves(a), halves(b)
    return p, ((ah * bh - p) + ah * bl + al * bh) + al * bl


def pair_add(a, b):
    s, e = two_sum(a[0], b[0])
    return renorm(s, e + (a[1] + b[1]))


def pair_sub(a, b):
    return pair_add(a, (-b[0], -b[1]))


def pair_mul(a, b):
    p, e = two_prod(a[0], b[0])
    return renorm(p, e + (a[0] * b[1] + a[1] * b[0]))


def pair_div(a, b):
    q = a[0] / b[0]
    r = pair_sub(a, pair_mul((q, jnp.zeros_like(q)), b))
    q2 = r[0] / b[0]
    r = pair_sub(r, pair_mul((q2, jnp.zeros_like(q)), b))
    return pair_add(renorm(q, q2), (r[0] / b[0], jnp.zeros_like(q)))


def iota(shape, dim):
    return lax.broadcasted_iota(jnp.int32, shape, dim)


def pick(table, index):
    row = jnp.broadcast_to(table, index.shape)
    return jnp.take_along_axis(row, index, axis=1, mode="promise_in_bounds")


def call(kernel, outs, scratch=(), flops=0, nbytes=0, vmem=32):
    return pl.pallas_call(
        kernel,
        out_shape=[jax.ShapeDtypeStruct(s, F32) for s in outs],
        scratch_shapes=scratch,
        compiler_params=pltpu.CompilerParams(vmem_limit_bytes=vmem * 2**20),
        cost_estimate=pl.CostEstimate(
            flops=flops, bytes_accessed=nbytes, transcendentals=0
        ),
    )


def local_kernel(
    pressure, rhs, geology, ks, alpha, expo, land, ponding, slope_class, slope,
    flow, cond, diag, up, down, east, south, tab,
):
    for row, ref in enumerate((ks, alpha, expo)):
        tab[row : row + 1, 0:16] = ref[...]
    tab[3:4, 0:8] = slope[...]
    t_ks = tab[0:1, :]
    t_la = jnp.log(tab[1:2, :])
    t_n = tab[2:3, :]
    t_m = 1.0 - 1.0 / t_n
    t_slope = jnp.sqrt(tab[3:4, :]) / 0.03
    sea = 4.0 * (1.0 - land[...].astype(F32))
    for l in range(LAYERS):
        g = geology[l]
        p = jnp.abs(pressure[l])
        n = pick(t_n, g)
        m = pick(t_m, g)
        t = jnp.exp(n * (pick(t_la, g) + jnp.log(p)))
        one_t = 1.0 + t
        e = jnp.exp(-m * jnp.log(one_t))
        k = pick(t_ks, g) * e
        d = 0.05 + 0.4 * m * n * t * e / (p * one_t) + sea
        cond[l] = k
        diag[l] = d
        for f, x in enumerate((rhs[l], k, d)):
            q = (f * LAYERS + l) * W
            up[q : q + W, :] = x[0:W]
            down[q : q + W, :] = x[X - W : X]
    out = pick(t_slope, slope_class[...]) * jnp.exp((5.0 / 3.0) * jnp.log(ponding[...]))
    eastward = jnp.where(flow[...] == 0, out, 0.0)
    east[...] = eastward
    south[...] = out - eastward
    up[45:48, :] = jnp.zeros((3, Y), F32)
    down[45:46, :] = eastward[X - 1 : X]
    down[46:48, :] = jnp.zeros((2, Y), F32)


def pack_kernel(rhs, cond, diag, before, after, south, ext, packed):
    lane = iota((E, Y), 1)
    q_all = jnp.zeros((E, Y), F32)
    for f, ref in enumerate((rhs, cond, diag)):
        for l in range(LAYERS):
            q = f * LAYERS + l
            ext[q, 0:X, :] = ref[l]
            ext[q, X : X + W, :] = after[q * W : q * W + W, :]
            ext[q, X + W : E - W, :] = jnp.zeros((E - X - 2 * W, Y), F32)
            ext[q, E - W : E, :] = before[q * W : q * W + W, :]
            x = pltpu.roll(ext[q], (W + G * q) % Y, 1)
            q_all = jnp.where((lane >= G * q) & (lane < G * q + G), x, q_all)
    q = FIELDS
    packed[...] = q_all
    x = pltpu.roll(south[...], (W + G * q) % Y, 1)
    ln = iota((X, Y), 1)
    packed[0:X, :] = jnp.where((ln >= G * q) & (ln < G * q + G), x, q_all[0:X])


def krylov_kernel(
    ext, right, left, before, east, south, ponding, land,
    v1_out, v2_out, row_out, pond_out, fr, fc, fv, dd, v,
):
    lane = iota((E, Y), 1)
    first, last = lane == 0, lane == Y - 1

    def turn(m, h, by, edge):
        m, h = pltpu.roll(m, by, 1), pltpu.roll(h, by, 1)
        return jnp.where(edge, h, m), jnp.where(edge, m, h)

    w = jnp.where(lane % G >= W, right[...], left[...])

    def halo(q):
        return pltpu.roll(w, (-(W + G * q)) % Y, 1)

    def harmonic(a, b):
        return 2.0 * a * b / jnp.maximum(a + b, 1e-30)

    above = None
    for l in range(LAYERS):
        v[0, l], v[1, l] = ext[l], halo(l)
        k = ext[LAYERS + l], halo(LAYERS + l)
        dd[0, l], dd[1, l] = ext[2 * LAYERS + l], halo(2 * LAYERS + l)
        west = turn(*k, 1, first)
        for s in range(2):
            fr[s, l] = harmonic(k[s], pltpu.roll(k[s], 1, 0))
            fc[s, l] = harmonic(k[s], west[s])
            if l:
                fv[s, l - 1] = harmonic(k[s], above[s])
        above = k

    def product(l, flux_above):
        vm, vh = v[0, l], v[1, l]
        west = turn(vm, vh, 1, first)
        side = fc[0, l] * (vm - west[0]), fc[1, l] * (vh - west[1])
        gone = turn(*side, Y - 1, last)
        outs, flux = [], []
        for s, x in enumerate((vm, vh)):
            rows = fr[s, l] * (x - pltpu.roll(x, 1, 0))
            r = dd[s, l] * x + (rows - pltpu.roll(rows, E - 1, 0)) + (side[s] - gone[s])
            if l:
                r = r - flux_above[s]
            if l < LAYERS - 1:
                fl = fv[s, l] * (x - v[s, l + 1])
                r = r + fl
                flux.append(fl)
            outs.append(r)
        return outs, flux

    zero = jnp.zeros((8, Y), F32)
    sums = [(zero, zero)] * 6

    def add_to(j, a, b):
        for i in range(0, X, 8):
            p, e = two_prod(a[i : i + 8], b[i : i + 8])
            s, e2 = two_sum(sums[j][0], p)
            sums[j] = s, sums[j][1] + (e + e2)

    for step in range(3):
        results, flux = [], None
        for l in range(LAYERS):
            outs, flux = product(l, flux)
            old, new = v[0, l][0:X], outs[0][0:X]
            add_to(2 * step, old, old)
            add_to(2 * step + 1, old, new)
            results.append(outs)
        if step < 2:
            for l in range(LAYERS):
                v[0, l], v[1, l] = results[l]
                (v1_out, v2_out)[step][l] = results[l][0][0:X]

    sub = iota((8, Y), 0)
    ln = iota((8, Y), 1)
    total = zero, zero
    for j in range(6):
        s = renorm(*sums[j])
        for by in (4, 2, 1):
            s = pair_add(s, tuple(pltpu.roll(t, by, 0) for t in s))
        total = tuple(jnp.where(sub == j, a, b) for a, b in zip(s, total))
    for by in (64, 32, 16, 8, 4, 2, 1):
        total = pair_add(total, tuple(pltpu.roll(t, by, 1) for t in total))
    row = jnp.where(ln == sub, total[0], jnp.where(ln == sub + 8, total[1], 0.0))
    row = jnp.sum(row, axis=0, keepdims=True)
    row_out[...] = jnp.broadcast_to(row, row_out.shape)

    es, so = east[...], south[...]
    north = pltpu.roll(w, (-(W + G * FIELDS)) % Y, 1)[0:X]
    x_row, x_lane = iota((X, Y), 0), iota((X, Y), 1)
    inflow = jnp.where(x_row == 0, before[45:46, :], pltpu.roll(es, 1, 0)) + jnp.where(
        x_lane == 0, pltpu.roll(north, 1, 1), pltpu.roll(so, 1, 1)
    )
    pond_out[...] = land[...].astype(F32) * (ponding[...] + 0.2 * (inflow - (es + so)))


def rows_total(ref):
    parts = [
        (ref[i : i + 8, :], pltpu.roll(ref[i : i + 8, :], Y - 8, 1))
        for i in range(0, ref.shape[0], 8)
    ]
    while len(parts) > 1:
        parts = [pair_add(a, b) for a, b in zip(parts[::2], parts[1::2])]
    s = parts[0]
    for by in (4, 2, 1):
        s = pair_add(s, tuple(pltpu.roll(t, by, 0) for t in s))
    return s


def relay_kernel(rows, row_out):
    hi, lo = rows_total(rows)
    ln = iota((8, Y), 1)
    both = jnp.where(ln < 8, hi, pltpu.roll(lo, 8, 1))
    for i in range(0, row_out.shape[0], 8):
        row_out[i : i + 8, :] = both


def soil_kernel(state, soil_class, land, table, out):
    index = soil_class[...]
    on_land = land[...] == 1

    def one(i, carry):
        total = None
        for j in range(STATE):
            term = pick(table[pl.ds(j * STATE + i, 1), :], index) * state[j]
            total = term if total is None else total + term
        out[i] = jnp.where(on_land, total, state[i])
        return carry

    lax.fori_loop(0, STATE, one, 0)


def final_kernel(
    rows, rhs, v1, v2, base, pond, soil_class, land, table, corr_out, soil_out
):
    hi, lo = rows_total(rows)
    mu = [
        tuple(jnp.broadcast_to(t[:, j : j + 1], (8, Y)) for t in (hi, lo))
        for j in range(6)
    ]
    l21 = pair_div(mu[2], mu[1])
    l31 = pair_div(mu[3], mu[1])
    d2 = pair_sub(mu[3], pair_mul(l21, mu[2]))
    u = pair_sub(mu[4], pair_mul(l31, mu[2]))
    l32 = pair_div(u, d2)
    d3 = pair_sub(pair_sub(mu[5], pair_mul(l31, mu[3])), pair_mul(l32, u))
    y2 = pair_sub(mu[1], pair_mul(l21, mu[0]))
    y3 = pair_sub(pair_sub(mu[2], pair_mul(l31, mu[0])), pair_mul(l32, y2))
    c3 = pair_div(y3, d3)
    c2 = pair_sub(pair_div(y2, d2), pair_mul(l32, c3))
    c1 = pair_sub(
        pair_sub(pair_div(mu[0], mu[1]), pair_mul(l21, c2)), pair_mul(l31, c3)
    )
    c1, c2, c3 = (jnp.concatenate([c[0]] * (X // 8), axis=0) for c in (c1, c2, c3))
    top = None
    for l in range(LAYERS):
        x = c1 * rhs[l] + c2 * v1[l] + c3 * v2[l]
        corr_out[l] = x
        top = x if top is None else top
    half = 0.5 * land[...].astype(F32)
    water = half * pond[...]
    head = half * top
    index = soil_class[...]
    for i in range(STATE):
        soil_out[i] = (
            base[i]
            + pick(table[i : i + 1, :], index) * water
            + pick(table[STATE + i : STATE + i + 1, :], index) * head
        )


def both_ways(to_next, to_previous, axis):
    count = lax.axis_size(axis)
    forth = [(i, i + 1) for i in range(count - 1)]
    back = [(i + 1, i) for i in range(count - 1)]
    return lax.ppermute(to_next, axis, forth), lax.ppermute(to_previous, axis, back)


def everyones(rows, axis):
    count = lax.axis_size(axis)
    return lax.all_to_all(rows.reshape(count, 1, Y), axis, 0, 0).reshape(count, Y)


def on_device(
    pressure, newton_rhs, geology, saturated_conductivity, genuchten_alpha,
    genuchten_exponent, land_mask, ponding, slope_class, slope_table,
    flow_direction, soil_class, soil_inverse, soil_state,
):
    block, plane = (LAYERS, X, Y), (X, Y)
    cond, diag, up, down, east, south = call(
        local_kernel,
        [block, block, (SLAB, Y), (SLAB, Y), plane, plane],
        [pltpu.VMEM((8, Y), F32)],
    )(
        pressure, newton_rhs, geology, saturated_conductivity[None],
        genuchten_alpha[None], genuchten_exponent[None], land_mask, ponding,
        slope_class, slope_table[None], flow_direction,
    )
    before, after = both_ways(down, up, "gx")
    ext, packed = call(pack_kernel, [(FIELDS, E, Y), (E, Y)])(
        newton_rhs, cond, diag, before, after, south
    )
    left, right = both_ways(packed, packed, "gy")
    table = jnp.pad(
        soil_inverse.transpose(2, 1, 0).reshape(STATE * STATE, -1),
        ((0, 0), (0, Y - soil_inverse.shape[0])),
    )
    (base,) = call(soil_kernel, [(STATE, X, Y)], flops=20_000_000, nbytes=2_000_000)(
        soil_state, soil_class, land_mask, table
    )
    v1, v2, rows, pond = call(
        krylov_kernel,
        [block, block, (lax.axis_size("gx"), Y), plane],
        [pltpu.VMEM((2, n, E, Y), F32) for n in (5, 5, 4, 5, 5)],
    )(ext, right, left, before, east, south, ponding, land_mask)
    rows = everyones(rows, "gx")
    (rows,) = call(relay_kernel, [(lax.axis_size("gy"), Y)])(rows)
    rows = everyones(rows, "gy")
    correction, soil_next = call(final_kernel, [block, (STATE, X, Y)])(
        rows, newton_rhs, v1, v2, base, pond, soil_class, land_mask, table[: 2 * STATE]
    )
    return correction, pond, soil_next


def solution(mesh):
    cells, plane, rest = P(None, "gx", "gy"), P("gx", "gy"), P()
    return jax.shard_map(
        on_device,
        mesh=mesh,
        in_specs=(
            cells, cells, cells, rest, rest, rest, plane, plane, plane, rest, plane,
            plane, rest, cells,
        ),
        out_specs=(cells, plane, cells),
        check_vma=False,
    )
```

```python
import jax
import jax.numpy as jnp
from jax import lax
from jax.experimental import pallas as pl
from jax.experimental.pallas import tpu as pltpu
from jax.sharding import PartitionSpec as P


LAYERS = 5
STATE = 20
CLASSES = 12
W = 3
X, Y = 32, 128
E = X + 8
FIELDS = 3 * LAYERS
G = 2 * W
PAD = 24
F32 = jnp.float32


def two_sum(a, b):
    s = a + b
    t = s - a
    return s, (a - (s - t)) + (b - t)


def renorm(a, b):
    s = a + b
    return s, b - (s - a)


def halves(a):
    t = a * 4097.0
    hi = t - (t - a)
    return hi, a - hi


def two_prod(a, b):
    p = a * b
    (ah, al), (bh, bl) = halves(a), halves(b)
    return p, ((ah * bh - p) + ah * bl + al * bh) + al * bl


def pair_add(a, b):
    s, e = two_sum(a[0], b[0])
    return renorm(s, e + (a[1] + b[1]))


def pair_sub(a, b):
    return pair_add(a, (-b[0], -b[1]))


def pair_mul(a, b):
    p, e = two_prod(a[0], b[0])
    return renorm(p, e + (a[0] * b[1] + a[1] * b[0]))


def pair_div(a, b):
    q = a[0] / b[0]
    r = pair_sub(a, pair_mul((q, jnp.zeros_like(q)), b))
    q2 = r[0] / b[0]
    r = pair_sub(r, pair_mul((q2, jnp.zeros_like(q)), b))
    return pair_add(renorm(q, q2), (r[0] / b[0], jnp.zeros_like(q)))


def iota(shape, dim):
    return lax.broadcasted_iota(jnp.int32, shape, dim)


def pick(table, index):
    row = jnp.broadcast_to(table, index.shape)
    return jnp.take_along_axis(row, index, axis=1, mode="promise_in_bounds")


def call(kernel, outs, scratch=(), specs=None, flops=0, nbytes=0):
    extra = {} if specs is None else {"in_specs": specs}
    return pl.pallas_call(
        kernel,
        out_shape=[jax.ShapeDtypeStruct(s, F32) for s in outs],
        scratch_shapes=scratch,
        compiler_params=pltpu.CompilerParams(vmem_limit_bytes=32 * 2**20),
        cost_estimate=pl.CostEstimate(
            flops=flops, bytes_accessed=nbytes, transcendentals=0
        ),
        **extra,
    )


def gather_table(ref, count):
    lane = iota((1, Y), 1)
    row = jnp.full((1, Y), 1.0, F32)
    for i in range(count):
        row = jnp.where(lane == i, ref[i], row)
    return row


def local_kernel(*refs):
    (cond, diag, slab, east, south), held, sem = refs[11:16], refs[16:27], refs[27]
    copies = [
        pltpu.make_async_copy(refs[i], held[i], sem.at[i]) for i in range(11)
    ]
    for copy in copies:
        copy.start()
    for copy in copies:
        copy.wait()
    (pressure, rhs, geology, ks, alpha, expo, land, ponding, slope_class, slope, flow) = held
    t_ks = gather_table(ks, 16)
    t_la = jnp.log(gather_table(alpha, 16))
    t_n = gather_table(expo, 16)
    t_m = 1.0 - 1.0 / t_n
    t_slope = jnp.sqrt(gather_table(slope, 8)) / 0.03
    sea = 4.0 * (1.0 - land[...].astype(F32))
    for l in range(LAYERS):
        g = geology[l]
        p = jnp.abs(pressure[l])
        n = pick(t_n, g)
        m = pick(t_m, g)
        t = jnp.exp(n * (pick(t_la, g) + jnp.log(p)))
        one_t = 1.0 + t
        e = jnp.exp(-m * jnp.log(one_t))
        k = pick(t_ks, g) * e
        d = 0.05 + 0.4 * m * n * t * e / (p * one_t) + sea
        cond[l] = k
        diag[l] = d
        for f, x in enumerate((rhs[l], k, d)):
            slab[f * LAYERS + l] = x[0 : E - X]
    out = pick(t_slope, slope_class[...]) * jnp.exp((5.0 / 3.0) * jnp.log(ponding[...]))
    eastward = jnp.where(flow[...] == 0, out, 0.0)
    east[...] = eastward
    south[...] = out - eastward


def pack_kernel(rhs, cond, diag, after, south, packed):
    for lo, rows in ((0, X), (X, E - X)):
        lane = iota((rows, Y), 1)
        total = jnp.zeros((rows, Y), F32)
        for f, ref in enumerate((rhs, cond, diag)):
            for l in range(LAYERS):
                q = f * LAYERS + l
                x = pltpu.roll(after[q] if lo else ref[l], (W + G * q) % Y, 1)
                total = jnp.where((lane >= G * q) & (lane < G * q + G), x, total)
        if not lo:
            x = pltpu.roll(south[...], (W + G * FIELDS) % Y, 1)
            total = jnp.where(lane >= G * FIELDS, x, total)
        packed[lo : lo + rows, :] = total


def krylov_kernel(
    rhs, cond, diag, after, right, left, east, v1_out, v2_out, row_out, back_out,
    fr, fc, fv, dd, v,
):
    lane, row_of = iota((E, Y), 1), iota((E, Y), 0)
    first, last = lane == 0, lane == Y - 1

    def turn(m, h, by, edge):
        m, h = pltpu.roll(m, by, 1), pltpu.roll(h, by, 1)
        return jnp.where(edge, h, m), jnp.where(edge, m, h)

    w = jnp.where(lane % G >= W, right[...], left[...])

    def both(ref, f, l):
        q = f * LAYERS + l
        return (
            jnp.concatenate([ref[l], after[q]], axis=0),
            pltpu.roll(w, (-(W + G * q)) % Y, 1),
        )

    def harmonic(a, b):
        return 2.0 * a * b / jnp.maximum(a + b, 1e-30)

    above = None
    for l in range(LAYERS):
        v[0, l], v[1, l] = both(rhs, 0, l)
        k = both(cond, 1, l)
        dd[0, l], dd[1, l] = both(diag, 2, l)
        west = turn(*k, 1, first)
        for s in range(2):
            fr[s, l] = jnp.where(row_of == 0, 0.0, harmonic(k[s], pltpu.roll(k[s], 1, 0)))
            fc[s, l] = harmonic(k[s], west[s])
            if l:
                fv[s, l - 1] = harmonic(k[s], above[s])
        above = k

    def product(l, flux_above):
        vm, vh = v[0, l], v[1, l]
        west = turn(vm, vh, 1, first)
        side = fc[0, l] * (vm - west[0]), fc[1, l] * (vh - west[1])
        gone = turn(*side, Y - 1, last)
        outs, flux = [], []
        for s, x in enumerate((vm, vh)):
            rows = fr[s, l] * (x - pltpu.roll(x, 1, 0))
            r = dd[s, l] * x + (rows - pltpu.roll(rows, E - 1, 0)) + (side[s] - gone[s])
            if l:
                r = r - flux_above[s]
            if l < LAYERS - 1:
                fl = fv[s, l] * (x - v[s, l + 1])
                r = r + fl
                flux.append(fl)
            outs.append(r)
        return outs, flux

    zero = jnp.zeros((8, Y), F32)
    sums = [(zero, zero)] * 6
    sub = iota((8, Y), 0)
    start = jnp.where(lax.axis_index("gx") == 0, 0, W)

    def add_to(j, a, b):
        p, e = two_prod(a, b)
        s, e2 = two_sum(sums[j][0], p)
        sums[j] = s, sums[j][1] + (e + e2)

    for step in range(3):
        results, flux = [], None
        for l in range(LAYERS):
            outs, flux = product(l, flux)
            old, new = v[0, l], outs[0]
            for i in range(0, E, 8):
                a, b = old[i : i + 8], new[i : i + 8]
                if i == 0 or i == X:
                    keep = sub >= start if i == 0 else sub < W
                    a, b = jnp.where(keep, a, 0.0), jnp.where(keep, b, 0.0)
                add_to(2 * step, a, a)
                add_to(2 * step + 1, a, b)
            results.append(outs)
        if step < 2:
            for l in range(LAYERS):
                m = results[l][0]
                v[0, l], v[1, l] = results[l]
                (v1_out, v2_out)[step][l] = m[0:X]
                if step:
                    back_out[LAYERS + 2 * l : LAYERS + 2 * l + 2, :] = m[X : X + 2]
                else:
                    back_out[l : l + 1, :] = m[X : X + 1]
    back_out[3 * LAYERS : 3 * LAYERS + 1, :] = east[X - 1 : X, :]

    ln = iota((8, Y), 1)
    total = zero, zero
    for j in range(6):
        s = fold(sums[j], (4, 2, 1), 0)
        total = tuple(jnp.where(sub == j, a, b) for a, b in zip(s, total))
    total = renorm(*fold(total, (64, 32, 16, 8, 4, 2, 1), 1))
    row = jnp.where(ln == sub, total[0], jnp.where(ln == sub + 8, total[1], 0.0))
    row = jnp.sum(row, axis=0, keepdims=True)
    row_out[...] = jnp.broadcast_to(row, row_out.shape)


def fold(s, steps, dim):
    for by in steps:
        hi, e = two_sum(s[0], pltpu.roll(s[0], by, dim))
        s = hi, s[1] + pltpu.roll(s[1], by, dim) + e
    return s


def rows_total(ref):
    parts = [
        (ref[i : i + 8, :], pltpu.roll(ref[i : i + 8, :], Y - 8, 1))
        for i in range(0, ref.shape[0], 8)
    ]
    while len(parts) > 1:
        parts = [pair_add(a, b) for a, b in zip(parts[::2], parts[1::2])]
    return renorm(*fold(parts[0], (4, 2, 1), 0))


def relay_kernel(rows, row_out):
    hi, lo = rows_total(rows)
    ln = iota((8, Y), 1)
    both = jnp.where(ln < 8, hi, pltpu.roll(lo, 8, 1))
    for i in range(0, row_out.shape[0], 8):
        row_out[i : i + 8, :] = both


def soil_kernel(state, soil_class, land, inverse, base, water, head, w, w01):
    w[...] = jnp.zeros(w.shape, F32)
    w01[...] = jnp.zeros(w01.shape, F32)
    for e in range(CLASSES):
        x = inverse[e]
        w[0:STATE, e * PAD : e * PAD + STATE] = x
        w01[0:STATE, e : e + 1] = x[:, 0:1]
        w01[PAD : PAD + STATE, e : e + 1] = x[:, 1:2]
    w_all, w_two = w[...], w01[...]
    zero = jnp.zeros((PAD - STATE, Y), F32)
    entry = iota((16, Y), 0)

    def dot(a, columns):
        return jnp.dot(
            a,
            jnp.concatenate(columns, axis=1),
            precision=lax.Precision.HIGHEST,
            preferred_element_type=F32,
        )

    for x0 in range(0, X, 4):
        fields, spread, hot, kinds = [], [], [], []
        for x in range(x0, x0 + 4):
            f = state[pl.ds(x, STATE, stride=X), :]
            kind = jnp.where(land[x : x + 1, :] == 1, soil_class[x : x + 1, :], -1)
            padded = jnp.concatenate([f, zero], axis=0)
            spread.append(
                jnp.concatenate(
                    [jnp.where(kind == e, padded, 0.0) for e in range(CLASSES)], axis=0
                )
            )
            hot.append(jnp.where(kind == entry, 0.5, 0.0))
            fields.append(f)
            kinds.append(kind)
        solved, two = dot(w_all, spread), dot(w_two, hot)
        for n in range(4):
            here = pl.ds(x0 + n, STATE, stride=X)
            cut = slice(n * Y, n * Y + Y)
            base[here, :] = jnp.where(kinds[n] >= 0, solved[0:STATE, cut], fields[n])
            water[here, :] = two[0:STATE, cut]
            head[here, :] = two[PAD : PAD + STATE, cut]


def final_kernel(
    rows, rhs, v1, v2, back, base, water, head, left, east, south, ponding, land,
    corr_out, pond_out, soil_out,
):
    hi, lo = rows_total(rows)
    mu = [
        tuple(jnp.broadcast_to(t[:, j : j + 1], (8, Y)) for t in (hi, lo))
        for j in range(6)
    ]
    l21 = pair_div(mu[2], mu[1])
    l31 = pair_div(mu[3], mu[1])
    d2 = pair_sub(mu[3], pair_mul(l21, mu[2]))
    u = pair_sub(mu[4], pair_mul(l31, mu[2]))
    l32 = pair_div(u, d2)
    d3 = pair_sub(pair_sub(mu[5], pair_mul(l31, mu[3])), pair_mul(l32, u))
    y2 = pair_sub(mu[1], pair_mul(l21, mu[0]))
    y3 = pair_sub(pair_sub(mu[2], pair_mul(l31, mu[0])), pair_mul(l32, y2))
    c3 = pair_div(y3, d3)
    c2 = pair_sub(pair_div(y2, d2), pair_mul(l32, c3))
    c1 = pair_sub(
        pair_sub(pair_div(mu[0], mu[1]), pair_mul(l21, c2)), pair_mul(l31, c3)
    )
    c1, c2, c3 = (jnp.concatenate([c[0]] * (X // 8), axis=0) for c in (c1, c2, c3))

    row, lane = iota((X, Y), 0), iota((X, Y), 1)
    es, so = east[...], south[...]
    north = pltpu.roll(left[0:X, :], (-(W + G * FIELDS)) % Y, 1)
    inflow = jnp.where(
        row == 0, back[3 * LAYERS : 3 * LAYERS + 1, :], pltpu.roll(es, 1, 0)
    ) + jnp.where(lane == 0, pltpu.roll(north, 1, 1), pltpu.roll(so, 1, 1))
    pond = land[...].astype(F32) * (ponding[...] + 0.2 * (inflow - (es + so)))
    pond_out[...] = pond

    given = jnp.where(lax.axis_index("gx") == 0, 0, 1)
    top = None
    for l in range(LAYERS):
        q = LAYERS + 2 * l
        a1 = jnp.where(row < given, back[l : l + 1, :], v1[l])
        a2 = jnp.where(row < given, back[q : q + 1, :], v2[l])
        a2 = jnp.where((row == 1) & (given > 0), back[q + 1 : q + 2, :], a2)
        x = c1 * rhs[l] + c2 * a1 + c3 * a2
        corr_out[l] = x
        top = x if top is None else top
    for i in range(STATE):
        here = slice(i * X, i * X + X)
        soil_out[i] = base[here, :] + water[here, :] * pond + head[here, :] * top


def ahead(x, axis):
    return lax.ppermute(x, axis, [(i, i + 1) for i in range(lax.axis_size(axis) - 1)])


def back(x, axis):
    return lax.ppermute(x, axis, [(i + 1, i) for i in range(lax.axis_size(axis) - 1)])


def everyones(rows, axis):
    count = lax.axis_size(axis)
    return lax.all_to_all(rows.reshape(count, 1, Y), axis, 0, 0).reshape(count, Y)


def on_device(
    pressure, newton_rhs, geology, saturated_conductivity, genuchten_alpha,
    genuchten_exponent, land_mask, ponding, slope_class, slope_table,
    flow_direction, soil_class, soil_inverse, soil_state,
):
    block, plane, tall = (LAYERS, X, Y), (X, Y), (STATE * X, Y)
    local = (
        pressure, newton_rhs, geology, saturated_conductivity, genuchten_alpha,
        genuchten_exponent, land_mask, ponding, slope_class, slope_table,
        flow_direction,
    )
    cond, diag, slab, east, south = call(
        local_kernel,
        [block, block, (FIELDS, E - X, Y), plane, plane],
        [(pltpu.SMEM if a.ndim == 1 else pltpu.VMEM)(a.shape, a.dtype) for a in local]
        + [pltpu.SemaphoreType.DMA((len(local),))],
        [pl.BlockSpec(memory_space=pltpu.HBM)] * len(local),
    )(*(pltpu.with_memory_space_constraint(a, pltpu.HBM) for a in local))
    after = back(slab, "gx")
    (packed,) = call(pack_kernel, [(E, Y)])(newton_rhs, cond, diag, after, south)
    left, right = ahead(packed, "gy"), back(packed, "gy")
    v1, v2, rows, edge = call(
        krylov_kernel,
        [block, block, (lax.axis_size("gx"), Y), (16, Y)],
        [pltpu.VMEM((2, n, E, Y), F32) for n in (5, 5, 4, 5, 5)],
    )(newton_rhs, cond, diag, after, right, left, east)
    edge = ahead(edge, "gx")
    base, water, head = call(
        soil_kernel,
        [tall] * 3,
        [pltpu.VMEM((PAD, CLASSES * PAD), F32), pltpu.VMEM((2 * PAD, 16), F32)],
        flops=20_000_000,
        nbytes=2_000_000,
    )(soil_state.reshape(tall), soil_class, land_mask, soil_inverse)
    rows = everyones(rows, "gx")
    rows, base, water, head = lax.optimization_barrier((rows, base, water, head))
    (rows,) = call(relay_kernel, [(lax.axis_size("gy"), Y)])(rows)
    rows = everyones(rows, "gy")
    return call(final_kernel, [block, plane, (STATE, X, Y)])(
        rows, newton_rhs, v1, v2, edge, base, water, head, left, east, south,
        ponding, land_mask,
    )


def solution(mesh):
    cells, plane, rest = P(None, "gx", "gy"), P("gx", "gy"), P()
    return jax.shard_map(
        on_device,
        mesh=mesh,
        in_specs=(
            cells, cells, cells, rest, rest, rest, plane, plane, plane, rest, plane,
            plane, rest, cells,
        ),
        out_specs=(cells, plane, cells),
        check_vma=False,
    )
```

```python
import jax
import jax.numpy as jnp
from jax import lax
from jax.experimental import pallas as pl
from jax.experimental.pallas import tpu as pltpu
from jax.sharding import PartitionSpec as P


LAYERS = 5
STATE = 20
CLASSES = 12
W = 3
X, Y = 32, 128
E = X + 8
FIELDS = 3 * LAYERS
G = 2 * W
PAD = 24
F32 = jnp.float32


def two_sum(a, b):
    s = a + b
    t = s - a
    return s, (a - (s - t)) + (b - t)


def renorm(a, b):
    s = a + b
    return s, b - (s - a)


def halves(a):
    t = a * 4097.0
    hi = t - (t - a)
    return hi, a - hi


def two_prod(a, b):
    p = a * b
    (ah, al), (bh, bl) = halves(a), halves(b)
    return p, ((ah * bh - p) + ah * bl + al * bh) + al * bl


def pair_add(a, b):
    s, e = two_sum(a[0], b[0])
    return renorm(s, e + (a[1] + b[1]))


def pair_sub(a, b):
    return pair_add(a, (-b[0], -b[1]))


def pair_mul(a, b):
    p, e = two_prod(a[0], b[0])
    return renorm(p, e + (a[0] * b[1] + a[1] * b[0]))


def pair_div(a, b):
    q = a[0] / b[0]
    r = pair_sub(a, pair_mul((q, jnp.zeros_like(q)), b))
    q2 = r[0] / b[0]
    r = pair_sub(r, pair_mul((q2, jnp.zeros_like(q)), b))
    return pair_add(renorm(q, q2), (r[0] / b[0], jnp.zeros_like(q)))


def iota(shape, dim):
    return lax.broadcasted_iota(jnp.int32, shape, dim)


def pick(table, index):
    row = jnp.broadcast_to(table, index.shape)
    return jnp.take_along_axis(row, index, axis=1, mode="promise_in_bounds")


def call(kernel, outs, scratch=(), specs=None, flops=0, nbytes=0):
    extra = {} if specs is None else {"in_specs": specs}
    return pl.pallas_call(
        kernel,
        out_shape=[jax.ShapeDtypeStruct(s, F32) for s in outs],
        scratch_shapes=scratch,
        compiler_params=pltpu.CompilerParams(vmem_limit_bytes=32 * 2**20),
        cost_estimate=pl.CostEstimate(
            flops=flops, bytes_accessed=nbytes, transcendentals=0
        ),
        **extra,
    )


def gather_table(ref, count):
    lane = iota((1, Y), 1)
    row = jnp.full((1, Y), 1.0, F32)
    for i in range(count):
        row = jnp.where(lane == i, ref[i], row)
    return row


def local_kernel(*refs):
    (cond, diag, slab, east, south), held, sem = refs[11:16], refs[16:27], refs[27]
    copies = [
        pltpu.make_async_copy(refs[i], held[i], sem.at[i]) for i in range(11)
    ]
    for copy in copies:
        copy.start()
    for copy in copies:
        copy.wait()
    (pressure, rhs, geology, ks, alpha, expo, land, ponding, slope_class, slope, flow) = held
    t_ks = gather_table(ks, 16)
    t_la = jnp.log(gather_table(alpha, 16))
    t_n = gather_table(expo, 16)
    t_m = 1.0 - 1.0 / t_n
    t_slope = jnp.sqrt(gather_table(slope, 8)) / 0.03
    sea = 4.0 * (1.0 - land[...].astype(F32))
    for l in range(LAYERS):
        g = geology[l]
        p = jnp.abs(pressure[l])
        n = pick(t_n, g)
        m = pick(t_m, g)
        t = jnp.exp(n * (pick(t_la, g) + jnp.log(p)))
        one_t = 1.0 + t
        e = jnp.exp(-m * jnp.log(one_t))
        k = pick(t_ks, g) * e
        d = 0.05 + 0.4 * m * n * t * e / (p * one_t) + sea
        cond[l] = k
        diag[l] = d
        for f, x in enumerate((rhs[l], k, d)):
            slab[f * LAYERS + l] = x[0 : E - X]
    out = pick(t_slope, slope_class[...]) * jnp.exp((5.0 / 3.0) * jnp.log(ponding[...]))
    eastward = jnp.where(flow[...] == 0, out, 0.0)
    east[...] = eastward
    south[...] = out - eastward


def pack_kernel(rhs, cond, diag, after, south, packed):
    for lo, rows in ((0, X), (X, E - X)):
        lane = iota((rows, Y), 1)
        total = jnp.zeros((rows, Y), F32)
        for f, ref in enumerate((rhs, cond, diag)):
            for l in range(LAYERS):
                q = f * LAYERS + l
                x = pltpu.roll(after[q] if lo else ref[l], (W + G * q) % Y, 1)
                total = jnp.where((lane >= G * q) & (lane < G * q + G), x, total)
        if not lo:
            x = pltpu.roll(south[...], (W + G * FIELDS) % Y, 1)
            total = jnp.where(lane >= G * FIELDS, x, total)
        packed[lo : lo + rows, :] = total


def krylov_kernel(
    rhs, cond, diag, after, right, left, east, v1_out, v2_out, row_out, back_out,
    fr, fc, fv, dd, v,
):
    lane, row_of = iota((E, Y), 1), iota((E, Y), 0)
    first, last = lane == 0, lane == Y - 1

    def turn(m, h, by, edge):
        m, h = pltpu.roll(m, by, 1), pltpu.roll(h, by, 1)
        return jnp.where(edge, h, m), jnp.where(edge, m, h)

    w = jnp.where(lane % G >= W, right[...], left[...])

    def both(ref, f, l):
        q = f * LAYERS + l
        return (
            jnp.concatenate([ref[l], after[q]], axis=0),
            pltpu.roll(w, (-(W + G * q)) % Y, 1),
        )

    def harmonic(a, b):
        return 2.0 * a * b / jnp.maximum(a + b, 1e-30)

    above = None
    for l in range(LAYERS):
        v[0, l], v[1, l] = both(rhs, 0, l)
        k = both(cond, 1, l)
        dd[0, l], dd[1, l] = both(diag, 2, l)
        west = turn(*k, 1, first)
        for s in range(2):
            fr[s, l] = jnp.where(row_of == 0, 0.0, harmonic(k[s], pltpu.roll(k[s], 1, 0)))
            fc[s, l] = harmonic(k[s], west[s])
            if l:
                fv[s, l - 1] = harmonic(k[s], above[s])
        above = k

    def product(l, flux_above):
        vm, vh = v[0, l], v[1, l]
        west = turn(vm, vh, 1, first)
        side = fc[0, l] * (vm - west[0]), fc[1, l] * (vh - west[1])
        gone = turn(*side, Y - 1, last)
        outs, flux = [], []
        for s, x in enumerate((vm, vh)):
            rows = fr[s, l] * (x - pltpu.roll(x, 1, 0))
            r = dd[s, l] * x + (rows - pltpu.roll(rows, E - 1, 0)) + (side[s] - gone[s])
            if l:
                r = r - flux_above[s]
            if l < LAYERS - 1:
                fl = fv[s, l] * (x - v[s, l + 1])
                r = r + fl
                flux.append(fl)
            outs.append(r)
        return outs, flux

    zero = jnp.zeros((8, Y), F32)
    sums = [(zero, zero)] * 6
    sub = iota((8, Y), 0)
    start = jnp.where(lax.axis_index("gx") == 0, 0, W)

    def add_to(j, a, b):
        p, e = two_prod(a, b)
        s, e2 = two_sum(sums[j][0], p)
        sums[j] = s, sums[j][1] + (e + e2)

    for step in range(3):
        results, flux = [], None
        for l in range(LAYERS):
            outs, flux = product(l, flux)
            old, new = v[0, l], outs[0]
            for i in range(0, E, 8):
                a, b = old[i : i + 8], new[i : i + 8]
                if i == 0 or i == X:
                    keep = sub >= start if i == 0 else sub < W
                    a, b = jnp.where(keep, a, 0.0), jnp.where(keep, b, 0.0)
                add_to(2 * step, a, a)
                add_to(2 * step + 1, a, b)
            results.append(outs)
        if step < 2:
            for l in range(LAYERS):
                m = results[l][0]
                v[0, l], v[1, l] = results[l]
                (v1_out, v2_out)[step][l] = m[0:X]
                if step:
                    back_out[LAYERS + 2 * l : LAYERS + 2 * l + 2, :] = m[X : X + 2]
                else:
                    back_out[l : l + 1, :] = m[X : X + 1]
    back_out[3 * LAYERS : 3 * LAYERS + 1, :] = east[X - 1 : X, :]

    ln = iota((8, Y), 1)
    total = zero, zero
    for j in range(6):
        s = fold(sums[j], (4, 2, 1), 0)
        total = tuple(jnp.where(sub == j, a, b) for a, b in zip(s, total))
    total = renorm(*fold(total, (64, 32, 16, 8, 4, 2, 1), 1))
    row = jnp.where(ln == sub, total[0], jnp.where(ln == sub + 8, total[1], 0.0))
    row = jnp.sum(row, axis=0, keepdims=True)
    row_out[...] = jnp.broadcast_to(row, row_out.shape)


def fold(s, steps, dim):
    for by in steps:
        hi, e = two_sum(s[0], pltpu.roll(s[0], by, dim))
        s = hi, s[1] + pltpu.roll(s[1], by, dim) + e
    return s


def rows_total(ref):
    parts = [
        (ref[i : i + 8, :], pltpu.roll(ref[i : i + 8, :], Y - 8, 1))
        for i in range(0, ref.shape[0], 8)
    ]
    while len(parts) > 1:
        parts = [pair_add(a, b) for a, b in zip(parts[::2], parts[1::2])]
    return renorm(*fold(parts[0], (4, 2, 1), 0))


def relay_kernel(rows, row_out):
    hi, lo = rows_total(rows)
    ln = iota((8, Y), 1)
    both = jnp.where(ln < 8, hi, pltpu.roll(lo, 8, 1))
    for i in range(0, row_out.shape[0], 8):
        row_out[i : i + 8, :] = both


def soil_kernel(state, soil_class, land, inverse, base, water, head, w, w01):
    w[...] = jnp.zeros(w.shape, F32)
    w01[...] = jnp.zeros(w01.shape, F32)
    for e in range(CLASSES):
        x = inverse[e]
        w[0:STATE, e * PAD : e * PAD + STATE] = x
        w01[0:STATE, e : e + 1] = x[:, 0:1]
        w01[PAD : PAD + STATE, e : e + 1] = x[:, 1:2]
    w_all, w_two = w[...], w01[...]
    zero = jnp.zeros((PAD - STATE, Y), F32)
    entry = iota((16, Y), 0)

    def dot(a, columns):
        return jnp.dot(
            a,
            jnp.concatenate(columns, axis=1),
            precision=lax.Precision.HIGHEST,
            preferred_element_type=F32,
        )

    for x0 in range(0, X, 4):
        fields, spread, hot, kinds = [], [], [], []
        for x in range(x0, x0 + 4):
            f = state[pl.ds(x, STATE, stride=X), :]
            kind = jnp.where(land[x : x + 1, :] == 1, soil_class[x : x + 1, :], -1)
            padded = jnp.concatenate([f, zero], axis=0)
            spread.append(
                jnp.concatenate(
                    [jnp.where(kind == e, padded, 0.0) for e in range(CLASSES)], axis=0
                )
            )
            hot.append(jnp.where(kind == entry, 0.5, 0.0))
            fields.append(f)
            kinds.append(kind)
        solved, two = dot(w_all, spread), dot(w_two, hot)
        for n in range(4):
            here = pl.ds(x0 + n, STATE, stride=X)
            cut = slice(n * Y, n * Y + Y)
            base[here, :] = jnp.where(kinds[n] >= 0, solved[0:STATE, cut], fields[n])
            water[here, :] = two[0:STATE, cut]
            head[here, :] = two[PAD : PAD + STATE, cut]


def final_kernel(
    rows, rhs, v1, v2, back, base, water, head, left, east, south, ponding, land,
    corr_out, pond_out, soil_out,
):
    hi, lo = rows_total(rows)
    mu = [
        tuple(jnp.broadcast_to(t[:, j : j + 1], (8, Y)) for t in (hi, lo))
        for j in range(6)
    ]
    l21 = pair_div(mu[2], mu[1])
    l31 = pair_div(mu[3], mu[1])
    d2 = pair_sub(mu[3], pair_mul(l21, mu[2]))
    u = pair_sub(mu[4], pair_mul(l31, mu[2]))
    l32 = pair_div(u, d2)
    d3 = pair_sub(pair_sub(mu[5], pair_mul(l31, mu[3])), pair_mul(l32, u))
    y2 = pair_sub(mu[1], pair_mul(l21, mu[0]))
    y3 = pair_sub(pair_sub(mu[2], pair_mul(l31, mu[0])), pair_mul(l32, y2))
    c3 = pair_div(y3, d3)
    c2 = pair_sub(pair_div(y2, d2), pair_mul(l32, c3))
    c1 = pair_sub(
        pair_sub(pair_div(mu[0], mu[1]), pair_mul(l21, c2)), pair_mul(l31, c3)
    )
    c1, c2, c3 = (jnp.concatenate([c[0]] * (X // 8), axis=0) for c in (c1, c2, c3))

    row, lane = iota((X, Y), 0), iota((X, Y), 1)
    es, so = east[...], south[...]
    north = pltpu.roll(left[0:X, :], (-(W + G * FIELDS)) % Y, 1)
    inflow = jnp.where(
        row == 0, back[3 * LAYERS : 3 * LAYERS + 1, :], pltpu.roll(es, 1, 0)
    ) + jnp.where(lane == 0, pltpu.roll(north, 1, 1), pltpu.roll(so, 1, 1))
    pond = land[...].astype(F32) * (ponding[...] + 0.2 * (inflow - (es + so)))
    pond_out[...] = pond

    given = jnp.where(lax.axis_index("gx") == 0, 0, 1)
    top = None
    for l in range(LAYERS):
        q = LAYERS + 2 * l
        a1 = jnp.where(row < given, back[l : l + 1, :], v1[l])
        a2 = jnp.where(row < given, back[q : q + 1, :], v2[l])
        a2 = jnp.where((row == 1) & (given > 0), back[q + 1 : q + 2, :], a2)
        x = c1 * rhs[l] + c2 * a1 + c3 * a2
        corr_out[l] = x
        top = x if top is None else top
    for i in range(STATE):
        here = slice(i * X, i * X + X)
        soil_out[i] = base[here, :] + water[here, :] * pond + head[here, :] * top


def ahead(x, axis):
    return lax.ppermute(x, axis, [(i, i + 1) for i in range(lax.axis_size(axis) - 1)])


def back(x, axis):
    return lax.ppermute(x, axis, [(i + 1, i) for i in range(lax.axis_size(axis) - 1)])


def everyones(rows, axis):
    count = lax.axis_size(axis)
    return lax.all_to_all(rows.reshape(count, 1, Y), axis, 0, 0).reshape(count, Y)


def on_device(
    pressure, newton_rhs, geology, saturated_conductivity, genuchten_alpha,
    genuchten_exponent, land_mask, ponding, slope_class, slope_table,
    flow_direction, soil_class, soil_inverse, soil_state,
):
    block, plane, tall = (LAYERS, X, Y), (X, Y), (STATE * X, Y)
    local = (
        pressure, newton_rhs, geology, saturated_conductivity, genuchten_alpha,
        genuchten_exponent, land_mask, ponding, slope_class, slope_table,
        flow_direction,
    )
    cond, diag, slab, east, south = call(
        local_kernel,
        [block, block, (FIELDS, E - X, Y), plane, plane],
        [(pltpu.SMEM if a.ndim == 1 else pltpu.VMEM)(a.shape, a.dtype) for a in local]
        + [pltpu.SemaphoreType.DMA((len(local),))],
        [pl.BlockSpec(memory_space=pltpu.HBM)] * len(local),
    )(*(pltpu.with_memory_space_constraint(a, pltpu.HBM) for a in local))
    after = back(slab, "gx")
    base, water, head = call(
        soil_kernel,
        [tall] * 3,
        [pltpu.VMEM((PAD, CLASSES * PAD), F32), pltpu.VMEM((2 * PAD, 16), F32)],
        flops=20_000_000,
        nbytes=2_000_000,
    )(soil_state.reshape(tall), soil_class, land_mask, soil_inverse)
    after, base, water, head = lax.optimization_barrier((after, base, water, head))
    (packed,) = call(pack_kernel, [(E, Y)])(newton_rhs, cond, diag, after, south)
    left, right = ahead(packed, "gy"), back(packed, "gy")
    v1, v2, rows, edge = call(
        krylov_kernel,
        [block, block, (lax.axis_size("gx"), Y), (16, Y)],
        [pltpu.VMEM((2, n, E, Y), F32) for n in (5, 5, 4, 5, 5)],
    )(newton_rhs, cond, diag, after, right, left, east)
    edge = ahead(edge, "gx")
    rows, edge = lax.optimization_barrier((rows, edge))
    rows = everyones(rows, "gx")
    (rows,) = call(relay_kernel, [(lax.axis_size("gy"), Y)])(rows)
    rows = everyones(rows, "gy")
    return call(final_kernel, [block, plane, (STATE, X, Y)])(
        rows, newton_rhs, v1, v2, edge, base, water, head, left, east, south,
        ponding, land_mask,
    )


def solution(mesh):
    cells, plane, rest = P(None, "gx", "gy"), P("gx", "gy"), P()
    return jax.shard_map(
        on_device,
        mesh=mesh,
        in_specs=(
            cells, cells, cells, rest, rest, rest, plane, plane, plane, rest, plane,
            plane, rest, cells,
        ),
        out_specs=(cells, plane, cells),
        check_vma=False,
    )
```

```python
import jax
import jax.numpy as jnp
from jax import lax
from jax.experimental import pallas as pl
from jax.experimental.pallas import tpu as pltpu
from jax.sharding import PartitionSpec as P


LAYERS = 5
STATE = 20
CLASSES = 12
W = 3
X, Y = 32, 128
E = X + 8
FIELDS = 3 * LAYERS
G = 2 * W
PAD = 24
F32 = jnp.float32


def two_sum(a, b):
    s = a + b
    t = s - a
    return s, (a - (s - t)) + (b - t)


def renorm(a, b):
    s = a + b
    return s, b - (s - a)


def halves(a):
    t = a * 4097.0
    hi = t - (t - a)
    return hi, a - hi


def two_prod(a, b):
    p = a * b
    (ah, al), (bh, bl) = halves(a), halves(b)
    return p, ((ah * bh - p) + ah * bl + al * bh) + al * bl


def pair_add(a, b):
    s, e = two_sum(a[0], b[0])
    return renorm(s, e + (a[1] + b[1]))


def pair_sub(a, b):
    return pair_add(a, (-b[0], -b[1]))


def pair_mul(a, b):
    p, e = two_prod(a[0], b[0])
    return renorm(p, e + (a[0] * b[1] + a[1] * b[0]))


def pair_div(a, b):
    q = a[0] / b[0]
    r = pair_sub(a, pair_mul((q, jnp.zeros_like(q)), b))
    q2 = r[0] / b[0]
    r = pair_sub(r, pair_mul((q2, jnp.zeros_like(q)), b))
    return pair_add(renorm(q, q2), (r[0] / b[0], jnp.zeros_like(q)))


def iota(shape, dim):
    return lax.broadcasted_iota(jnp.int32, shape, dim)


def pick(table, index):
    row = jnp.broadcast_to(table, index.shape)
    return jnp.take_along_axis(row, index, axis=1, mode="promise_in_bounds")


def call(kernel, outs, scratch=(), specs=None, flops=0, nbytes=0):
    extra = {} if specs is None else {"in_specs": specs}
    return pl.pallas_call(
        kernel,
        out_shape=[jax.ShapeDtypeStruct(s, F32) for s in outs],
        scratch_shapes=scratch,
        compiler_params=pltpu.CompilerParams(vmem_limit_bytes=32 * 2**20),
        cost_estimate=pl.CostEstimate(
            flops=flops, bytes_accessed=nbytes, transcendentals=0
        ),
        **extra,
    )


def gather_table(ref, count):
    lane = iota((1, Y), 1)
    row = jnp.full((1, Y), 1.0, F32)
    for i in range(count):
        row = jnp.where(lane == i, ref[i], row)
    return row


def local_kernel(*refs):
    (cond, diag, slab, east, south), held, sem = refs[11:16], refs[16:27], refs[27]
    copies = [
        pltpu.make_async_copy(refs[i], held[i], sem.at[i]) for i in range(11)
    ]
    for copy in copies:
        copy.start()
    for copy in copies:
        copy.wait()
    (pressure, rhs, geology, ks, alpha, expo, land, ponding, slope_class, slope, flow) = held
    t_ks = gather_table(ks, 16)
    t_la = jnp.log(gather_table(alpha, 16))
    t_n = gather_table(expo, 16)
    t_m = 1.0 - 1.0 / t_n
    t_slope = jnp.sqrt(gather_table(slope, 8)) / 0.03
    sea = 4.0 * (1.0 - land[...].astype(F32))
    for l in range(LAYERS):
        g = geology[l]
        p = jnp.abs(pressure[l])
        n = pick(t_n, g)
        m = pick(t_m, g)
        t = jnp.exp(n * (pick(t_la, g) + jnp.log(p)))
        one_t = 1.0 + t
        e = jnp.exp(-m * jnp.log(one_t))
        k = pick(t_ks, g) * e
        d = 0.05 + 0.4 * m * n * t * e / (p * one_t) + sea
        cond[l] = k
        diag[l] = d
        for f, x in enumerate((rhs[l], k, d)):
            slab[f * LAYERS + l] = x[0 : E - X]
    out = pick(t_slope, slope_class[...]) * jnp.exp((5.0 / 3.0) * jnp.log(ponding[...]))
    eastward = jnp.where(flow[...] == 0, out, 0.0)
    east[...] = eastward
    south[...] = out - eastward


def pack_kernel(rhs, cond, diag, after, south, packed):
    for lo, rows in ((0, X), (X, E - X)):
        lane = iota((rows, Y), 1)
        total = jnp.zeros((rows, Y), F32)
        for f, ref in enumerate((rhs, cond, diag)):
            for l in range(LAYERS):
                q = f * LAYERS + l
                x = pltpu.roll(after[q] if lo else ref[l], (W + G * q) % Y, 1)
                total = jnp.where((lane >= G * q) & (lane < G * q + G), x, total)
        if not lo:
            x = pltpu.roll(south[...], (W + G * FIELDS) % Y, 1)
            total = jnp.where(lane >= G * FIELDS, x, total)
        packed[lo : lo + rows, :] = total


def krylov_kernel(
    rhs, cond, diag, after, right, left, east, v1_out, v2_out, row_out, back_out,
    fr, fc, fv, dd, v,
):
    lane, row_of = iota((E, Y), 1), iota((E, Y), 0)
    first, last = lane == 0, lane == Y - 1

    def turn(m, h, by, edge):
        m, h = pltpu.roll(m, by, 1), pltpu.roll(h, by, 1)
        return jnp.where(edge, h, m), jnp.where(edge, m, h)

    w = jnp.where(lane % G >= W, right[...], left[...])

    def both(ref, f, l):
        q = f * LAYERS + l
        return (
            jnp.concatenate([ref[l], after[q]], axis=0),
            pltpu.roll(w, (-(W + G * q)) % Y, 1),
        )

    def harmonic(a, b):
        return 2.0 * a * b / jnp.maximum(a + b, 1e-30)

    above = None
    for l in range(LAYERS):
        v[0, l], v[1, l] = both(rhs, 0, l)
        k = both(cond, 1, l)
        dd[0, l], dd[1, l] = both(diag, 2, l)
        west = turn(*k, 1, first)
        for s in range(2):
            fr[s, l] = jnp.where(row_of == 0, 0.0, harmonic(k[s], pltpu.roll(k[s], 1, 0)))
            fc[s, l] = harmonic(k[s], west[s])
            if l:
                fv[s, l - 1] = harmonic(k[s], above[s])
        above = k

    def product(l, flux_above):
        vm, vh = v[0, l], v[1, l]
        west = turn(vm, vh, 1, first)
        side = fc[0, l] * (vm - west[0]), fc[1, l] * (vh - west[1])
        gone = turn(*side, Y - 1, last)
        outs, flux = [], []
        for s, x in enumerate((vm, vh)):
            rows = fr[s, l] * (x - pltpu.roll(x, 1, 0))
            r = dd[s, l] * x + (rows - pltpu.roll(rows, E - 1, 0)) + (side[s] - gone[s])
            if l:
                r = r - flux_above[s]
            if l < LAYERS - 1:
                fl = fv[s, l] * (x - v[s, l + 1])
                r = r + fl
                flux.append(fl)
            outs.append(r)
        return outs, flux

    zero = jnp.zeros((8, Y), F32)
    sums = [(zero, zero)] * 6
    sub = iota((8, Y), 0)
    start = jnp.where(lax.axis_index("gx") == 0, 0, W)

    def add_to(j, a, b):
        p, e = two_prod(a, b)
        s, e2 = two_sum(sums[j][0], p)
        sums[j] = s, sums[j][1] + (e + e2)

    for step in range(3):
        results, flux = [], None
        for l in range(LAYERS):
            outs, flux = product(l, flux)
            old, new = v[0, l], outs[0]
            for i in range(0, E, 8):
                a, b = old[i : i + 8], new[i : i + 8]
                if i == 0 or i == X:
                    keep = sub >= start if i == 0 else sub < W
                    a, b = jnp.where(keep, a, 0.0), jnp.where(keep, b, 0.0)
                add_to(2 * step, a, a)
                add_to(2 * step + 1, a, b)
            results.append(outs)
        if step < 2:
            for l in range(LAYERS):
                m = results[l][0]
                v[0, l], v[1, l] = results[l]
                (v1_out, v2_out)[step][l] = m[0:X]
                if step:
                    back_out[LAYERS + 2 * l : LAYERS + 2 * l + 2, :] = m[X : X + 2]
                else:
                    back_out[l : l + 1, :] = m[X : X + 1]
    back_out[3 * LAYERS : 3 * LAYERS + 1, :] = east[X - 1 : X, :]

    ln = iota((8, Y), 1)
    total = zero, zero
    for j in range(6):
        s = fold(sums[j], (4, 2, 1), 0)
        total = tuple(jnp.where(sub == j, a, b) for a, b in zip(s, total))
    total = renorm(*fold(total, (64, 32, 16, 8, 4, 2, 1), 1))
    row = jnp.where(ln == sub, total[0], jnp.where(ln == sub + 8, total[1], 0.0))
    row = jnp.sum(row, axis=0, keepdims=True)
    row_out[...] = jnp.broadcast_to(row, row_out.shape)


def fold(s, steps, dim):
    for by in steps:
        hi, e = two_sum(s[0], pltpu.roll(s[0], by, dim))
        s = hi, s[1] + pltpu.roll(s[1], by, dim) + e
    return s


def rows_total(ref):
    parts = [
        (ref[i : i + 8, :], pltpu.roll(ref[i : i + 8, :], Y - 8, 1))
        for i in range(0, ref.shape[0], 8)
    ]
    while len(parts) > 1:
        parts = [pair_add(a, b) for a, b in zip(parts[::2], parts[1::2])]
    return renorm(*fold(parts[0], (4, 2, 1), 0))


def relay_kernel(rows, row_out):
    hi, lo = rows_total(rows)
    ln = iota((8, Y), 1)
    both = jnp.where(ln < 8, hi, pltpu.roll(lo, 8, 1))
    for i in range(0, row_out.shape[0], 8):
        row_out[i : i + 8, :] = both


def soil_kernel(
    state_hbm, soil_class, land, inverse, base, water, head, w, w01, state, sem
):
    copy = pltpu.make_async_copy(state_hbm, state, sem)
    copy.start()
    w[...] = jnp.zeros(w.shape, F32)
    w01[...] = jnp.zeros(w01.shape, F32)
    for e in range(CLASSES):
        x = inverse[e]
        w[0:STATE, e * PAD : e * PAD + STATE] = x
        w01[0:STATE, e : e + 1] = x[:, 0:1]
        w01[PAD : PAD + STATE, e : e + 1] = x[:, 1:2]
    w_all, w_two = w[...], w01[...]
    copy.wait()
    zero = jnp.zeros((PAD - STATE, Y), F32)
    entry = iota((16, Y), 0)

    def dot(a, columns):
        return jnp.dot(
            a,
            jnp.concatenate(columns, axis=1),
            precision=lax.Precision.HIGHEST,
            preferred_element_type=F32,
        )

    for x0 in range(0, X, 4):
        fields, spread, hot, kinds = [], [], [], []
        for x in range(x0, x0 + 4):
            f = state[pl.ds(x, STATE, stride=X), :]
            kind = jnp.where(land[x : x + 1, :] == 1, soil_class[x : x + 1, :], -1)
            padded = jnp.concatenate([f, zero], axis=0)
            spread.append(
                jnp.concatenate(
                    [jnp.where(kind == e, padded, 0.0) for e in range(CLASSES)], axis=0
                )
            )
            hot.append(jnp.where(kind == entry, 0.5, 0.0))
            fields.append(f)
            kinds.append(kind)
        solved, two = dot(w_all, spread), dot(w_two, hot)
        for n in range(4):
            here = pl.ds(x0 + n, STATE, stride=X)
            cut = slice(n * Y, n * Y + Y)
            base[here, :] = jnp.where(kinds[n] >= 0, solved[0:STATE, cut], fields[n])
            water[here, :] = two[0:STATE, cut]
            head[here, :] = two[PAD : PAD + STATE, cut]


def final_kernel(
    rows, rhs, v1, v2, back, base, water, head, left, east, south, ponding, land,
    corr_out, pond_out, soil_out,
):
    hi, lo = rows_total(rows)
    mu = [
        tuple(jnp.broadcast_to(t[:, j : j + 1], (8, Y)) for t in (hi, lo))
        for j in range(6)
    ]
    l21 = pair_div(mu[2], mu[1])
    l31 = pair_div(mu[3], mu[1])
    d2 = pair_sub(mu[3], pair_mul(l21, mu[2]))
    u = pair_sub(mu[4], pair_mul(l31, mu[2]))
    l32 = pair_div(u, d2)
    d3 = pair_sub(pair_sub(mu[5], pair_mul(l31, mu[3])), pair_mul(l32, u))
    y2 = pair_sub(mu[1], pair_mul(l21, mu[0]))
    y3 = pair_sub(pair_sub(mu[2], pair_mul(l31, mu[0])), pair_mul(l32, y2))
    c3 = pair_div(y3, d3)
    c2 = pair_sub(pair_div(y2, d2), pair_mul(l32, c3))
    c1 = pair_sub(
        pair_sub(pair_div(mu[0], mu[1]), pair_mul(l21, c2)), pair_mul(l31, c3)
    )
    c1, c2, c3 = (jnp.concatenate([c[0]] * (X // 8), axis=0) for c in (c1, c2, c3))

    row, lane = iota((X, Y), 0), iota((X, Y), 1)
    es, so = east[...], south[...]
    north = pltpu.roll(left[0:X, :], (-(W + G * FIELDS)) % Y, 1)
    inflow = jnp.where(
        row == 0, back[3 * LAYERS : 3 * LAYERS + 1, :], pltpu.roll(es, 1, 0)
    ) + jnp.where(lane == 0, pltpu.roll(north, 1, 1), pltpu.roll(so, 1, 1))
    pond = land[...].astype(F32) * (ponding[...] + 0.2 * (inflow - (es + so)))
    pond_out[...] = pond

    given = jnp.where(lax.axis_index("gx") == 0, 0, 1)
    top = None
    for l in range(LAYERS):
        q = LAYERS + 2 * l
        a1 = jnp.where(row < given, back[l : l + 1, :], v1[l])
        a2 = jnp.where(row < given, back[q : q + 1, :], v2[l])
        a2 = jnp.where((row == 1) & (given > 0), back[q + 1 : q + 2, :], a2)
        x = c1 * rhs[l] + c2 * a1 + c3 * a2
        corr_out[l] = x
        top = x if top is None else top
    for i in range(STATE):
        here = slice(i * X, i * X + X)
        soil_out[i] = base[here, :] + water[here, :] * pond + head[here, :] * top


def ahead(x, axis):
    return lax.ppermute(x, axis, [(i, i + 1) for i in range(lax.axis_size(axis) - 1)])


def back(x, axis):
    return lax.ppermute(x, axis, [(i + 1, i) for i in range(lax.axis_size(axis) - 1)])


def everyones(rows, axis):
    count = lax.axis_size(axis)
    return lax.all_to_all(rows.reshape(count, 1, Y), axis, 0, 0).reshape(count, Y)


def on_device(
    pressure, newton_rhs, geology, saturated_conductivity, genuchten_alpha,
    genuchten_exponent, land_mask, ponding, slope_class, slope_table,
    flow_direction, soil_class, soil_inverse, soil_state,
):
    block, plane, tall = (LAYERS, X, Y), (X, Y), (STATE * X, Y)
    local = (
        pressure, newton_rhs, geology, saturated_conductivity, genuchten_alpha,
        genuchten_exponent, land_mask, ponding, slope_class, slope_table,
        flow_direction,
    )
    cond, diag, slab, east, south = call(
        local_kernel,
        [block, block, (FIELDS, E - X, Y), plane, plane],
        [(pltpu.SMEM if a.ndim == 1 else pltpu.VMEM)(a.shape, a.dtype) for a in local]
        + [pltpu.SemaphoreType.DMA((len(local),))],
        [pl.BlockSpec(memory_space=pltpu.HBM)] * len(local),
    )(*(pltpu.with_memory_space_constraint(a, pltpu.HBM) for a in local))
    after = back(slab, "gx")
    base, water, head = call(
        soil_kernel,
        [tall] * 3,
        [
            pltpu.VMEM((PAD, CLASSES * PAD), F32),
            pltpu.VMEM((2 * PAD, 16), F32),
            pltpu.VMEM(tall, F32),
            pltpu.SemaphoreType.DMA,
        ],
        [pl.BlockSpec(memory_space=pltpu.HBM)] + [pl.BlockSpec()] * 3,
        flops=20_000_000,
        nbytes=2_000_000,
    )(
        pltpu.with_memory_space_constraint(soil_state.reshape(tall), pltpu.HBM),
        soil_class, land_mask, soil_inverse,
    )
    after, base, water, head = lax.optimization_barrier((after, base, water, head))
    (packed,) = call(pack_kernel, [(E, Y)])(newton_rhs, cond, diag, after, south)
    left, right = ahead(packed, "gy"), back(packed, "gy")
    v1, v2, rows, edge = call(
        krylov_kernel,
        [block, block, (lax.axis_size("gx"), Y), (16, Y)],
        [pltpu.VMEM((2, n, E, Y), F32) for n in (5, 5, 4, 5, 5)],
    )(newton_rhs, cond, diag, after, right, left, east)
    edge = ahead(edge, "gx")
    rows = everyones(rows, "gx")
    (rows,) = call(relay_kernel, [(lax.axis_size("gy"), Y)])(rows)
    rows = everyones(rows, "gy")
    return call(final_kernel, [block, plane, (STATE, X, Y)])(
        rows, newton_rhs, v1, v2, edge, base, water, head, left, east, south,
        ponding, land_mask,
    )


def solution(mesh):
    cells, plane, rest = P(None, "gx", "gy"), P("gx", "gy"), P()
    return jax.shard_map(
        on_device,
        mesh=mesh,
        in_specs=(
            cells, cells, cells, rest, rest, rest, plane, plane, plane, rest, plane,
            plane, rest, cells,
        ),
        out_specs=(cells, plane, cells),
        check_vma=False,
    )
```

```python
import jax
import jax.numpy as jnp
from jax import lax
from jax.experimental import pallas as pl
from jax.experimental.pallas import tpu as pltpu
from jax.sharding import PartitionSpec as P


LAYERS = 5
STATE = 20
CLASSES = 12
W = 3
X, Y = 32, 128
E = X + 8
FIELDS = 3 * LAYERS
G = 2 * W
PAD = 24
F32 = jnp.float32


def two_sum(a, b):
    s = a + b
    t = s - a
    return s, (a - (s - t)) + (b - t)


def renorm(a, b):
    s = a + b
    return s, b - (s - a)


def halves(a):
    t = a * 4097.0
    hi = t - (t - a)
    return hi, a - hi


def two_prod(a, b):
    p = a * b
    (ah, al), (bh, bl) = halves(a), halves(b)
    return p, ((ah * bh - p) + ah * bl + al * bh) + al * bl


def pair_add(a, b):
    s, e = two_sum(a[0], b[0])
    return renorm(s, e + (a[1] + b[1]))


def pair_sub(a, b):
    return pair_add(a, (-b[0], -b[1]))


def pair_mul(a, b):
    p, e = two_prod(a[0], b[0])
    return renorm(p, e + (a[0] * b[1] + a[1] * b[0]))


def pair_div(a, b):
    q = a[0] / b[0]
    r = pair_sub(a, pair_mul((q, jnp.zeros_like(q)), b))
    q2 = r[0] / b[0]
    r = pair_sub(r, pair_mul((q2, jnp.zeros_like(q)), b))
    return pair_add(renorm(q, q2), (r[0] / b[0], jnp.zeros_like(q)))


def iota(shape, dim):
    return lax.broadcasted_iota(jnp.int32, shape, dim)


def pick(table, index):
    row = jnp.broadcast_to(table, index.shape)
    return jnp.take_along_axis(row, index, axis=1, mode="promise_in_bounds")


def call(kernel, outs, scratch=(), specs=None, flops=0, nbytes=0):
    extra = {} if specs is None else {"in_specs": specs}
    return pl.pallas_call(
        kernel,
        out_shape=[jax.ShapeDtypeStruct(s, F32) for s in outs],
        scratch_shapes=scratch,
        compiler_params=pltpu.CompilerParams(vmem_limit_bytes=32 * 2**20),
        cost_estimate=pl.CostEstimate(
            flops=flops, bytes_accessed=nbytes, transcendentals=0
        ),
        **extra,
    )


def gather_table(ref, count):
    lane = iota((1, Y), 1)
    row = jnp.full((1, Y), 1.0, F32)
    for i in range(count):
        row = jnp.where(lane == i, ref[i], row)
    return row


def local_kernel(*refs):
    (cond, diag, slab, east, south), held, sem = refs[11:16], refs[16:27], refs[27]
    copies = [
        pltpu.make_async_copy(refs[i], held[i], sem.at[i]) for i in range(11)
    ]
    for copy in copies:
        copy.start()
    for copy in copies:
        copy.wait()
    (pressure, rhs, geology, ks, alpha, expo, land, ponding, slope_class, slope, flow) = held
    t_ks = gather_table(ks, 16)
    t_la = jnp.log(gather_table(alpha, 16))
    t_n = gather_table(expo, 16)
    t_m = 1.0 - 1.0 / t_n
    t_slope = jnp.sqrt(gather_table(slope, 8)) / 0.03
    sea = 4.0 * (1.0 - land[...].astype(F32))
    for l in range(LAYERS):
        g = geology[l]
        p = jnp.abs(pressure[l])
        n = pick(t_n, g)
        m = pick(t_m, g)
        t = jnp.exp(n * (pick(t_la, g) + jnp.log(p)))
        one_t = 1.0 + t
        e = jnp.exp(-m * jnp.log(one_t))
        k = pick(t_ks, g) * e
        d = 0.05 + 0.4 * m * n * t * e / (p * one_t) + sea
        cond[l] = k
        diag[l] = d
        for f, x in enumerate((rhs[l], k, d)):
            slab[f * LAYERS + l] = x[0 : E - X]
    out = pick(t_slope, slope_class[...]) * jnp.exp((5.0 / 3.0) * jnp.log(ponding[...]))
    eastward = jnp.where(flow[...] == 0, out, 0.0)
    east[...] = eastward
    south[...] = out - eastward


def pack_kernel(rhs, cond, diag, after, south, packed):
    for lo, rows in ((0, X), (X, E - X)):
        lane = iota((rows, Y), 1)
        total = jnp.zeros((rows, Y), F32)
        for f, ref in enumerate((rhs, cond, diag)):
            for l in range(LAYERS):
                q = f * LAYERS + l
                x = pltpu.roll(after[q] if lo else ref[l], (W + G * q) % Y, 1)
                total = jnp.where((lane >= G * q) & (lane < G * q + G), x, total)
        if not lo:
            x = pltpu.roll(south[...], (W + G * FIELDS) % Y, 1)
            total = jnp.where(lane >= G * FIELDS, x, total)
        packed[lo : lo + rows, :] = total


def krylov_kernel(
    rhs, cond, diag, after, right, left, east, v1_out, v2_out, row_out, back_out,
    fr, fc, fv, dd, v,
):
    lane, row_of = iota((E, Y), 1), iota((E, Y), 0)
    first, last = lane == 0, lane == Y - 1
    x, y = lax.axis_index("gx"), lax.axis_index("gy")
    x_end, y_end = x == lax.axis_size("gx") - 1, y == lax.axis_size("gy") - 1
    closed_rows = (row_of == 0) | (row_of == jnp.where(x_end, X, 0))
    closed_lanes = (
        lane == jnp.where(y == 0, 0, -1),
        lane == jnp.where(y_end, 0, -1),
    )

    def turn(m, h, by, edge):
        m, h = pltpu.roll(m, by, 1), pltpu.roll(h, by, 1)
        return jnp.where(edge, h, m), jnp.where(edge, m, h)

    w = jnp.where(lane % G >= W, right[...], left[...])

    def both(ref, f, l):
        q = f * LAYERS + l
        return (
            jnp.concatenate([ref[l], after[q]], axis=0),
            pltpu.roll(w, (-(W + G * q)) % Y, 1),
        )

    def harmonic(a, b):
        return 2.0 * a * b / jnp.maximum(a + b, 1e-30)

    above = None
    for l in range(LAYERS):
        v[0, l], v[1, l] = both(rhs, 0, l)
        k = both(cond, 1, l)
        dd[0, l], dd[1, l] = both(diag, 2, l)
        west = turn(*k, 1, first)
        for s in range(2):
            fr[s, l] = jnp.where(
                closed_rows, 0.0, harmonic(k[s], pltpu.roll(k[s], 1, 0))
            )
            fc[s, l] = jnp.where(closed_lanes[s], 0.0, harmonic(k[s], west[s]))
            if l:
                fv[s, l - 1] = harmonic(k[s], above[s])
        above = k

    def product(l, flux_above):
        vm, vh = v[0, l], v[1, l]
        west = turn(vm, vh, 1, first)
        side = fc[0, l] * (vm - west[0]), fc[1, l] * (vh - west[1])
        gone = turn(*side, Y - 1, last)
        outs, flux = [], []
        for s, x in enumerate((vm, vh)):
            rows = fr[s, l] * (x - pltpu.roll(x, 1, 0))
            r = dd[s, l] * x + (rows - pltpu.roll(rows, E - 1, 0)) + (side[s] - gone[s])
            if l:
                r = r - flux_above[s]
            if l < LAYERS - 1:
                fl = fv[s, l] * (x - v[s, l + 1])
                r = r + fl
                flux.append(fl)
            outs.append(r)
        return outs, flux

    zero = jnp.zeros((8, Y), F32)
    sums = [(zero, zero)] * 6
    sub = iota((8, Y), 0)
    start, stop = jnp.where(x == 0, 0, W), jnp.where(x_end, 0, W)

    def add_to(j, a, b):
        p, e = two_prod(a, b)
        s, e2 = two_sum(sums[j][0], p)
        sums[j] = s, sums[j][1] + (e + e2)

    for step in range(3):
        results, flux = [], None
        for l in range(LAYERS):
            outs, flux = product(l, flux)
            old, new = v[0, l], outs[0]
            for i in range(0, E, 8):
                a, b = old[i : i + 8], new[i : i + 8]
                if i == 0 or i == X:
                    keep = sub >= start if i == 0 else sub < stop
                    a, b = jnp.where(keep, a, 0.0), jnp.where(keep, b, 0.0)
                add_to(2 * step, a, a)
                add_to(2 * step + 1, a, b)
            results.append(outs)
        if step < 2:
            for l in range(LAYERS):
                m = results[l][0]
                v[0, l], v[1, l] = results[l]
                (v1_out, v2_out)[step][l] = m[0:X]
                if step:
                    back_out[LAYERS + 2 * l : LAYERS + 2 * l + 2, :] = m[X : X + 2]
                else:
                    back_out[l : l + 1, :] = m[X : X + 1]
    back_out[3 * LAYERS : 3 * LAYERS + 1, :] = east[X - 1 : X, :]

    ln = iota((8, Y), 1)
    total = zero, zero
    for j in range(6):
        s = fold(sums[j], (4, 2, 1), 0)
        total = tuple(jnp.where(sub == j, a, b) for a, b in zip(s, total))
    total = renorm(*fold(total, (64, 32, 16, 8, 4, 2, 1), 1))
    row = jnp.where(ln == sub, total[0], jnp.where(ln == sub + 8, total[1], 0.0))
    row = jnp.sum(row, axis=0, keepdims=True)
    row_out[...] = jnp.broadcast_to(row, row_out.shape)


def fold(s, steps, dim):
    for by in steps:
        hi, e = two_sum(s[0], pltpu.roll(s[0], by, dim))
        s = hi, s[1] + pltpu.roll(s[1], by, dim) + e
    return s


def rows_total(ref):
    parts = [
        (ref[i : i + 8, :], pltpu.roll(ref[i : i + 8, :], Y - 8, 1))
        for i in range(0, ref.shape[0], 8)
    ]
    while len(parts) > 1:
        parts = [pair_add(a, b) for a, b in zip(parts[::2], parts[1::2])]
    return renorm(*fold(parts[0], (4, 2, 1), 0))


def relay_kernel(rows, row_out):
    hi, lo = rows_total(rows)
    ln = iota((8, Y), 1)
    both = jnp.where(ln < 8, hi, pltpu.roll(lo, 8, 1))
    for i in range(0, row_out.shape[0], 8):
        row_out[i : i + 8, :] = both


def soil_kernel(
    state_hbm, soil_class, land, inverse, base, water, head, w, w01, state, sem
):
    copy = pltpu.make_async_copy(state_hbm, state, sem)
    copy.start()
    w[...] = jnp.zeros(w.shape, F32)
    w01[...] = jnp.zeros(w01.shape, F32)
    for e in range(CLASSES):
        x = inverse[e]
        w[0:STATE, e * PAD : e * PAD + STATE] = x
        w01[0:STATE, e : e + 1] = x[:, 0:1]
        w01[PAD : PAD + STATE, e : e + 1] = x[:, 1:2]
    w_all, w_two = w[...], w01[...]
    copy.wait()
    zero = jnp.zeros((PAD - STATE, Y), F32)
    entry = iota((16, Y), 0)

    def dot(a, columns):
        return jnp.dot(
            a,
            jnp.concatenate(columns, axis=1),
            precision=lax.Precision.HIGHEST,
            preferred_element_type=F32,
        )

    for x0 in range(0, X, 4):
        fields, spread, hot, kinds = [], [], [], []
        for x in range(x0, x0 + 4):
            f = state[pl.ds(x, STATE, stride=X), :]
            kind = jnp.where(land[x : x + 1, :] == 1, soil_class[x : x + 1, :], -1)
            padded = jnp.concatenate([f, zero], axis=0)
            spread.append(
                jnp.concatenate(
                    [jnp.where(kind == e, padded, 0.0) for e in range(CLASSES)], axis=0
                )
            )
            hot.append(jnp.where(kind == entry, 0.5, 0.0))
            fields.append(f)
            kinds.append(kind)
        solved, two = dot(w_all, spread), dot(w_two, hot)
        for n in range(4):
            here = pl.ds(x0 + n, STATE, stride=X)
            cut = slice(n * Y, n * Y + Y)
            base[here, :] = jnp.where(kinds[n] >= 0, solved[0:STATE, cut], fields[n])
            water[here, :] = two[0:STATE, cut]
            head[here, :] = two[PAD : PAD + STATE, cut]


def final_kernel(
    rows, rhs, v1, v2, back, base, water, head, left, east, south, ponding, land,
    corr_out, pond_out, soil_out,
):
    hi, lo = rows_total(rows)
    mu = [
        tuple(jnp.broadcast_to(t[:, j : j + 1], (8, Y)) for t in (hi, lo))
        for j in range(6)
    ]
    l21 = pair_div(mu[2], mu[1])
    l31 = pair_div(mu[3], mu[1])
    d2 = pair_sub(mu[3], pair_mul(l21, mu[2]))
    u = pair_sub(mu[4], pair_mul(l31, mu[2]))
    l32 = pair_div(u, d2)
    d3 = pair_sub(pair_sub(mu[5], pair_mul(l31, mu[3])), pair_mul(l32, u))
    y2 = pair_sub(mu[1], pair_mul(l21, mu[0]))
    y3 = pair_sub(pair_sub(mu[2], pair_mul(l31, mu[0])), pair_mul(l32, y2))
    c3 = pair_div(y3, d3)
    c2 = pair_sub(pair_div(y2, d2), pair_mul(l32, c3))
    c1 = pair_sub(
        pair_sub(pair_div(mu[0], mu[1]), pair_mul(l21, c2)), pair_mul(l31, c3)
    )
    c1, c2, c3 = (jnp.concatenate([c[0]] * (X // 8), axis=0) for c in (c1, c2, c3))

    row, lane = iota((X, Y), 0), iota((X, Y), 1)
    es, so = east[...], south[...]
    north = pltpu.roll(left[0:X, :], (-(W + G * FIELDS)) % Y, 1)
    given = jnp.where(lax.axis_index("gx") == 0, 0, 1)
    west = jnp.where(given == 0, 0.0, back[3 * LAYERS : 3 * LAYERS + 1, :])
    north = jnp.where(lax.axis_index("gy") == 0, 0.0, pltpu.roll(north, 1, 1))
    inflow = jnp.where(row == 0, west, pltpu.roll(es, 1, 0)) + jnp.where(
        lane == 0, north, pltpu.roll(so, 1, 1)
    )
    pond = land[...].astype(F32) * (ponding[...] + 0.2 * (inflow - (es + so)))
    pond_out[...] = pond

    top = None
    for l in range(LAYERS):
        q = LAYERS + 2 * l
        a1 = jnp.where(row < given, back[l : l + 1, :], v1[l])
        a2 = jnp.where(row < given, back[q : q + 1, :], v2[l])
        a2 = jnp.where((row == 1) & (given > 0), back[q + 1 : q + 2, :], a2)
        x = c1 * rhs[l] + c2 * a1 + c3 * a2
        corr_out[l] = x
        top = x if top is None else top
    for i in range(STATE):
        here = slice(i * X, i * X + X)
        soil_out[i] = base[here, :] + water[here, :] * pond + head[here, :] * top


def ahead(x, axis):
    n = lax.axis_size(axis)
    return lax.ppermute(x, axis, [(i, (i + 1) % n) for i in range(n)])


def back(x, axis):
    n = lax.axis_size(axis)
    return lax.ppermute(x, axis, [((i + 1) % n, i) for i in range(n)])


def everyones(rows, axis):
    count = lax.axis_size(axis)
    return lax.all_to_all(rows.reshape(count, 1, Y), axis, 0, 0).reshape(count, Y)


def on_device(
    pressure, newton_rhs, geology, saturated_conductivity, genuchten_alpha,
    genuchten_exponent, land_mask, ponding, slope_class, slope_table,
    flow_direction, soil_class, soil_inverse, soil_state,
):
    block, plane, tall = (LAYERS, X, Y), (X, Y), (STATE * X, Y)
    local = (
        pressure, newton_rhs, geology, saturated_conductivity, genuchten_alpha,
        genuchten_exponent, land_mask, ponding, slope_class, slope_table,
        flow_direction,
    )
    cond, diag, slab, east, south = call(
        local_kernel,
        [block, block, (FIELDS, E - X, Y), plane, plane],
        [(pltpu.SMEM if a.ndim == 1 else pltpu.VMEM)(a.shape, a.dtype) for a in local]
        + [pltpu.SemaphoreType.DMA((len(local),))],
        [pl.BlockSpec(memory_space=pltpu.HBM)] * len(local),
    )(*(pltpu.with_memory_space_constraint(a, pltpu.HBM) for a in local))
    after = back(slab, "gx")
    base, water, head = call(
        soil_kernel,
        [tall] * 3,
        [
            pltpu.VMEM((PAD, CLASSES * PAD), F32),
            pltpu.VMEM((2 * PAD, 16), F32),
            pltpu.VMEM(tall, F32),
            pltpu.SemaphoreType.DMA,
        ],
        [pl.BlockSpec(memory_space=pltpu.HBM)] + [pl.BlockSpec()] * 3,
        flops=20_000_000,
        nbytes=2_000_000,
    )(
        pltpu.with_memory_space_constraint(soil_state.reshape(tall), pltpu.HBM),
        soil_class, land_mask, soil_inverse,
    )
    after, base, water, head = lax.optimization_barrier((after, base, water, head))
    (packed,) = call(pack_kernel, [(E, Y)])(newton_rhs, cond, diag, after, south)
    left, right = ahead(packed, "gy"), back(packed, "gy")
    v1, v2, rows, edge = call(
        krylov_kernel,
        [block, block, (lax.axis_size("gy"), Y), (16, Y)],
        [pltpu.VMEM((2, n, E, Y), F32) for n in (5, 5, 4, 5, 5)],
    )(newton_rhs, cond, diag, after, right, left, east)
    edge = ahead(edge, "gx")
    rows = everyones(rows, "gy")
    (rows,) = call(relay_kernel, [(lax.axis_size("gx"), Y)])(rows)
    rows = everyones(rows, "gx")
    return call(final_kernel, [block, plane, (STATE, X, Y)])(
        rows, newton_rhs, v1, v2, edge, base, water, head, left, east, south,
        ponding, land_mask,
    )


def solution(mesh):
    cells, plane, rest = P(None, "gx", "gy"), P("gx", "gy"), P()
    return jax.shard_map(
        on_device,
        mesh=mesh,
        in_specs=(
            cells, cells, cells, rest, rest, rest, plane, plane, plane, rest, plane,
            plane, rest, cells,
        ),
        out_specs=(cells, plane, cells),
        check_vma=False,
    )
```

```python
import jax
import jax.numpy as jnp
from jax import lax
from jax.experimental import pallas as pl
from jax.experimental.pallas import tpu as pltpu
from jax.sharding import PartitionSpec as P


LAYERS = 5
STATE = 20
CLASSES = 12
W = 3
X, Y = 32, 128
E = X + 8
FIELDS = 3 * LAYERS
G = 2 * W
PAD = 24
F32 = jnp.float32


def two_sum(a, b):
    s = a + b
    t = s - a
    return s, (a - (s - t)) + (b - t)


def renorm(a, b):
    s = a + b
    return s, b - (s - a)


def halves(a):
    t = a * 4097.0
    hi = t - (t - a)
    return hi, a - hi


def two_prod(a, b):
    p = a * b
    (ah, al), (bh, bl) = halves(a), halves(b)
    return p, ((ah * bh - p) + ah * bl + al * bh) + al * bl


def pair_add(a, b):
    s, e = two_sum(a[0], b[0])
    return renorm(s, e + (a[1] + b[1]))


def pair_sub(a, b):
    return pair_add(a, (-b[0], -b[1]))


def pair_mul(a, b):
    p, e = two_prod(a[0], b[0])
    return renorm(p, e + (a[0] * b[1] + a[1] * b[0]))


def pair_div(a, b):
    q = a[0] / b[0]
    r = pair_sub(a, pair_mul((q, jnp.zeros_like(q)), b))
    q2 = r[0] / b[0]
    r = pair_sub(r, pair_mul((q2, jnp.zeros_like(q)), b))
    return pair_add(renorm(q, q2), (r[0] / b[0], jnp.zeros_like(q)))


def iota(shape, dim):
    return lax.broadcasted_iota(jnp.int32, shape, dim)


def pick(table, index):
    row = jnp.broadcast_to(table, index.shape)
    return jnp.take_along_axis(row, index, axis=1, mode="promise_in_bounds")


def call(kernel, outs, scratch=(), specs=None, flops=0, nbytes=0):
    extra = {} if specs is None else {"in_specs": specs}
    return pl.pallas_call(
        kernel,
        out_shape=[jax.ShapeDtypeStruct(s, F32) for s in outs],
        scratch_shapes=scratch,
        compiler_params=pltpu.CompilerParams(vmem_limit_bytes=32 * 2**20),
        cost_estimate=pl.CostEstimate(
            flops=flops, bytes_accessed=nbytes, transcendentals=0
        ),
        **extra,
    )


def gather_table(ref, count):
    lane = iota((1, Y), 1)
    row = jnp.full((1, Y), 1.0, F32)
    for i in range(count):
        row = jnp.where(lane == i, ref[i], row)
    return row


def local_kernel(*refs):
    (cond, diag, slab, east, south), held, sem = refs[11:16], refs[16:27], refs[27]
    copies = [
        pltpu.make_async_copy(refs[i], held[i], sem.at[i]) for i in range(11)
    ]
    for copy in copies:
        copy.start()
    for copy in copies:
        copy.wait()
    (pressure, rhs, geology, ks, alpha, expo, land, ponding, slope_class, slope, flow) = held
    t_ks = gather_table(ks, 16)
    t_la = jnp.log(gather_table(alpha, 16))
    t_n = gather_table(expo, 16)
    t_m = 1.0 - 1.0 / t_n
    t_slope = jnp.sqrt(gather_table(slope, 8)) / 0.03
    sea = 4.0 * (1.0 - land[...].astype(F32))
    for l in range(LAYERS):
        g = geology[l]
        p = jnp.abs(pressure[l])
        n = pick(t_n, g)
        m = pick(t_m, g)
        t = jnp.exp(n * (pick(t_la, g) + jnp.log(p)))
        one_t = 1.0 + t
        e = jnp.exp(-m * jnp.log(one_t))
        k = pick(t_ks, g) * e
        d = 0.05 + 0.4 * m * n * t * e / (p * one_t) + sea
        cond[l] = k
        diag[l] = d
        for f, x in enumerate((rhs[l], k, d)):
            slab[f * LAYERS + l] = x[0 : E - X]
    out = pick(t_slope, slope_class[...]) * jnp.exp((5.0 / 3.0) * jnp.log(ponding[...]))
    eastward = jnp.where(flow[...] == 0, out, 0.0)
    east[...] = eastward
    south[...] = out - eastward


def pack_kernel(rhs, cond, diag, after, south, packed):
    for lo, rows in ((0, X), (X, E - X)):
        lane = iota((rows, Y), 1)
        total = jnp.zeros((rows, Y), F32)
        for f, ref in enumerate((rhs, cond, diag)):
            for l in range(LAYERS):
                q = f * LAYERS + l
                x = pltpu.roll(after[q] if lo else ref[l], (W + G * q) % Y, 1)
                total = jnp.where((lane >= G * q) & (lane < G * q + G), x, total)
        if not lo:
            x = pltpu.roll(south[...], (W + G * FIELDS) % Y, 1)
            total = jnp.where(lane >= G * FIELDS, x, total)
        packed[lo : lo + rows, :] = total


def krylov_kernel(
    rhs, cond, diag, after, right, left, east, v1_out, v2_out, row_out, back_out,
    fr, fc, fv, dd, v,
):
    lane, row_of = iota((E, Y), 1), iota((E, Y), 0)
    first, last = lane == 0, lane == Y - 1
    x, y = lax.axis_index("gx"), lax.axis_index("gy")
    x_end, y_end = x == lax.axis_size("gx") - 1, y == lax.axis_size("gy") - 1
    closed_rows = (row_of == 0) | (row_of == jnp.where(x_end, X, 0))
    closed_lanes = (
        lane == jnp.where(y == 0, 0, -1),
        lane == jnp.where(y_end, 0, -1),
    )

    def turn(m, h, by, edge):
        m, h = pltpu.roll(m, by, 1), pltpu.roll(h, by, 1)
        return jnp.where(edge, h, m), jnp.where(edge, m, h)

    w = jnp.where(lane % G >= W, right[...], left[...])

    def both(ref, f, l):
        q = f * LAYERS + l
        return (
            jnp.concatenate([ref[l], after[q]], axis=0),
            pltpu.roll(w, (-(W + G * q)) % Y, 1),
        )

    def harmonic(a, b):
        return 2.0 * a * b / jnp.maximum(a + b, 1e-30)

    above = None
    for l in range(LAYERS):
        v[0, l], v[1, l] = both(rhs, 0, l)
        k = both(cond, 1, l)
        dd[0, l], dd[1, l] = both(diag, 2, l)
        west = turn(*k, 1, first)
        for s in range(2):
            fr[s, l] = jnp.where(
                closed_rows, 0.0, harmonic(k[s], pltpu.roll(k[s], 1, 0))
            )
            fc[s, l] = jnp.where(closed_lanes[s], 0.0, harmonic(k[s], west[s]))
            if l:
                fv[s, l - 1] = harmonic(k[s], above[s])
        above = k

    def product(l, flux_above):
        vm, vh = v[0, l], v[1, l]
        west = turn(vm, vh, 1, first)
        side = fc[0, l] * (vm - west[0]), fc[1, l] * (vh - west[1])
        gone = turn(*side, Y - 1, last)
        outs, flux = [], []
        for s, x in enumerate((vm, vh)):
            rows = fr[s, l] * (x - pltpu.roll(x, 1, 0))
            r = dd[s, l] * x + (rows - pltpu.roll(rows, E - 1, 0)) + (side[s] - gone[s])
            if l:
                r = r - flux_above[s]
            if l < LAYERS - 1:
                fl = fv[s, l] * (x - v[s, l + 1])
                r = r + fl
                flux.append(fl)
            outs.append(r)
        return outs, flux

    zero = jnp.zeros((8, Y), F32)
    sums = [(zero, zero)] * 6
    sub = iota((8, Y), 0)
    start, stop = jnp.where(x == 0, 0, W), jnp.where(x_end, 0, W)

    def add_to(j, a, b):
        p, e = two_prod(a, b)
        s, e2 = two_sum(sums[j][0], p)
        sums[j] = s, sums[j][1] + (e + e2)

    for step in range(3):
        results, flux = [], None
        for l in range(LAYERS):
            outs, flux = product(l, flux)
            old, new = v[0, l], outs[0]
            for i in range(0, E, 8):
                a, b = old[i : i + 8], new[i : i + 8]
                if i == 0 or i == X:
                    keep = sub >= start if i == 0 else sub < stop
                    a, b = jnp.where(keep, a, 0.0), jnp.where(keep, b, 0.0)
                add_to(2 * step, a, a)
                add_to(2 * step + 1, a, b)
            results.append(outs)
        if step < 2:
            for l in range(LAYERS):
                m = results[l][0]
                v[0, l], v[1, l] = results[l]
                (v1_out, v2_out)[step][l] = m[0:X]
                if step:
                    back_out[LAYERS + 2 * l : LAYERS + 2 * l + 2, :] = m[X : X + 2]
                else:
                    back_out[l : l + 1, :] = m[X : X + 1]
    back_out[3 * LAYERS : 3 * LAYERS + 1, :] = east[X - 1 : X, :]

    ln = iota((8, Y), 1)
    total = zero, zero
    for j in range(6):
        s = fold(sums[j], (4, 2, 1), 0)
        total = tuple(jnp.where(sub == j, a, b) for a, b in zip(s, total))
    total = renorm(*fold(total, (64, 32, 16, 8, 4, 2, 1), 1))
    row = jnp.where(ln == sub, total[0], jnp.where(ln == sub + 8, total[1], 0.0))
    row = jnp.sum(row, axis=0, keepdims=True)
    row_out[...] = jnp.broadcast_to(row, row_out.shape)


def fold(s, steps, dim):
    for by in steps:
        hi, e = two_sum(s[0], pltpu.roll(s[0], by, dim))
        s = hi, s[1] + pltpu.roll(s[1], by, dim) + e
    return s


def rows_total(ref):
    parts = [
        (ref[i : i + 8, :], pltpu.roll(ref[i : i + 8, :], Y - 8, 1))
        for i in range(0, ref.shape[0], 8)
    ]
    while len(parts) > 1:
        parts = [pair_add(a, b) for a, b in zip(parts[::2], parts[1::2])]
    return renorm(*fold(parts[0], (4, 2, 1), 0))


def relay_kernel(rows, row_out):
    hi, lo = rows_total(rows)
    ln = iota((8, Y), 1)
    both = jnp.where(ln < 8, hi, pltpu.roll(lo, 8, 1))
    for i in range(0, row_out.shape[0], 8):
        row_out[i : i + 8, :] = both


def soil_kernel(
    state_hbm, soil_class, land, inverse, base, water, head, w, w01, state, sem
):
    copy = pltpu.make_async_copy(state_hbm, state, sem)
    copy.start()
    w[...] = jnp.zeros(w.shape, F32)
    w01[...] = jnp.zeros(w01.shape, F32)
    for e in range(CLASSES):
        x = inverse[e]
        w[0:STATE, e * PAD : e * PAD + STATE] = x
        w01[0:STATE, e : e + 1] = x[:, 0:1]
        w01[PAD : PAD + STATE, e : e + 1] = x[:, 1:2]
    w_all, w_two = w[...], w01[...]
    copy.wait()
    zero = jnp.zeros((PAD - STATE, Y), F32)
    entry = iota((16, Y), 0)

    def dot(a, columns):
        return jnp.dot(
            a,
            jnp.concatenate(columns, axis=1),
            precision=lax.Precision.HIGHEST,
            preferred_element_type=F32,
        )

    for x0 in range(0, X, 4):
        fields, spread, hot, kinds = [], [], [], []
        for x in range(x0, x0 + 4):
            f = state[pl.ds(x, STATE, stride=X), :]
            kind = jnp.where(land[x : x + 1, :] == 1, soil_class[x : x + 1, :], -1)
            padded = jnp.concatenate([f, zero], axis=0)
            spread.append(
                jnp.concatenate(
                    [jnp.where(kind == e, padded, 0.0) for e in range(CLASSES)], axis=0
                )
            )
            hot.append(jnp.where(kind == entry, 0.5, 0.0))
            fields.append(f)
            kinds.append(kind)
        solved, two = dot(w_all, spread), dot(w_two, hot)
        for n in range(4):
            here = pl.ds(x0 + n, STATE, stride=X)
            cut = slice(n * Y, n * Y + Y)
            base[here, :] = jnp.where(kinds[n] >= 0, solved[0:STATE, cut], fields[n])
            water[here, :] = two[0:STATE, cut]
            head[here, :] = two[PAD : PAD + STATE, cut]


def final_kernel(
    rows, rhs, v1, v2, back, base, water, head, left, east, south, ponding, land,
    corr_out, pond_out, soil_out,
):
    hi, lo = rows_total(rows)
    mu = [
        tuple(jnp.broadcast_to(t[:, j : j + 1], (8, Y)) for t in (hi, lo))
        for j in range(6)
    ]
    l21 = pair_div(mu[2], mu[1])
    l31 = pair_div(mu[3], mu[1])
    d2 = pair_sub(mu[3], pair_mul(l21, mu[2]))
    u = pair_sub(mu[4], pair_mul(l31, mu[2]))
    l32 = pair_div(u, d2)
    d3 = pair_sub(pair_sub(mu[5], pair_mul(l31, mu[3])), pair_mul(l32, u))
    y2 = pair_sub(mu[1], pair_mul(l21, mu[0]))
    y3 = pair_sub(pair_sub(mu[2], pair_mul(l31, mu[0])), pair_mul(l32, y2))
    c3 = pair_div(y3, d3)
    c2 = pair_sub(pair_div(y2, d2), pair_mul(l32, c3))
    c1 = pair_sub(
        pair_sub(pair_div(mu[0], mu[1]), pair_mul(l21, c2)), pair_mul(l31, c3)
    )
    c1, c2, c3 = (jnp.concatenate([c[0]] * (X // 8), axis=0) for c in (c1, c2, c3))

    row, lane = iota((X, Y), 0), iota((X, Y), 1)
    es, so = east[...], south[...]
    north = pltpu.roll(left[0:X, :], (-(W + G * FIELDS)) % Y, 1)
    given = jnp.where(lax.axis_index("gx") == 0, 0, 1)
    west = jnp.where(given == 0, 0.0, back[3 * LAYERS : 3 * LAYERS + 1, :])
    north = jnp.where(lax.axis_index("gy") == 0, 0.0, pltpu.roll(north, 1, 1))
    inflow = jnp.where(row == 0, west, pltpu.roll(es, 1, 0)) + jnp.where(
        lane == 0, north, pltpu.roll(so, 1, 1)
    )
    pond = land[...].astype(F32) * (ponding[...] + 0.2 * (inflow - (es + so)))
    pond_out[...] = pond

    top = None
    for l in range(LAYERS):
        q = LAYERS + 2 * l
        a1 = jnp.where(row < given, back[l : l + 1, :], v1[l])
        a2 = jnp.where(row < given, back[q : q + 1, :], v2[l])
        a2 = jnp.where((row == 1) & (given > 0), back[q + 1 : q + 2, :], a2)
        x = c1 * rhs[l] + c2 * a1 + c3 * a2
        corr_out[l] = x
        top = x if top is None else top
    for i in range(STATE):
        here = slice(i * X, i * X + X)
        soil_out[i] = base[here, :] + water[here, :] * pond + head[here, :] * top


def ahead(x, axis):
    n = lax.axis_size(axis)
    return lax.ppermute(x, axis, [(i, (i + 1) % n) for i in range(n)])


def back(x, axis):
    n = lax.axis_size(axis)
    return lax.ppermute(x, axis, [((i + 1) % n, i) for i in range(n)])


def everyones(rows, axis):
    count = lax.axis_size(axis)
    return lax.all_to_all(rows.reshape(count, 1, Y), axis, 0, 0).reshape(count, Y)


def on_device(
    pressure, newton_rhs, geology, saturated_conductivity, genuchten_alpha,
    genuchten_exponent, land_mask, ponding, slope_class, slope_table,
    flow_direction, soil_class, soil_inverse, soil_state,
):
    block, plane, tall = (LAYERS, X, Y), (X, Y), (STATE * X, Y)
    local = (
        pressure, newton_rhs, geology, saturated_conductivity, genuchten_alpha,
        genuchten_exponent, land_mask, ponding, slope_class, slope_table,
        flow_direction,
    )
    cond, diag, slab, east, south = call(
        local_kernel,
        [block, block, (FIELDS, E - X, Y), plane, plane],
        [(pltpu.SMEM if a.ndim == 1 else pltpu.VMEM)(a.shape, a.dtype) for a in local]
        + [pltpu.SemaphoreType.DMA((len(local),))],
        [pl.BlockSpec(memory_space=pltpu.HBM)] * len(local),
    )(*(pltpu.with_memory_space_constraint(a, pltpu.HBM) for a in local))
    after = back(slab, "gx")
    (packed,) = call(pack_kernel, [(E, Y)])(newton_rhs, cond, diag, after, south)
    left, right = ahead(packed, "gy"), back(packed, "gy")
    v1, v2, rows, edge = call(
        krylov_kernel,
        [block, block, (lax.axis_size("gy"), Y), (16, Y)],
        [pltpu.VMEM((2, n, E, Y), F32) for n in (5, 5, 4, 5, 5)],
    )(newton_rhs, cond, diag, after, right, left, east)
    edge = ahead(edge, "gx")
    rows = everyones(rows, "gy")
    (rows,) = call(relay_kernel, [(lax.axis_size("gx"), Y)])(rows)
    rows, kinds = lax.optimization_barrier((rows, soil_class))
    base, water, head = call(
        soil_kernel,
        [tall] * 3,
        [
            pltpu.VMEM((PAD, CLASSES * PAD), F32),
            pltpu.VMEM((2 * PAD, 16), F32),
            pltpu.VMEM(tall, F32),
            pltpu.SemaphoreType.DMA,
        ],
        [pl.BlockSpec(memory_space=pltpu.HBM)] + [pl.BlockSpec()] * 3,
        flops=20_000_000,
        nbytes=2_000_000,
    )(
        pltpu.with_memory_space_constraint(soil_state.reshape(tall), pltpu.HBM),
        kinds, land_mask, soil_inverse,
    )
    rows = everyones(rows, "gx")
    return call(final_kernel, [block, plane, (STATE, X, Y)])(
        rows, newton_rhs, v1, v2, edge, base, water, head, left, east, south,
        ponding, land_mask,
    )


def solution(mesh):
    cells, plane, rest = P(None, "gx", "gy"), P("gx", "gy"), P()
    return jax.shard_map(
        on_device,
        mesh=mesh,
        in_specs=(
            cells, cells, cells, rest, rest, rest, plane, plane, plane, rest, plane,
            plane, rest, cells,
        ),
        out_specs=(cells, plane, cells),
        check_vma=False,
    )
```

```python
import jax
import jax.numpy as jnp
from jax import lax
from jax.experimental import pallas as pl
from jax.experimental.pallas import tpu as pltpu
from jax.sharding import PartitionSpec as P


LAYERS = 5
STATE = 20
CLASSES = 12
W = 3
X, Y = 32, 128
E = X + 8
FIELDS = 3 * LAYERS
G = 2 * W
PAD = 24
F32 = jnp.float32


def two_sum(a, b):
    s = a + b
    t = s - a
    return s, (a - (s - t)) + (b - t)


def renorm(a, b):
    s = a + b
    return s, b - (s - a)


def halves(a):
    t = a * 4097.0
    hi = t - (t - a)
    return hi, a - hi


def two_prod(a, b):
    p = a * b
    (ah, al), (bh, bl) = halves(a), halves(b)
    return p, ((ah * bh - p) + ah * bl + al * bh) + al * bl


def pair_add(a, b):
    s, e = two_sum(a[0], b[0])
    return renorm(s, e + (a[1] + b[1]))


def pair_sub(a, b):
    return pair_add(a, (-b[0], -b[1]))


def pair_mul(a, b):
    p, e = two_prod(a[0], b[0])
    return renorm(p, e + (a[0] * b[1] + a[1] * b[0]))


def pair_div(a, b):
    q = a[0] / b[0]
    r = pair_sub(a, pair_mul((q, jnp.zeros_like(q)), b))
    q2 = r[0] / b[0]
    r = pair_sub(r, pair_mul((q2, jnp.zeros_like(q)), b))
    return pair_add(renorm(q, q2), (r[0] / b[0], jnp.zeros_like(q)))


def iota(shape, dim):
    return lax.broadcasted_iota(jnp.int32, shape, dim)


def pick(table, index):
    row = jnp.broadcast_to(table, index.shape)
    return jnp.take_along_axis(row, index, axis=1, mode="promise_in_bounds")


def call(kernel, outs, scratch=(), specs=None, flops=0, nbytes=0):
    extra = {} if specs is None else {"in_specs": specs}
    return pl.pallas_call(
        kernel,
        out_shape=[jax.ShapeDtypeStruct(s, F32) for s in outs],
        scratch_shapes=scratch,
        compiler_params=pltpu.CompilerParams(vmem_limit_bytes=32 * 2**20),
        cost_estimate=pl.CostEstimate(
            flops=flops, bytes_accessed=nbytes, transcendentals=0
        ),
        **extra,
    )


def gather_table(ref, count):
    lane = iota((1, Y), 1)
    row = jnp.full((1, Y), 1.0, F32)
    for i in range(count):
        row = jnp.where(lane == i, ref[i], row)
    return row


def local_kernel(*refs):
    (cond, diag, slab, east, south), held, sem = refs[11:16], refs[16:27], refs[27]
    copies = [
        pltpu.make_async_copy(refs[i], held[i], sem.at[i]) for i in range(11)
    ]
    for copy in copies:
        copy.start()
    for copy in copies:
        copy.wait()
    (pressure, rhs, geology, ks, alpha, expo, land, ponding, slope_class, slope, flow) = held
    t_ks = gather_table(ks, 16)
    t_la = jnp.log(gather_table(alpha, 16))
    t_n = gather_table(expo, 16)
    t_m = 1.0 - 1.0 / t_n
    t_slope = jnp.sqrt(gather_table(slope, 8)) / 0.03
    sea = 4.0 * (1.0 - land[...].astype(F32))
    for l in range(LAYERS):
        g = geology[l]
        p = jnp.abs(pressure[l])
        n = pick(t_n, g)
        m = pick(t_m, g)
        t = jnp.exp(n * (pick(t_la, g) + jnp.log(p)))
        one_t = 1.0 + t
        e = jnp.exp(-m * jnp.log(one_t))
        k = pick(t_ks, g) * e
        d = 0.05 + 0.4 * m * n * t * e / (p * one_t) + sea
        cond[l] = k
        diag[l] = d
        for f, x in enumerate((rhs[l], k, d)):
            slab[f * LAYERS + l] = x[0 : E - X]
    out = pick(t_slope, slope_class[...]) * jnp.exp((5.0 / 3.0) * jnp.log(ponding[...]))
    eastward = jnp.where(flow[...] == 0, out, 0.0)
    east[...] = eastward
    south[...] = out - eastward


def pack_kernel(rhs, cond, diag, after, south, packed):
    for lo, rows in ((0, X), (X, E - X)):
        lane = iota((rows, Y), 1)
        total = jnp.zeros((rows, Y), F32)
        for f, ref in enumerate((rhs, cond, diag)):
            for l in range(LAYERS):
                q = f * LAYERS + l
                x = pltpu.roll(after[q] if lo else ref[l], (W + G * q) % Y, 1)
                total = jnp.where((lane >= G * q) & (lane < G * q + G), x, total)
        if not lo:
            x = pltpu.roll(south[...], (W + G * FIELDS) % Y, 1)
            total = jnp.where(lane >= G * FIELDS, x, total)
        packed[lo : lo + rows, :] = total


def krylov_kernel(
    rhs, cond, diag, after, right, left, east, v1_out, v2_out, row_out, back_out,
    fr, fc, fv, dd, v,
):
    lane, row_of = iota((E, Y), 1), iota((E, Y), 0)
    first, last = lane == 0, lane == Y - 1
    x, y = lax.axis_index("gx"), lax.axis_index("gy")
    x_end, y_end = x == lax.axis_size("gx") - 1, y == lax.axis_size("gy") - 1
    closed_rows = (row_of == 0) | (row_of == jnp.where(x_end, X, 0))
    closed_lanes = (
        lane == jnp.where(y == 0, 0, -1),
        lane == jnp.where(y_end, 0, -1),
    )

    def turn(m, h, by, edge):
        m, h = pltpu.roll(m, by, 1), pltpu.roll(h, by, 1)
        return jnp.where(edge, h, m), jnp.where(edge, m, h)

    w = jnp.where(lane % G >= W, right[...], left[...])

    def both(ref, f, l):
        q = f * LAYERS + l
        return (
            jnp.concatenate([ref[l], after[q]], axis=0),
            pltpu.roll(w, (-(W + G * q)) % Y, 1),
        )

    def harmonic(a, b):
        return 2.0 * a * b / jnp.maximum(a + b, 1e-30)

    above = None
    for l in range(LAYERS):
        v[0, l], v[1, l] = both(rhs, 0, l)
        k = both(cond, 1, l)
        dd[0, l], dd[1, l] = both(diag, 2, l)
        west = turn(*k, 1, first)
        for s in range(2):
            fr[s, l] = jnp.where(
                closed_rows, 0.0, harmonic(k[s], pltpu.roll(k[s], 1, 0))
            )
            fc[s, l] = jnp.where(closed_lanes[s], 0.0, harmonic(k[s], west[s]))
            if l:
                fv[s, l - 1] = harmonic(k[s], above[s])
        above = k

    def product(l, flux_above):
        vm, vh = v[0, l], v[1, l]
        west = turn(vm, vh, 1, first)
        side = fc[0, l] * (vm - west[0]), fc[1, l] * (vh - west[1])
        gone = turn(*side, Y - 1, last)
        outs, flux = [], []
        for s, x in enumerate((vm, vh)):
            rows = fr[s, l] * (x - pltpu.roll(x, 1, 0))
            r = dd[s, l] * x + (rows - pltpu.roll(rows, E - 1, 0)) + (side[s] - gone[s])
            if l:
                r = r - flux_above[s]
            if l < LAYERS - 1:
                fl = fv[s, l] * (x - v[s, l + 1])
                r = r + fl
                flux.append(fl)
            outs.append(r)
        return outs, flux

    zero = jnp.zeros((8, Y), F32)
    sums = [(zero, zero)] * 6
    sub = iota((8, Y), 0)
    start, stop = jnp.where(x == 0, 0, W), jnp.where(x_end, 0, W)

    def add_to(j, a, b):
        p, e = two_prod(a, b)
        s, e2 = two_sum(sums[j][0], p)
        sums[j] = s, sums[j][1] + (e + e2)

    for step in range(3):
        results, flux = [], None
        for l in range(LAYERS):
            outs, flux = product(l, flux)
            old, new = v[0, l], outs[0]
            for i in range(0, E, 8):
                a, b = old[i : i + 8], new[i : i + 8]
                if i == 0 or i == X:
                    keep = sub >= start if i == 0 else sub < stop
                    a, b = jnp.where(keep, a, 0.0), jnp.where(keep, b, 0.0)
                add_to(2 * step, a, a)
                add_to(2 * step + 1, a, b)
            results.append(outs)
        if step < 2:
            for l in range(LAYERS):
                m = results[l][0]
                v[0, l], v[1, l] = results[l]
                (v1_out, v2_out)[step][l] = m[0:X]
                if step:
                    back_out[LAYERS + 2 * l : LAYERS + 2 * l + 2, :] = m[X : X + 2]
                else:
                    back_out[l : l + 1, :] = m[X : X + 1]
    back_out[3 * LAYERS : 3 * LAYERS + 1, :] = east[X - 1 : X, :]

    ln = iota((8, Y), 1)
    total = zero, zero
    for j in range(6):
        s = fold(sums[j], (4, 2, 1), 0)
        total = tuple(jnp.where(sub == j, a, b) for a, b in zip(s, total))
    total = renorm(*fold(total, (64, 32, 16, 8, 4, 2, 1), 1))
    row = jnp.where(ln == sub, total[0], jnp.where(ln == sub + 8, total[1], 0.0))
    row = jnp.sum(row, axis=0, keepdims=True)
    row_out[...] = jnp.broadcast_to(row, row_out.shape)


def fold(s, steps, dim):
    for by in steps:
        hi, e = two_sum(s[0], pltpu.roll(s[0], by, dim))
        s = hi, s[1] + pltpu.roll(s[1], by, dim) + e
    return s


def rows_total(ref):
    parts = [
        (ref[i : i + 8, :], pltpu.roll(ref[i : i + 8, :], Y - 8, 1))
        for i in range(0, ref.shape[0], 8)
    ]
    while len(parts) > 1:
        parts = [pair_add(a, b) for a, b in zip(parts[::2], parts[1::2])]
    return renorm(*fold(parts[0], (4, 2, 1), 0))


def relay_kernel(rows, row_out):
    hi, lo = rows_total(rows)
    ln = iota((8, Y), 1)
    both = jnp.where(ln < 8, hi, pltpu.roll(lo, 8, 1))
    for i in range(0, row_out.shape[0], 8):
        row_out[i : i + 8, :] = both


def soil_kernel(state, soil_class, land, inverse, base, water, head, w, w01):
    w[...] = jnp.zeros(w.shape, F32)
    w01[...] = jnp.zeros(w01.shape, F32)
    for e in range(CLASSES):
        x = inverse[e]
        w[0:STATE, e * PAD : e * PAD + STATE] = x
        w01[0:STATE, e : e + 1] = x[:, 0:1]
        w01[PAD : PAD + STATE, e : e + 1] = x[:, 1:2]
    w_all, w_two = w[...], w01[...]
    zero = jnp.zeros((PAD - STATE, Y), F32)
    entry = iota((16, Y), 0)

    def dot(a, columns):
        return jnp.dot(
            a,
            jnp.concatenate(columns, axis=1),
            precision=lax.Precision.HIGHEST,
            preferred_element_type=F32,
        )

    for x0 in range(0, X, 4):
        fields, spread, hot, kinds = [], [], [], []
        for x in range(x0, x0 + 4):
            f = state[pl.ds(x, STATE, stride=X), :]
            kind = jnp.where(land[x : x + 1, :] == 1, soil_class[x : x + 1, :], -1)
            padded = jnp.concatenate([f, zero], axis=0)
            spread.append(
                jnp.concatenate(
                    [jnp.where(kind == e, padded, 0.0) for e in range(CLASSES)], axis=0
                )
            )
            hot.append(jnp.where(kind == entry, 0.5, 0.0))
            fields.append(f)
            kinds.append(kind)
        solved, two = dot(w_all, spread), dot(w_two, hot)
        for n in range(4):
            here = pl.ds(x0 + n, STATE, stride=X)
            cut = slice(n * Y, n * Y + Y)
            base[here, :] = jnp.where(kinds[n] >= 0, solved[0:STATE, cut], fields[n])
            water[here, :] = two[0:STATE, cut]
            head[here, :] = two[PAD : PAD + STATE, cut]


def final_kernel(
    rows, rhs, v1, v2, back, base, water, head, left, east, south, ponding, land,
    corr_out, pond_out, soil_out,
):
    hi, lo = rows_total(rows)
    mu = [
        tuple(jnp.broadcast_to(t[:, j : j + 1], (8, Y)) for t in (hi, lo))
        for j in range(6)
    ]
    l21 = pair_div(mu[2], mu[1])
    l31 = pair_div(mu[3], mu[1])
    d2 = pair_sub(mu[3], pair_mul(l21, mu[2]))
    u = pair_sub(mu[4], pair_mul(l31, mu[2]))
    l32 = pair_div(u, d2)
    d3 = pair_sub(pair_sub(mu[5], pair_mul(l31, mu[3])), pair_mul(l32, u))
    y2 = pair_sub(mu[1], pair_mul(l21, mu[0]))
    y3 = pair_sub(pair_sub(mu[2], pair_mul(l31, mu[0])), pair_mul(l32, y2))
    c3 = pair_div(y3, d3)
    c2 = pair_sub(pair_div(y2, d2), pair_mul(l32, c3))
    c1 = pair_sub(
        pair_sub(pair_div(mu[0], mu[1]), pair_mul(l21, c2)), pair_mul(l31, c3)
    )
    c1, c2, c3 = (jnp.concatenate([c[0]] * (X // 8), axis=0) for c in (c1, c2, c3))

    row, lane = iota((X, Y), 0), iota((X, Y), 1)
    es, so = east[...], south[...]
    north = pltpu.roll(left[0:X, :], (-(W + G * FIELDS)) % Y, 1)
    given = jnp.where(lax.axis_index("gx") == 0, 0, 1)
    west = jnp.where(given == 0, 0.0, back[3 * LAYERS : 3 * LAYERS + 1, :])
    north = jnp.where(lax.axis_index("gy") == 0, 0.0, pltpu.roll(north, 1, 1))
    inflow = jnp.where(row == 0, west, pltpu.roll(es, 1, 0)) + jnp.where(
        lane == 0, north, pltpu.roll(so, 1, 1)
    )
    pond = land[...].astype(F32) * (ponding[...] + 0.2 * (inflow - (es + so)))
    pond_out[...] = pond

    top = None
    for l in range(LAYERS):
        q = LAYERS + 2 * l
        a1 = jnp.where(row < given, back[l : l + 1, :], v1[l])
        a2 = jnp.where(row < given, back[q : q + 1, :], v2[l])
        a2 = jnp.where((row == 1) & (given > 0), back[q + 1 : q + 2, :], a2)
        x = c1 * rhs[l] + c2 * a1 + c3 * a2
        corr_out[l] = x
        top = x if top is None else top
    for i in range(STATE):
        here = slice(i * X, i * X + X)
        soil_out[i] = base[here, :] + water[here, :] * pond + head[here, :] * top


def ahead(x, axis):
    n = lax.axis_size(axis)
    return lax.ppermute(x, axis, [(i, (i + 1) % n) for i in range(n)])


def back(x, axis):
    n = lax.axis_size(axis)
    return lax.ppermute(x, axis, [((i + 1) % n, i) for i in range(n)])


def everyones(rows, axis):
    count = lax.axis_size(axis)
    return lax.all_to_all(rows.reshape(count, 1, Y), axis, 0, 0).reshape(count, Y)


def on_device(
    pressure, newton_rhs, geology, saturated_conductivity, genuchten_alpha,
    genuchten_exponent, land_mask, ponding, slope_class, slope_table,
    flow_direction, soil_class, soil_inverse, soil_state,
):
    block, plane, tall = (LAYERS, X, Y), (X, Y), (STATE * X, Y)
    local = (
        pressure, newton_rhs, geology, saturated_conductivity, genuchten_alpha,
        genuchten_exponent, land_mask, ponding, slope_class, slope_table,
        flow_direction,
    )
    cond, diag, slab, east, south = call(
        local_kernel,
        [block, block, (FIELDS, E - X, Y), plane, plane],
        [(pltpu.SMEM if a.ndim == 1 else pltpu.VMEM)(a.shape, a.dtype) for a in local]
        + [pltpu.SemaphoreType.DMA((len(local),))],
        [pl.BlockSpec(memory_space=pltpu.HBM)] * len(local),
    )(*(pltpu.with_memory_space_constraint(a, pltpu.HBM) for a in local))
    after = back(slab, "gx")
    (packed,) = call(pack_kernel, [(E, Y)])(newton_rhs, cond, diag, after, south)
    left, right = ahead(packed, "gy"), back(packed, "gy")
    v1, v2, rows, edge = call(
        krylov_kernel,
        [block, block, (lax.axis_size("gy"), Y), (16, Y)],
        [pltpu.VMEM((2, n, E, Y), F32) for n in (5, 5, 4, 5, 5)],
    )(newton_rhs, cond, diag, after, right, left, east)
    edge = ahead(edge, "gx")
    rows = everyones(rows, "gy")
    (rows,) = call(relay_kernel, [(lax.axis_size("gx"), Y)])(rows)
    rows, kinds = lax.optimization_barrier((rows, soil_class))
    base, water, head = call(
        soil_kernel,
        [tall] * 3,
        [
            pltpu.VMEM((PAD, CLASSES * PAD), F32),
            pltpu.VMEM((2 * PAD, 16), F32),
        ],
        flops=20_000_000,
        nbytes=2_000_000,
    )(soil_state.reshape(tall), kinds, land_mask, soil_inverse)
    rows = everyones(rows, "gx")
    return call(final_kernel, [block, plane, (STATE, X, Y)])(
        rows, newton_rhs, v1, v2, edge, base, water, head, left, east, south,
        ponding, land_mask,
    )


def solution(mesh):
    cells, plane, rest = P(None, "gx", "gy"), P("gx", "gy"), P()
    return jax.shard_map(
        on_device,
        mesh=mesh,
        in_specs=(
            cells, cells, cells, rest, rest, rest, plane, plane, plane, rest, plane,
            plane, rest, cells,
        ),
        out_specs=(cells, plane, cells),
        check_vma=False,
    )
```

```python
import jax
import jax.numpy as jnp
from jax import lax
from jax.experimental import pallas as pl
from jax.experimental.pallas import tpu as pltpu
from jax.sharding import PartitionSpec as P


LAYERS = 5
STATE = 20
CLASSES = 12
W = 3
X, Y = 32, 128
E = X + 8
FIELDS = 3 * LAYERS
G = 2 * W
PAD = 24
F32 = jnp.float32


def two_sum(a, b):
    s = a + b
    t = s - a
    return s, (a - (s - t)) + (b - t)


def renorm(a, b):
    s = a + b
    return s, b - (s - a)


def halves(a):
    t = a * 4097.0
    hi = t - (t - a)
    return hi, a - hi


def two_prod(a, b):
    p = a * b
    (ah, al), (bh, bl) = halves(a), halves(b)
    return p, ((ah * bh - p) + ah * bl + al * bh) + al * bl


def pair_add(a, b):
    s, e = two_sum(a[0], b[0])
    return renorm(s, e + (a[1] + b[1]))


def pair_sub(a, b):
    return pair_add(a, (-b[0], -b[1]))


def pair_mul(a, b):
    p, e = two_prod(a[0], b[0])
    return renorm(p, e + (a[0] * b[1] + a[1] * b[0]))


def pair_div(a, b):
    q = a[0] / b[0]
    r = pair_sub(a, pair_mul((q, jnp.zeros_like(q)), b))
    q2 = r[0] / b[0]
    r = pair_sub(r, pair_mul((q2, jnp.zeros_like(q)), b))
    return pair_add(renorm(q, q2), (r[0] / b[0], jnp.zeros_like(q)))


def iota(shape, dim):
    return lax.broadcasted_iota(jnp.int32, shape, dim)


def pick(table, index):
    row = jnp.broadcast_to(table, index.shape)
    return jnp.take_along_axis(row, index, axis=1, mode="promise_in_bounds")


def call(kernel, outs, scratch=(), specs=None, flops=0, nbytes=0):
    extra = {} if specs is None else {"in_specs": specs}
    return pl.pallas_call(
        kernel,
        out_shape=[jax.ShapeDtypeStruct(s, F32) for s in outs],
        scratch_shapes=scratch,
        compiler_params=pltpu.CompilerParams(vmem_limit_bytes=32 * 2**20),
        cost_estimate=pl.CostEstimate(
            flops=flops, bytes_accessed=nbytes, transcendentals=0
        ),
        **extra,
    )


def gather_table(ref, count):
    lane = iota((1, Y), 1)
    row = jnp.full((1, Y), 1.0, F32)
    for i in range(count):
        row = jnp.where(lane == i, ref[i], row)
    return row


def local_kernel(*refs):
    (cond, diag, slab, east, south, state), held, sem = refs[12:18], refs[18:29], refs[29]
    copies = [
        pltpu.make_async_copy(refs[i], (*held, state)[i], sem.at[i]) for i in range(12)
    ]
    for copy in copies:
        copy.start()
    for copy in copies[:11]:
        copy.wait()
    (pressure, rhs, geology, ks, alpha, expo, land, ponding, slope_class, slope, flow) = held
    t_ks = gather_table(ks, 16)
    t_la = jnp.log(gather_table(alpha, 16))
    t_n = gather_table(expo, 16)
    t_m = 1.0 - 1.0 / t_n
    t_slope = jnp.sqrt(gather_table(slope, 8)) / 0.03
    sea = 4.0 * (1.0 - land[...].astype(F32))
    for l in range(LAYERS):
        g = geology[l]
        p = jnp.abs(pressure[l])
        n = pick(t_n, g)
        m = pick(t_m, g)
        t = jnp.exp(n * (pick(t_la, g) + jnp.log(p)))
        one_t = 1.0 + t
        e = jnp.exp(-m * jnp.log(one_t))
        k = pick(t_ks, g) * e
        d = 0.05 + 0.4 * m * n * t * e / (p * one_t) + sea
        cond[l] = k
        diag[l] = d
        for f, x in enumerate((rhs[l], k, d)):
            slab[f * LAYERS + l] = x[0 : E - X]
    out = pick(t_slope, slope_class[...]) * jnp.exp((5.0 / 3.0) * jnp.log(ponding[...]))
    eastward = jnp.where(flow[...] == 0, out, 0.0)
    east[...] = eastward
    south[...] = out - eastward
    copies[11].wait()


def pack_kernel(rhs, cond, diag, after, south, packed):
    for lo, rows in ((0, X), (X, E - X)):
        lane = iota((rows, Y), 1)
        total = jnp.zeros((rows, Y), F32)
        for f, ref in enumerate((rhs, cond, diag)):
            for l in range(LAYERS):
                q = f * LAYERS + l
                x = pltpu.roll(after[q] if lo else ref[l], (W + G * q) % Y, 1)
                total = jnp.where((lane >= G * q) & (lane < G * q + G), x, total)
        if not lo:
            x = pltpu.roll(south[...], (W + G * FIELDS) % Y, 1)
            total = jnp.where(lane >= G * FIELDS, x, total)
        packed[lo : lo + rows, :] = total


def krylov_kernel(
    rhs, cond, diag, after, right, left, east, v1_out, v2_out, row_out, back_out,
    fr, fc, fv, dd, v,
):
    lane, row_of = iota((E, Y), 1), iota((E, Y), 0)
    first, last = lane == 0, lane == Y - 1
    x, y = lax.axis_index("gx"), lax.axis_index("gy")
    x_end, y_end = x == lax.axis_size("gx") - 1, y == lax.axis_size("gy") - 1
    closed_rows = (row_of == 0) | (row_of == jnp.where(x_end, X, 0))
    closed_lanes = (
        lane == jnp.where(y == 0, 0, -1),
        lane == jnp.where(y_end, 0, -1),
    )

    def turn(m, h, by, edge):
        m, h = pltpu.roll(m, by, 1), pltpu.roll(h, by, 1)
        return jnp.where(edge, h, m), jnp.where(edge, m, h)

    w = jnp.where(lane % G >= W, right[...], left[...])

    def both(ref, f, l):
        q = f * LAYERS + l
        return (
            jnp.concatenate([ref[l], after[q]], axis=0),
            pltpu.roll(w, (-(W + G * q)) % Y, 1),
        )

    def harmonic(a, b):
        return 2.0 * a * b / jnp.maximum(a + b, 1e-30)

    above = None
    for l in range(LAYERS):
        v[0, l], v[1, l] = both(rhs, 0, l)
        k = both(cond, 1, l)
        dd[0, l], dd[1, l] = both(diag, 2, l)
        west = turn(*k, 1, first)
        for s in range(2):
            fr[s, l] = jnp.where(
                closed_rows, 0.0, harmonic(k[s], pltpu.roll(k[s], 1, 0))
            )
            fc[s, l] = jnp.where(closed_lanes[s], 0.0, harmonic(k[s], west[s]))
            if l:
                fv[s, l - 1] = harmonic(k[s], above[s])
        above = k

    def product(l, flux_above):
        vm, vh = v[0, l], v[1, l]
        west = turn(vm, vh, 1, first)
        side = fc[0, l] * (vm - west[0]), fc[1, l] * (vh - west[1])
        gone = turn(*side, Y - 1, last)
        outs, flux = [], []
        for s, x in enumerate((vm, vh)):
            rows = fr[s, l] * (x - pltpu.roll(x, 1, 0))
            r = dd[s, l] * x + (rows - pltpu.roll(rows, E - 1, 0)) + (side[s] - gone[s])
            if l:
                r = r - flux_above[s]
            if l < LAYERS - 1:
                fl = fv[s, l] * (x - v[s, l + 1])
                r = r + fl
                flux.append(fl)
            outs.append(r)
        return outs, flux

    zero = jnp.zeros((8, Y), F32)
    sums = [(zero, zero)] * 6
    sub = iota((8, Y), 0)
    start, stop = jnp.where(x == 0, 0, W), jnp.where(x_end, 0, W)

    def add_to(j, a, b):
        p, e = two_prod(a, b)
        s, e2 = two_sum(sums[j][0], p)
        sums[j] = s, sums[j][1] + (e + e2)

    for step in range(3):
        results, flux = [], None
        for l in range(LAYERS):
            outs, flux = product(l, flux)
            old, new = v[0, l], outs[0]
            for i in range(0, E, 8):
                a, b = old[i : i + 8], new[i : i + 8]
                if i == 0 or i == X:
                    keep = sub >= start if i == 0 else sub < stop
                    a, b = jnp.where(keep, a, 0.0), jnp.where(keep, b, 0.0)
                add_to(2 * step, a, a)
                add_to(2 * step + 1, a, b)
            results.append(outs)
        if step < 2:
            for l in range(LAYERS):
                m = results[l][0]
                v[0, l], v[1, l] = results[l]
                (v1_out, v2_out)[step][l] = m[0:X]
                if step:
                    back_out[LAYERS + 2 * l : LAYERS + 2 * l + 2, :] = m[X : X + 2]
                else:
                    back_out[l : l + 1, :] = m[X : X + 1]
    back_out[3 * LAYERS : 3 * LAYERS + 1, :] = east[X - 1 : X, :]

    ln = iota((8, Y), 1)
    total = zero, zero
    for j in range(6):
        s = fold(sums[j], (4, 2, 1), 0)
        total = tuple(jnp.where(sub == j, a, b) for a, b in zip(s, total))
    total = renorm(*fold(total, (64, 32, 16, 8, 4, 2, 1), 1))
    row = jnp.where(ln == sub, total[0], jnp.where(ln == sub + 8, total[1], 0.0))
    row = jnp.sum(row, axis=0, keepdims=True)
    row_out[...] = jnp.broadcast_to(row, row_out.shape)


def fold(s, steps, dim):
    for by in steps:
        hi, e = two_sum(s[0], pltpu.roll(s[0], by, dim))
        s = hi, s[1] + pltpu.roll(s[1], by, dim) + e
    return s


def rows_total(ref):
    parts = [
        (ref[i : i + 8, :], pltpu.roll(ref[i : i + 8, :], Y - 8, 1))
        for i in range(0, ref.shape[0], 8)
    ]
    while len(parts) > 1:
        parts = [pair_add(a, b) for a, b in zip(parts[::2], parts[1::2])]
    return renorm(*fold(parts[0], (4, 2, 1), 0))


def relay_kernel(rows, row_out):
    hi, lo = rows_total(rows)
    ln = iota((8, Y), 1)
    both = jnp.where(ln < 8, hi, pltpu.roll(lo, 8, 1))
    for i in range(0, row_out.shape[0], 8):
        row_out[i : i + 8, :] = both


def soil_kernel(state, soil_class, land, inverse, base, w):
    w[...] = jnp.zeros(w.shape, F32)
    for e in range(CLASSES):
        x = inverse[e]
        w[0:STATE, 16 * e : 16 * e + 16] = x[:, 0:16]
        w[0:STATE, 192 + 4 * e : 196 + 4 * e] = x[:, 16:STATE]
    w_all = w[...]
    half = (iota((8, Y), 0) >= 4).astype(jnp.int32)
    for x0 in range(0, X, 4):
        fields, spread, kinds = [], [], []
        for x in range(x0, x0 + 4):
            f = state[pl.ds(x, STATE, stride=X), :]
            kind = jnp.where(land[x : x + 1, :] == 1, soil_class[x : x + 1, :], -1)
            twice = jnp.concatenate([f[16:STATE], f[16:STATE]], axis=0)
            parts = [jnp.where(kind == e, f[0:16], 0.0) for e in range(CLASSES)]
            for e in range(0, CLASSES, 2):
                parts.append(jnp.where(kind == e + half, twice, 0.0))
            spread.append(jnp.concatenate(parts, axis=0))
            fields.append(f)
            kinds.append(kind)
        solved = jnp.dot(
            w_all,
            jnp.concatenate(spread, axis=1),
            precision=lax.Precision.HIGHEST,
            preferred_element_type=F32,
        )
        for n in range(4):
            base[pl.ds(x0 + n, STATE, stride=X), :] = jnp.where(
                kinds[n] >= 0, solved[0:STATE, n * Y : n * Y + Y], fields[n]
            )


def unit_kernel(soil_class, land, inverse, water, head, table):
    for e in range(CLASSES):
        x = inverse[e]
        table[0:STATE, e : e + 1] = x[:, 0:1]
        table[PAD : PAD + STATE, e : e + 1] = x[:, 1:2]
    index = soil_class[...]
    half = 0.5 * land[...].astype(F32)
    for i in range(STATE):
        here = slice(i * X, i * X + X)
        water[here, :] = half * pick(table[i : i + 1, :], index)
        head[here, :] = half * pick(table[PAD + i : PAD + i + 1, :], index)


def final_kernel(
    rows, rhs, v1, v2, back, base, water, head, left, east, south, ponding, land,
    corr_out, pond_out, soil_out,
):
    hi, lo = rows_total(rows)
    mu = [
        tuple(jnp.broadcast_to(t[:, j : j + 1], (8, Y)) for t in (hi, lo))
        for j in range(6)
    ]
    l21 = pair_div(mu[2], mu[1])
    l31 = pair_div(mu[3], mu[1])
    d2 = pair_sub(mu[3], pair_mul(l21, mu[2]))
    u = pair_sub(mu[4], pair_mul(l31, mu[2]))
    l32 = pair_div(u, d2)
    d3 = pair_sub(pair_sub(mu[5], pair_mul(l31, mu[3])), pair_mul(l32, u))
    y2 = pair_sub(mu[1], pair_mul(l21, mu[0]))
    y3 = pair_sub(pair_sub(mu[2], pair_mul(l31, mu[0])), pair_mul(l32, y2))
    c3 = pair_div(y3, d3)
    c2 = pair_sub(pair_div(y2, d2), pair_mul(l32, c3))
    c1 = pair_sub(
        pair_sub(pair_div(mu[0], mu[1]), pair_mul(l21, c2)), pair_mul(l31, c3)
    )
    c1, c2, c3 = (jnp.concatenate([c[0]] * (X // 8), axis=0) for c in (c1, c2, c3))

    row, lane = iota((X, Y), 0), iota((X, Y), 1)
    es, so = east[...], south[...]
    north = pltpu.roll(left[0:X, :], (-(W + G * FIELDS)) % Y, 1)
    given = jnp.where(lax.axis_index("gx") == 0, 0, 1)
    west = jnp.where(given == 0, 0.0, back[3 * LAYERS : 3 * LAYERS + 1, :])
    north = jnp.where(lax.axis_index("gy") == 0, 0.0, pltpu.roll(north, 1, 1))
    inflow = jnp.where(row == 0, west, pltpu.roll(es, 1, 0)) + jnp.where(
        lane == 0, north, pltpu.roll(so, 1, 1)
    )
    pond = land[...].astype(F32) * (ponding[...] + 0.2 * (inflow - (es + so)))
    pond_out[...] = pond

    top = None
    for l in range(LAYERS):
        q = LAYERS + 2 * l
        a1 = jnp.where(row < given, back[l : l + 1, :], v1[l])
        a2 = jnp.where(row < given, back[q : q + 1, :], v2[l])
        a2 = jnp.where((row == 1) & (given > 0), back[q + 1 : q + 2, :], a2)
        x = c1 * rhs[l] + c2 * a1 + c3 * a2
        corr_out[l] = x
        top = x if top is None else top
    for i in range(STATE):
        here = slice(i * X, i * X + X)
        soil_out[i] = base[here, :] + water[here, :] * pond + head[here, :] * top


def ahead(x, axis):
    n = lax.axis_size(axis)
    return lax.ppermute(x, axis, [(i, (i + 1) % n) for i in range(n)])


def back(x, axis):
    n = lax.axis_size(axis)
    return lax.ppermute(x, axis, [((i + 1) % n, i) for i in range(n)])


def everyones(rows, axis):
    count = lax.axis_size(axis)
    return lax.all_to_all(rows.reshape(count, 1, Y), axis, 0, 0).reshape(count, Y)


def on_device(
    pressure, newton_rhs, geology, saturated_conductivity, genuchten_alpha,
    genuchten_exponent, land_mask, ponding, slope_class, slope_table,
    flow_direction, soil_class, soil_inverse, soil_state,
):
    block, plane, tall = (LAYERS, X, Y), (X, Y), (STATE * X, Y)
    local = (
        pressure, newton_rhs, geology, saturated_conductivity, genuchten_alpha,
        genuchten_exponent, land_mask, ponding, slope_class, slope_table,
        flow_direction, soil_state.reshape(tall),
    )
    cond, diag, slab, east, south, state = call(
        local_kernel,
        [block, block, (FIELDS, E - X, Y), plane, plane, tall],
        [
            (pltpu.SMEM if a.ndim == 1 else pltpu.VMEM)(a.shape, a.dtype)
            for a in local[:-1]
        ]
        + [pltpu.SemaphoreType.DMA((len(local),))],
        [pl.BlockSpec(memory_space=pltpu.HBM)] * len(local),
    )(*(pltpu.with_memory_space_constraint(a, pltpu.HBM) for a in local))
    after = back(slab, "gx")
    (base,) = call(
        soil_kernel, [tall], [pltpu.VMEM((PAD, 240), F32)], flops=20_000_000
    )(state, soil_class, land_mask, soil_inverse)
    after, base = lax.optimization_barrier((after, base))
    (packed,) = call(pack_kernel, [(E, Y)])(newton_rhs, cond, diag, after, south)
    left, right = ahead(packed, "gy"), back(packed, "gy")
    v1, v2, rows, edge = call(
        krylov_kernel,
        [block, block, (lax.axis_size("gy"), Y), (16, Y)],
        [pltpu.VMEM((2, n, E, Y), F32) for n in (5, 5, 4, 5, 5)],
    )(newton_rhs, cond, diag, after, right, left, east)
    edge = ahead(edge, "gx")
    rows = everyones(rows, "gy")
    (rows,) = call(relay_kernel, [(lax.axis_size("gx"), Y)])(rows)
    rows, kinds = lax.optimization_barrier((rows, soil_class))
    water, head = call(unit_kernel, [tall] * 2, [pltpu.VMEM((2 * PAD, Y), F32)])(
        kinds, land_mask, soil_inverse
    )
    rows = everyones(rows, "gx")
    return call(final_kernel, [block, plane, (STATE, X, Y)])(
        rows, newton_rhs, v1, v2, edge, base, water, head, left, east, south,
        ponding, land_mask,
    )


def solution(mesh):
    cells, plane, rest = P(None, "gx", "gy"), P("gx", "gy"), P()
    return jax.shard_map(
        on_device,
        mesh=mesh,
        in_specs=(
            cells, cells, cells, rest, rest, rest, plane, plane, plane, rest, plane,
            plane, rest, cells,
        ),
        out_specs=(cells, plane, cells),
        check_vma=False,
    )
```

```python
import jax
import jax.numpy as jnp
from jax import lax
from jax.experimental import pallas as pl
from jax.experimental.pallas import tpu as pltpu
from jax.sharding import PartitionSpec as P


LAYERS = 5
STATE = 20
CLASSES = 12
W = 3
X, Y = 32, 128
E = X + 8
FIELDS = 3 * LAYERS
G = 2 * W
PAD = 24
F32 = jnp.float32


def two_sum(a, b):
    s = a + b
    t = s - a
    return s, (a - (s - t)) + (b - t)


def renorm(a, b):
    s = a + b
    return s, b - (s - a)


def halves(a):
    t = a * 4097.0
    hi = t - (t - a)
    return hi, a - hi


def two_prod(a, b):
    p = a * b
    (ah, al), (bh, bl) = halves(a), halves(b)
    return p, ((ah * bh - p) + ah * bl + al * bh) + al * bl


def pair_add(a, b):
    s, e = two_sum(a[0], b[0])
    return renorm(s, e + (a[1] + b[1]))


def pair_sub(a, b):
    return pair_add(a, (-b[0], -b[1]))


def pair_mul(a, b):
    p, e = two_prod(a[0], b[0])
    return renorm(p, e + (a[0] * b[1] + a[1] * b[0]))


def pair_div(a, b):
    q = a[0] / b[0]
    r = pair_sub(a, pair_mul((q, jnp.zeros_like(q)), b))
    q2 = r[0] / b[0]
    r = pair_sub(r, pair_mul((q2, jnp.zeros_like(q)), b))
    return pair_add(renorm(q, q2), (r[0] / b[0], jnp.zeros_like(q)))


def iota(shape, dim):
    return lax.broadcasted_iota(jnp.int32, shape, dim)


def pick(table, index):
    row = jnp.broadcast_to(table, index.shape)
    return jnp.take_along_axis(row, index, axis=1, mode="promise_in_bounds")


def call(kernel, outs, scratch=(), specs=None, flops=0, nbytes=0):
    extra = {} if specs is None else {"in_specs": specs}
    return pl.pallas_call(
        kernel,
        out_shape=[jax.ShapeDtypeStruct(s, F32) for s in outs],
        scratch_shapes=scratch,
        compiler_params=pltpu.CompilerParams(vmem_limit_bytes=32 * 2**20),
        cost_estimate=pl.CostEstimate(
            flops=flops, bytes_accessed=nbytes, transcendentals=0
        ),
        **extra,
    )


def gather_table(ref, count):
    lane = iota((1, Y), 1)
    row = jnp.full((1, Y), 1.0, F32)
    for i in range(count):
        row = jnp.where(lane == i, ref[i], row)
    return row


def local_kernel(*refs):
    (cond, diag, slab, east, south, state), held, sem = refs[12:18], refs[18:29], refs[29]
    copies = [
        pltpu.make_async_copy(refs[i], (*held, state)[i], sem.at[i]) for i in range(12)
    ]
    for copy in copies:
        copy.start()
    for copy in copies[:11]:
        copy.wait()
    (pressure, rhs, geology, ks, alpha, expo, land, ponding, slope_class, slope, flow) = held
    t_ks = gather_table(ks, 16)
    t_la = jnp.log(gather_table(alpha, 16))
    t_n = gather_table(expo, 16)
    t_m = 1.0 - 1.0 / t_n
    t_slope = jnp.sqrt(gather_table(slope, 8)) / 0.03
    sea = 4.0 * (1.0 - land[...].astype(F32))
    for l in range(LAYERS):
        g = geology[l]
        p = jnp.abs(pressure[l])
        n = pick(t_n, g)
        m = pick(t_m, g)
        t = jnp.exp(n * (pick(t_la, g) + jnp.log(p)))
        one_t = 1.0 + t
        e = jnp.exp(-m * jnp.log(one_t))
        k = pick(t_ks, g) * e
        d = 0.05 + 0.4 * m * n * t * e / (p * one_t) + sea
        cond[l] = k
        diag[l] = d
        for f, x in enumerate((rhs[l], k, d)):
            slab[f * LAYERS + l] = x[0 : E - X]
    out = pick(t_slope, slope_class[...]) * jnp.exp((5.0 / 3.0) * jnp.log(ponding[...]))
    eastward = jnp.where(flow[...] == 0, out, 0.0)
    east[...] = eastward
    south[...] = out - eastward
    copies[11].wait()


def pack_kernel(rhs, cond, diag, after, packed):
    for lo, rows in ((0, X), (X, E - X)):
        lane = iota((rows, Y), 1)
        total = jnp.zeros((rows, Y), F32)
        for f, ref in enumerate((rhs, cond, diag)):
            for l in range(LAYERS):
                q = f * LAYERS + l
                x = pltpu.roll(after[q] if lo else ref[l], (G * q) % Y, 1)
                total = jnp.where((lane >= G * q) & (lane < G * q + G), x, total)
        packed[lo : lo + rows, :] = total


def krylov_kernel(
    rhs, cond, diag, after, right, east, south, v1_out, v2_out, row_out, back_out,
    strip_out, fr, fc, fv, dd, v,
):
    lane, row_of = iota((E, Y), 1), iota((E, Y), 0)
    first, last = lane == 0, lane == Y - 1
    x, y = lax.axis_index("gx"), lax.axis_index("gy")
    x_end, y_end = x == lax.axis_size("gx") - 1, y == lax.axis_size("gy") - 1
    closed_rows = (row_of == 0) | (row_of == jnp.where(x_end, X, 0))
    closed_lanes = (
        lane == 0,
        lane == jnp.where(y_end, 0, -1),
    )

    def turn(m, h, by, edge):
        m, h = pltpu.roll(m, by, 1), pltpu.roll(h, by, 1)
        return jnp.where(edge, h, m), jnp.where(edge, m, h)

    w = right[...]

    def both(ref, f, l):
        q = f * LAYERS + l
        return (
            jnp.concatenate([ref[l], after[q]], axis=0),
            pltpu.roll(w, (-G * q) % Y, 1),
        )

    def harmonic(a, b):
        return 2.0 * a * b / jnp.maximum(a + b, 1e-30)

    above = None
    for l in range(LAYERS):
        v[0, l], v[1, l] = both(rhs, 0, l)
        k = both(cond, 1, l)
        dd[0, l], dd[1, l] = both(diag, 2, l)
        west = turn(*k, 1, first)
        for s in range(2):
            fr[s, l] = jnp.where(
                closed_rows, 0.0, harmonic(k[s], pltpu.roll(k[s], 1, 0))
            )
            fc[s, l] = harmonic(k[s], west[s])
            if l:
                fv[s, l - 1] = harmonic(k[s], above[s])
        above = k

    def product(l, flux_above):
        vm, vh = v[0, l], v[1, l]
        west = turn(vm, vh, 1, first)
        side = [
            jnp.where(closed_lanes[s], 0.0, fc[s, l] * (x - west[s]))
            for s, x in enumerate((vm, vh))
        ]
        gone = turn(*side, Y - 1, last)
        outs, flux = [], []
        for s, x in enumerate((vm, vh)):
            rows = fr[s, l] * (x - pltpu.roll(x, 1, 0))
            r = dd[s, l] * x + (rows - pltpu.roll(rows, E - 1, 0)) + (side[s] - gone[s])
            if l:
                r = r - flux_above[s]
            if l < LAYERS - 1:
                fl = fv[s, l] * (x - v[s, l + 1])
                r = r + fl
                flux.append(fl)
            outs.append(r)
        return outs, flux

    zero = jnp.zeros((8, Y), F32)
    sums = [(zero, zero)] * 6
    sub = iota((8, Y), 0)
    start, stop = jnp.where(x == 0, 0, W), jnp.where(x_end, 0, W)

    def add_to(j, a, b):
        p, e = two_prod(a, b)
        s, e2 = two_sum(sums[j][0], p)
        sums[j] = s, sums[j][1] + (e + e2)

    def count(step, old, new):
        for i in range(0, E, 8):
            a, b = old[i : i + 8], new[i : i + 8]
            if i == 0 or i == X:
                keep = sub >= start if i == 0 else sub < stop
                a, b = jnp.where(keep, a, 0.0), jnp.where(keep, b, 0.0)
            add_to(2 * step, a, a)
            add_to(2 * step + 1, a, b)

    def counted(m, h):
        return jnp.where(lane >= W, m, jnp.where(y_end, 0.0, h))

    strip = jnp.zeros((E, Y), F32)
    for step in range(3):
        results, flux = [], None
        head = [jnp.zeros((E, Y), F32)] * 2
        for l in range(LAYERS):
            outs, flux = product(l, flux)
            old, new = (v[0, l], v[1, l]), outs
            count(step, counted(*old), counted(*new))
            here = (lane >= W * l) & (lane < W * l + W) & (y == 0)
            head = [
                jnp.where(here, pltpu.roll(t[0], W * l, 1), h)
                for t, h in zip((old, new), head)
            ]
            results.append(outs)
        count(step, *head)
        if step < 2:
            for l in range(LAYERS):
                m, h = results[l]
                v[0, l], v[1, l] = m, h
                (v1_out, v2_out)[step][l] = m[0:X]
                q, n = (LAYERS + 2 * l, 2) if step else (l, 1)
                back_out[q : q + n, :] = m[X : X + n]
                strip = jnp.where(
                    (lane >= q) & (lane < q + n), pltpu.roll(h, q, 1), strip
                )
    back_out[3 * LAYERS : 3 * LAYERS + 1, :] = east[X - 1 : X, :]
    back_out[16:24, :] = strip[X:E]
    strip_out[...] = jnp.where(lane[0:X] == Y - 1, south[...], strip[0:X])

    ln = iota((8, Y), 1)
    total = zero, zero
    for j in range(6):
        s = fold(sums[j], (4, 2, 1), 0)
        total = tuple(jnp.where(sub == j, a, b) for a, b in zip(s, total))
    total = renorm(*fold(total, (64, 32, 16, 8, 4, 2, 1), 1))
    row = jnp.where(ln == sub, total[0], jnp.where(ln == sub + 8, total[1], 0.0))
    row = jnp.sum(row, axis=0, keepdims=True)
    row_out[...] = jnp.broadcast_to(row, row_out.shape)


def fold(s, steps, dim):
    for by in steps:
        hi, e = two_sum(s[0], pltpu.roll(s[0], by, dim))
        s = hi, s[1] + pltpu.roll(s[1], by, dim) + e
    return s


def rows_total(ref):
    parts = [
        (ref[i : i + 8, :], pltpu.roll(ref[i : i + 8, :], Y - 8, 1))
        for i in range(0, ref.shape[0], 8)
    ]
    while len(parts) > 1:
        parts = [pair_add(a, b) for a, b in zip(parts[::2], parts[1::2])]
    return renorm(*fold(parts[0], (4, 2, 1), 0))


def relay_kernel(rows, edge, strip, row_out, west_out):
    row, lane = iota((X, Y), 0), iota((X, Y), 1)
    given = jnp.where(lax.axis_index("gx") == 0, 0, 3 * LAYERS)
    west = jnp.where((row == 0) & (lane < given), edge[16:17, :], strip[...])
    west_out[...] = jnp.where(
        (row == 1) & (lane >= LAYERS) & (lane < given), edge[17:18, :], west
    )
    hi, lo = rows_total(rows)
    ln = iota((8, Y), 1)
    both = jnp.where(ln < 8, hi, pltpu.roll(lo, 8, 1))
    for i in range(0, row_out.shape[0], 8):
        row_out[i : i + 8, :] = both


def soil_kernel(state, soil_class, land, inverse, base, w):
    w[...] = jnp.zeros(w.shape, F32)
    for e in range(CLASSES):
        x = inverse[e]
        w[0:STATE, 16 * e : 16 * e + 16] = x[:, 0:16]
        w[0:STATE, 192 + 4 * e : 196 + 4 * e] = x[:, 16:STATE]
    w_all = w[...]
    half = (iota((8, Y), 0) >= 4).astype(jnp.int32)
    for x0 in range(0, X, 4):
        fields, spread, kinds = [], [], []
        for x in range(x0, x0 + 4):
            f = state[pl.ds(x, STATE, stride=X), :]
            kind = jnp.where(land[x : x + 1, :] == 1, soil_class[x : x + 1, :], -1)
            twice = jnp.concatenate([f[16:STATE], f[16:STATE]], axis=0)
            parts = [jnp.where(kind == e, f[0:16], 0.0) for e in range(CLASSES)]
            for e in range(0, CLASSES, 2):
                parts.append(jnp.where(kind == e + half, twice, 0.0))
            spread.append(jnp.concatenate(parts, axis=0))
            fields.append(f)
            kinds.append(kind)
        solved = jnp.dot(
            w_all,
            jnp.concatenate(spread, axis=1),
            precision=lax.Precision.HIGHEST,
            preferred_element_type=F32,
        )
        for n in range(4):
            base[pl.ds(x0 + n, STATE, stride=X), :] = jnp.where(
                kinds[n] >= 0, solved[0:STATE, n * Y : n * Y + Y], fields[n]
            )


def unit_kernel(soil_class, land, inverse, water, head, table):
    for e in range(CLASSES):
        x = inverse[e]
        table[0:STATE, e : e + 1] = x[:, 0:1]
        table[PAD : PAD + STATE, e : e + 1] = x[:, 1:2]
    index = soil_class[...]
    half = 0.5 * land[...].astype(F32)
    for i in range(STATE):
        here = slice(i * X, i * X + X)
        water[here, :] = half * pick(table[i : i + 1, :], index)
        head[here, :] = half * pick(table[PAD + i : PAD + i + 1, :], index)


def final_kernel(
    rows, rhs, v1, v2, back, base, water, head, strip, east, south, ponding, land,
    corr_out, pond_out, soil_out,
):
    hi, lo = rows_total(rows)
    mu = [
        tuple(jnp.broadcast_to(t[:, j : j + 1], (8, Y)) for t in (hi, lo))
        for j in range(6)
    ]
    l21 = pair_div(mu[2], mu[1])
    l31 = pair_div(mu[3], mu[1])
    d2 = pair_sub(mu[3], pair_mul(l21, mu[2]))
    u = pair_sub(mu[4], pair_mul(l31, mu[2]))
    l32 = pair_div(u, d2)
    d3 = pair_sub(pair_sub(mu[5], pair_mul(l31, mu[3])), pair_mul(l32, u))
    y2 = pair_sub(mu[1], pair_mul(l21, mu[0]))
    y3 = pair_sub(pair_sub(mu[2], pair_mul(l31, mu[0])), pair_mul(l32, y2))
    c3 = pair_div(y3, d3)
    c2 = pair_sub(pair_div(y2, d2), pair_mul(l32, c3))
    c1 = pair_sub(
        pair_sub(pair_div(mu[0], mu[1]), pair_mul(l21, c2)), pair_mul(l31, c3)
    )
    c1, c2, c3 = (jnp.concatenate([c[0]] * (X // 8), axis=0) for c in (c1, c2, c3))

    row, lane = iota((X, Y), 0), iota((X, Y), 1)
    es, so = east[...], south[...]
    side = strip[...]
    given = jnp.where(lax.axis_index("gx") == 0, 0, 1)
    west = jnp.where(given == 0, 0.0, back[3 * LAYERS : 3 * LAYERS + 1, :])
    north = jnp.where(lax.axis_index("gy") == 0, 0.0, pltpu.roll(side, 1, 1))
    inflow = jnp.where(row == 0, west, pltpu.roll(es, 1, 0)) + jnp.where(
        lane == 0, north, pltpu.roll(so, 1, 1)
    )
    pond = land[...].astype(F32) * (ponding[...] + 0.2 * (inflow - (es + so)))
    pond_out[...] = pond

    lanes = jnp.where(lax.axis_index("gy") == 0, 0, 1)
    top = None
    for l in range(LAYERS):
        q = LAYERS + 2 * l
        a1 = jnp.where(row < given, back[l : l + 1, :], v1[l])
        a2 = jnp.where(row < given, back[q : q + 1, :], v2[l])
        a2 = jnp.where((row == 1) & (given > 0), back[q + 1 : q + 2, :], a2)
        a1 = jnp.where(lane < lanes, pltpu.roll(side, (-l) % Y, 1), a1)
        a2 = jnp.where(lane < 2 * lanes, pltpu.roll(side, (-q) % Y, 1), a2)
        x = c1 * rhs[l] + c2 * a1 + c3 * a2
        corr_out[l] = x
        top = x if top is None else top
    for i in range(STATE):
        here = slice(i * X, i * X + X)
        soil_out[i] = base[here, :] + water[here, :] * pond + head[here, :] * top


def ahead(x, axis):
    n = lax.axis_size(axis)
    return lax.ppermute(x, axis, [(i, (i + 1) % n) for i in range(n)])


def back(x, axis):
    n = lax.axis_size(axis)
    return lax.ppermute(x, axis, [((i + 1) % n, i) for i in range(n)])


def everyones(rows, axis):
    count = lax.axis_size(axis)
    return lax.all_to_all(rows.reshape(count, 1, Y), axis, 0, 0).reshape(count, Y)


def on_device(
    pressure, newton_rhs, geology, saturated_conductivity, genuchten_alpha,
    genuchten_exponent, land_mask, ponding, slope_class, slope_table,
    flow_direction, soil_class, soil_inverse, soil_state,
):
    block, plane, tall = (LAYERS, X, Y), (X, Y), (STATE * X, Y)
    local = (
        pressure, newton_rhs, geology, saturated_conductivity, genuchten_alpha,
        genuchten_exponent, land_mask, ponding, slope_class, slope_table,
        flow_direction, soil_state.reshape(tall),
    )
    cond, diag, slab, east, south, state = call(
        local_kernel,
        [block, block, (FIELDS, E - X, Y), plane, plane, tall],
        [
            (pltpu.SMEM if a.ndim == 1 else pltpu.VMEM)(a.shape, a.dtype)
            for a in local[:-1]
        ]
        + [pltpu.SemaphoreType.DMA((len(local),))],
        [pl.BlockSpec(memory_space=pltpu.HBM)] * len(local),
    )(*(pltpu.with_memory_space_constraint(a, pltpu.HBM) for a in local))
    after = back(slab, "gx")
    (base,) = call(
        soil_kernel, [tall], [pltpu.VMEM((PAD, 240), F32)], flops=20_000_000
    )(state, soil_class, land_mask, soil_inverse)
    after, base = lax.optimization_barrier((after, base))
    (packed,) = call(pack_kernel, [(E, Y)])(newton_rhs, cond, diag, after)
    right = back(packed, "gy")
    v1, v2, rows, edge, strip = call(
        krylov_kernel,
        [block, block, (lax.axis_size("gy"), Y), (24, Y), plane],
        [pltpu.VMEM((2, n, E, Y), F32) for n in (5, 5, 4, 5, 5)],
    )(newton_rhs, cond, diag, after, right, east, south)
    edge = ahead(edge, "gx")
    rows = everyones(rows, "gy")
    water, head = call(unit_kernel, [tall] * 2, [pltpu.VMEM((2 * PAD, Y), F32)])(
        soil_class, land_mask, soil_inverse
    )
    rows, edge, water, head = lax.optimization_barrier((rows, edge, water, head))
    rows, strip = call(relay_kernel, [(lax.axis_size("gx"), Y), plane])(
        rows, edge, strip
    )
    strip = ahead(strip, "gy")
    rows = everyones(rows, "gx")
    return call(final_kernel, [block, plane, (STATE, X, Y)])(
        rows, newton_rhs, v1, v2, edge, base, water, head, strip, east, south,
        ponding, land_mask,
    )


def solution(mesh):
    cells, plane, rest = P(None, "gx", "gy"), P("gx", "gy"), P()
    return jax.shard_map(
        on_device,
        mesh=mesh,
        in_specs=(
            cells, cells, cells, rest, rest, rest, plane, plane, plane, rest, plane,
            plane, rest, cells,
        ),
        out_specs=(cells, plane, cells),
        check_vma=False,
    )
```

```python
import jax
import jax.numpy as jnp
from jax import lax
from jax.experimental import pallas as pl
from jax.experimental.pallas import tpu as pltpu
from jax.sharding import PartitionSpec as P


LAYERS = 5
STATE = 20
CLASSES = 12
W = 3
X, Y = 32, 128
E = X + 8
FIELDS = 3 * LAYERS
G = 2 * W
PAD = 24
F32 = jnp.float32


def two_sum(a, b):
    s = a + b
    t = s - a
    return s, (a - (s - t)) + (b - t)


def renorm(a, b):
    s = a + b
    return s, b - (s - a)


def halves(a):
    t = a * 4097.0
    hi = t - (t - a)
    return hi, a - hi


def two_prod(a, b):
    p = a * b
    (ah, al), (bh, bl) = halves(a), halves(b)
    return p, ((ah * bh - p) + ah * bl + al * bh) + al * bl


def pair_add(a, b):
    s, e = two_sum(a[0], b[0])
    return renorm(s, e + (a[1] + b[1]))


def pair_sub(a, b):
    return pair_add(a, (-b[0], -b[1]))


def pair_mul(a, b):
    p, e = two_prod(a[0], b[0])
    return renorm(p, e + (a[0] * b[1] + a[1] * b[0]))


def pair_div(a, b):
    q = a[0] / b[0]
    r = pair_sub(a, pair_mul((q, jnp.zeros_like(q)), b))
    return renorm(q, r[0] / b[0])


def iota(shape, dim):
    return lax.broadcasted_iota(jnp.int32, shape, dim)


def pick(table, index):
    row = jnp.broadcast_to(table, index.shape)
    return jnp.take_along_axis(row, index, axis=1, mode="promise_in_bounds")


def call(kernel, outs, scratch=(), specs=None, flops=0, nbytes=0):
    extra = {} if specs is None else {"in_specs": specs}
    return pl.pallas_call(
        kernel,
        out_shape=[jax.ShapeDtypeStruct(s, F32) for s in outs],
        scratch_shapes=scratch,
        compiler_params=pltpu.CompilerParams(vmem_limit_bytes=32 * 2**20),
        cost_estimate=pl.CostEstimate(
            flops=flops, bytes_accessed=nbytes, transcendentals=0
        ),
        **extra,
    )


def gather_table(ref, count):
    lane = iota((1, Y), 1)
    row = jnp.full((1, Y), 1.0, F32)
    for i in range(count):
        row = jnp.where(lane == i, ref[i], row)
    return row


def local_kernel(*refs):
    (cond, diag, slab, east, south, state), held, sem = refs[12:18], refs[18:29], refs[29]
    copies = [
        pltpu.make_async_copy(refs[i], (*held, state)[i], sem.at[i]) for i in range(12)
    ]
    for copy in copies:
        copy.start()
    for copy in copies[:11]:
        copy.wait()
    (pressure, rhs, geology, ks, alpha, expo, land, ponding, slope_class, slope, flow) = held
    t_ks = gather_table(ks, 16)
    t_la = jnp.log(gather_table(alpha, 16))
    t_n = gather_table(expo, 16)
    t_m = 1.0 - 1.0 / t_n
    t_slope = jnp.sqrt(gather_table(slope, 8)) / 0.03
    sea = 4.0 * (1.0 - land[...].astype(F32))
    for l in range(LAYERS):
        g = geology[l]
        p = jnp.abs(pressure[l])
        n = pick(t_n, g)
        m = pick(t_m, g)
        t = jnp.exp(n * (pick(t_la, g) + jnp.log(p)))
        one_t = 1.0 + t
        e = jnp.exp(-m * jnp.log(one_t))
        k = pick(t_ks, g) * e
        d = 0.05 + 0.4 * m * n * t * e / (p * one_t) + sea
        cond[l] = k
        diag[l] = d
        for f, x in enumerate((rhs[l], k, d)):
            slab[f * LAYERS + l] = x[0 : E - X]
    out = pick(t_slope, slope_class[...]) * jnp.exp((5.0 / 3.0) * jnp.log(ponding[...]))
    eastward = jnp.where(flow[...] == 0, out, 0.0)
    east[...] = eastward
    south[...] = out - eastward
    copies[11].wait()


def pack_kernel(rhs, cond, diag, after, packed):
    for lo, rows in ((0, X), (X, E - X)):
        lane = iota((rows, Y), 1)
        total = jnp.zeros((rows, Y), F32)
        for f, ref in enumerate((rhs, cond, diag)):
            for l in range(LAYERS):
                q = f * LAYERS + l
                x = pltpu.roll(after[q] if lo else ref[l], (G * q) % Y, 1)
                total = jnp.where((lane >= G * q) & (lane < G * q + G), x, total)
        packed[lo : lo + rows, :] = total


def krylov_kernel(
    rhs, cond, diag, after, right, east, south, v1_out, v2_out, row_out, back_out,
    strip_out, fr, fc, fv, dd, v,
):
    lane, row_of = iota((E, Y), 1), iota((E, Y), 0)
    first, last = lane == 0, lane == Y - 1
    x, y = lax.axis_index("gx"), lax.axis_index("gy")
    x_end, y_end = x == lax.axis_size("gx") - 1, y == lax.axis_size("gy") - 1
    closed_rows = (row_of == 0) | (row_of == jnp.where(x_end, X, 0))
    closed_lanes = (
        lane == 0,
        lane == jnp.where(y_end, 0, -1),
    )

    def turn(m, h, by, edge):
        m, h = pltpu.roll(m, by, 1), pltpu.roll(h, by, 1)
        return jnp.where(edge, h, m), jnp.where(edge, m, h)

    w = right[...]

    def both(ref, f, l):
        q = f * LAYERS + l
        return (
            jnp.concatenate([ref[l], after[q]], axis=0),
            pltpu.roll(w, (-G * q) % Y, 1),
        )

    def harmonic(a, b):
        return 2.0 * a * b / jnp.maximum(a + b, 1e-30)

    above = None
    for l in range(LAYERS):
        v[0, l], v[1, l] = both(rhs, 0, l)
        k = both(cond, 1, l)
        dd[0, l], dd[1, l] = both(diag, 2, l)
        west = turn(*k, 1, first)
        for s in range(2):
            fr[s, l] = jnp.where(
                closed_rows, 0.0, harmonic(k[s], pltpu.roll(k[s], 1, 0))
            )
            fc[s, l] = harmonic(k[s], west[s])
            if l:
                fv[s, l - 1] = harmonic(k[s], above[s])
        above = k

    def product(l, flux_above):
        vm, vh = v[0, l], v[1, l]
        west = turn(vm, vh, 1, first)
        side = [
            jnp.where(closed_lanes[s], 0.0, fc[s, l] * (x - west[s]))
            for s, x in enumerate((vm, vh))
        ]
        gone = turn(*side, Y - 1, last)
        outs, flux = [], []
        for s, x in enumerate((vm, vh)):
            rows = fr[s, l] * (x - pltpu.roll(x, 1, 0))
            r = dd[s, l] * x + (rows - pltpu.roll(rows, E - 1, 0)) + (side[s] - gone[s])
            if l:
                r = r - flux_above[s]
            if l < LAYERS - 1:
                fl = fv[s, l] * (x - v[s, l + 1])
                r = r + fl
                flux.append(fl)
            outs.append(r)
        return outs, flux

    zero = jnp.zeros((8, Y), F32)
    sums = [(zero, zero)] * 6
    sub = iota((8, Y), 0)
    start, stop = jnp.where(x == 0, 0, W), jnp.where(x_end, 0, W)

    def add_to(j, a, b):
        p, e = two_prod(a, b)
        s, e2 = two_sum(sums[j][0], p)
        sums[j] = s, sums[j][1] + (e + e2)

    def count(step, old, new):
        for i in range(0, E, 8):
            a, b = old[i : i + 8], new[i : i + 8]
            if i == 0 or i == X:
                keep = sub >= start if i == 0 else sub < stop
                a, b = jnp.where(keep, a, 0.0), jnp.where(keep, b, 0.0)
            add_to(2 * step, a, a)
            add_to(2 * step + 1, a, b)

    def counted(m, h):
        return jnp.where(lane >= W, m, jnp.where(y_end, 0.0, h))

    strip = jnp.zeros((E, Y), F32)
    for step in range(3):
        results, flux = [], None
        head = [jnp.zeros((E, Y), F32)] * 2
        for l in range(LAYERS):
            outs, flux = product(l, flux)
            old, new = (v[0, l], v[1, l]), outs
            count(step, counted(*old), counted(*new))
            here = (lane >= W * l) & (lane < W * l + W) & (y == 0)
            head = [
                jnp.where(here, pltpu.roll(t[0], W * l, 1), h)
                for t, h in zip((old, new), head)
            ]
            results.append(outs)
        count(step, *head)
        if step < 2:
            for l in range(LAYERS):
                m, h = results[l]
                v[0, l], v[1, l] = m, h
                (v1_out, v2_out)[step][l] = m[0:X]
                q, n = (LAYERS + 2 * l, 2) if step else (l, 1)
                back_out[q : q + n, :] = m[X : X + n]
                strip = jnp.where(
                    (lane >= q) & (lane < q + n), pltpu.roll(h, q, 1), strip
                )
    back_out[3 * LAYERS : 3 * LAYERS + 1, :] = east[X - 1 : X, :]
    back_out[16:24, :] = strip[X:E]
    strip_out[...] = jnp.where(lane[0:X] == Y - 1, south[...], strip[0:X])

    ln = iota((8, Y), 1)
    total = zero, zero
    for j in range(6):
        s = fold(sums[j], (4, 2, 1), 0)
        total = tuple(jnp.where(sub == j, a, b) for a, b in zip(s, total))
    total = renorm(*fold(total, (64, 32, 16, 8, 4, 2, 1), 1))
    row = jnp.where(ln == sub, total[0], jnp.where(ln == sub + 8, total[1], 0.0))
    row = jnp.sum(row, axis=0, keepdims=True)
    row_out[...] = jnp.broadcast_to(row, row_out.shape)


def fold(s, steps, dim):
    for by in steps:
        hi, e = two_sum(s[0], pltpu.roll(s[0], by, dim))
        s = hi, s[1] + pltpu.roll(s[1], by, dim) + e
    return s


def rows_total(ref):
    parts = [
        (ref[i : i + 8, :], pltpu.roll(ref[i : i + 8, :], Y - 8, 1))
        for i in range(0, ref.shape[0], 8)
    ]
    while len(parts) > 1:
        parts = [pair_add(a, b) for a, b in zip(parts[::2], parts[1::2])]
    return renorm(*fold(parts[0], (4, 2, 1), 0))


def relay_kernel(rows, edge, strip, row_out, west_out):
    row, lane = iota((X, Y), 0), iota((X, Y), 1)
    given = jnp.where(lax.axis_index("gx") == 0, 0, 3 * LAYERS)
    west = jnp.where((row == 0) & (lane < given), edge[16:17, :], strip[...])
    west_out[...] = jnp.where(
        (row == 1) & (lane >= LAYERS) & (lane < given), edge[17:18, :], west
    )
    hi, lo = rows_total(rows)
    ln = iota((8, Y), 1)
    both = jnp.where(ln < 8, hi, pltpu.roll(lo, 8, 1))
    for i in range(0, row_out.shape[0], 8):
        row_out[i : i + 8, :] = both


def soil_kernel(state, soil_class, land, inverse, base, w):
    w[...] = jnp.zeros(w.shape, F32)
    for e in range(CLASSES):
        x = inverse[e]
        w[0:STATE, 16 * e : 16 * e + 16] = x[:, 0:16]
        w[0:STATE, 192 + 4 * e : 196 + 4 * e] = x[:, 16:STATE]
    w_all = w[...]
    half = (iota((8, Y), 0) >= 4).astype(jnp.int32)
    for x0 in range(0, X, 4):
        fields, spread, kinds = [], [], []
        for x in range(x0, x0 + 4):
            f = state[pl.ds(x, STATE, stride=X), :]
            kind = jnp.where(land[x : x + 1, :] == 1, soil_class[x : x + 1, :], -1)
            twice = jnp.concatenate([f[16:STATE], f[16:STATE]], axis=0)
            parts = [jnp.where(kind == e, f[0:16], 0.0) for e in range(CLASSES)]
            for e in range(0, CLASSES, 2):
                parts.append(jnp.where(kind == e + half, twice, 0.0))
            spread.append(jnp.concatenate(parts, axis=0))
            fields.append(f)
            kinds.append(kind)
        solved = jnp.dot(
            w_all,
            jnp.concatenate(spread, axis=1),
            precision=lax.Precision.HIGHEST,
            preferred_element_type=F32,
        )
        for n in range(4):
            base[pl.ds(x0 + n, STATE, stride=X), :] = jnp.where(
                kinds[n] >= 0, solved[0:STATE, n * Y : n * Y + Y], fields[n]
            )


def unit_kernel(soil_class, land, inverse, water, head, table):
    for e in range(CLASSES):
        x = inverse[e]
        table[0:STATE, e : e + 1] = x[:, 0:1]
        table[PAD : PAD + STATE, e : e + 1] = x[:, 1:2]
    index = soil_class[...]
    half = 0.5 * land[...].astype(F32)
    for i in range(STATE):
        here = slice(i * X, i * X + X)
        water[here, :] = half * pick(table[i : i + 1, :], index)
        head[here, :] = half * pick(table[PAD + i : PAD + i + 1, :], index)


def final_kernel(
    rows, rhs, v1, v2, back, base, water, head, strip, east, south, ponding, land,
    corr_out, pond_out, soil_out,
):
    hi, lo = rows_total(rows)
    mu = [
        tuple(jnp.broadcast_to(t[:, j : j + 1], (8, Y)) for t in (hi, lo))
        for j in range(6)
    ]
    l21 = pair_div(mu[2], mu[1])
    l31 = pair_div(mu[3], mu[1])
    d2 = pair_sub(mu[3], pair_mul(l21, mu[2]))
    u = pair_sub(mu[4], pair_mul(l31, mu[2]))
    l32 = pair_div(u, d2)
    d3 = pair_sub(pair_sub(mu[5], pair_mul(l31, mu[3])), pair_mul(l32, u))
    y2 = pair_sub(mu[1], pair_mul(l21, mu[0]))
    y3 = pair_sub(pair_sub(mu[2], pair_mul(l31, mu[0])), pair_mul(l32, y2))
    c3 = pair_div(y3, d3)
    c2 = pair_sub(pair_div(y2, d2), pair_mul(l32, c3))
    c1 = pair_sub(
        pair_sub(pair_div(mu[0], mu[1]), pair_mul(l21, c2)), pair_mul(l31, c3)
    )
    c1, c2, c3 = (jnp.concatenate([c[0]] * (X // 8), axis=0) for c in (c1, c2, c3))

    row, lane = iota((X, Y), 0), iota((X, Y), 1)
    es, so = east[...], south[...]
    side = strip[...]
    given = jnp.where(lax.axis_index("gx") == 0, 0, 1)
    west = jnp.where(given == 0, 0.0, back[3 * LAYERS : 3 * LAYERS + 1, :])
    north = jnp.where(lax.axis_index("gy") == 0, 0.0, pltpu.roll(side, 1, 1))
    inflow = jnp.where(row == 0, west, pltpu.roll(es, 1, 0)) + jnp.where(
        lane == 0, north, pltpu.roll(so, 1, 1)
    )
    pond = land[...].astype(F32) * (ponding[...] + 0.2 * (inflow - (es + so)))
    pond_out[...] = pond

    lanes = jnp.where(lax.axis_index("gy") == 0, 0, 1)
    top = None
    for l in range(LAYERS):
        q = LAYERS + 2 * l
        a1 = jnp.where(row < given, back[l : l + 1, :], v1[l])
        a2 = jnp.where(row < given, back[q : q + 1, :], v2[l])
        a2 = jnp.where((row == 1) & (given > 0), back[q + 1 : q + 2, :], a2)
        a1 = jnp.where(lane < lanes, pltpu.roll(side, (-l) % Y, 1), a1)
        a2 = jnp.where(lane < 2 * lanes, pltpu.roll(side, (-q) % Y, 1), a2)
        x = c1 * rhs[l] + c2 * a1 + c3 * a2
        corr_out[l] = x
        top = x if top is None else top
    for i in range(STATE):
        here = slice(i * X, i * X + X)
        soil_out[i] = base[here, :] + water[here, :] * pond + head[here, :] * top


def ahead(x, axis):
    n = lax.axis_size(axis)
    return lax.ppermute(x, axis, [(i, (i + 1) % n) for i in range(n)])


def back(x, axis):
    n = lax.axis_size(axis)
    return lax.ppermute(x, axis, [((i + 1) % n, i) for i in range(n)])


def everyones(rows, axis):
    count = lax.axis_size(axis)
    return lax.all_to_all(rows.reshape(count, 1, Y), axis, 0, 0).reshape(count, Y)


def on_device(
    pressure, newton_rhs, geology, saturated_conductivity, genuchten_alpha,
    genuchten_exponent, land_mask, ponding, slope_class, slope_table,
    flow_direction, soil_class, soil_inverse, soil_state,
):
    block, plane, tall = (LAYERS, X, Y), (X, Y), (STATE * X, Y)
    local = (
        pressure, newton_rhs, geology, saturated_conductivity, genuchten_alpha,
        genuchten_exponent, land_mask, ponding, slope_class, slope_table,
        flow_direction, soil_state.reshape(tall),
    )
    cond, diag, slab, east, south, state = call(
        local_kernel,
        [block, block, (FIELDS, E - X, Y), plane, plane, tall],
        [
            (pltpu.SMEM if a.ndim == 1 else pltpu.VMEM)(a.shape, a.dtype)
            for a in local[:-1]
        ]
        + [pltpu.SemaphoreType.DMA((len(local),))],
        [pl.BlockSpec(memory_space=pltpu.HBM)] * len(local),
    )(*(pltpu.with_memory_space_constraint(a, pltpu.HBM) for a in local))
    after = back(slab, "gx")
    (packed,) = call(pack_kernel, [(E, Y)])(newton_rhs, cond, diag, after)
    right = back(packed, "gy")
    water, head = call(unit_kernel, [tall] * 2, [pltpu.VMEM((2 * PAD, Y), F32)])(
        soil_class, land_mask, soil_inverse
    )
    right, water, head = lax.optimization_barrier((right, water, head))
    v1, v2, rows, edge, strip = call(
        krylov_kernel,
        [block, block, (lax.axis_size("gy"), Y), (24, Y), plane],
        [pltpu.VMEM((2, n, E, Y), F32) for n in (5, 5, 4, 5, 5)],
    )(newton_rhs, cond, diag, after, right, east, south)
    edge = ahead(edge, "gx")
    rows = everyones(rows, "gy")
    rows, strip = call(relay_kernel, [(lax.axis_size("gx"), Y), plane])(
        rows, edge, strip
    )
    strip = ahead(strip, "gy")
    rows, kinds = lax.optimization_barrier((rows, soil_class))
    (base,) = call(
        soil_kernel, [tall], [pltpu.VMEM((PAD, 240), F32)], flops=20_000_000
    )(state, kinds, land_mask, soil_inverse)
    rows = everyones(rows, "gx")
    return call(final_kernel, [block, plane, (STATE, X, Y)])(
        rows, newton_rhs, v1, v2, edge, base, water, head, strip, east, south,
        ponding, land_mask,
    )


def solution(mesh):
    cells, plane, rest = P(None, "gx", "gy"), P("gx", "gy"), P()
    return jax.shard_map(
        on_device,
        mesh=mesh,
        in_specs=(
            cells, cells, cells, rest, rest, rest, plane, plane, plane, rest, plane,
            plane, rest, cells,
        ),
        out_specs=(cells, plane, cells),
        check_vma=False,
    )
```

```python
import jax
import jax.numpy as jnp
from jax import lax
from jax.experimental import pallas as pl
from jax.experimental.pallas import tpu as pltpu
from jax.sharding import PartitionSpec as P


LAYERS = 5
STATE = 20
CLASSES = 12
W = 3
X, Y = 32, 128
E = X + 8
FIELDS = 3 * LAYERS
G = 2 * W
PAD = 24
F32 = jnp.float32


def two_sum(a, b):
    s = a + b
    t = s - a
    return s, (a - (s - t)) + (b - t)


def renorm(a, b):
    s = a + b
    return s, b - (s - a)


def halves(a):
    t = a * 4097.0
    hi = t - (t - a)
    return hi, a - hi


def two_prod(a, b):
    p = a * b
    (ah, al), (bh, bl) = halves(a), halves(b)
    return p, ((ah * bh - p) + ah * bl + al * bh) + al * bl


def pair_add(a, b):
    s, e = two_sum(a[0], b[0])
    return renorm(s, e + (a[1] + b[1]))


def pair_sub(a, b):
    return pair_add(a, (-b[0], -b[1]))


def pair_mul(a, b):
    p, e = two_prod(a[0], b[0])
    return renorm(p, e + (a[0] * b[1] + a[1] * b[0]))


def pair_div(a, b):
    q = a[0] / b[0]
    r = pair_sub(a, pair_mul((q, jnp.zeros_like(q)), b))
    return renorm(q, r[0] / b[0])


def iota(shape, dim):
    return lax.broadcasted_iota(jnp.int32, shape, dim)


def pick(table, index):
    row = jnp.broadcast_to(table, index.shape)
    return jnp.take_along_axis(row, index, axis=1, mode="promise_in_bounds")


def call(kernel, outs, scratch=(), specs=None, flops=0, nbytes=0):
    extra = {} if specs is None else {"in_specs": specs}
    return pl.pallas_call(
        kernel,
        out_shape=[jax.ShapeDtypeStruct(s, F32) for s in outs],
        scratch_shapes=scratch,
        compiler_params=pltpu.CompilerParams(vmem_limit_bytes=32 * 2**20),
        cost_estimate=pl.CostEstimate(
            flops=flops, bytes_accessed=nbytes, transcendentals=0
        ),
        **extra,
    )


def gather_table(ref, count):
    lane = iota((1, Y), 1)
    row = jnp.full((1, Y), 1.0, F32)
    for i in range(count):
        row = jnp.where(lane == i, ref[i], row)
    return row


def local_kernel(*refs):
    (cond, diag, slab, east, south, state), held, sem = refs[12:18], refs[18:29], refs[29]
    copies = [
        pltpu.make_async_copy(refs[i], (*held, state)[i], sem.at[i]) for i in range(12)
    ]
    for copy in copies:
        copy.start()
    for copy in copies[:11]:
        copy.wait()
    (pressure, rhs, geology, ks, alpha, expo, land, ponding, slope_class, slope, flow) = held
    t_ks = gather_table(ks, 16)
    t_la = jnp.log(gather_table(alpha, 16))
    t_n = gather_table(expo, 16)
    t_m = 1.0 - 1.0 / t_n
    t_slope = jnp.sqrt(gather_table(slope, 8)) / 0.03
    sea = 4.0 * (1.0 - land[...].astype(F32))
    for l in range(LAYERS):
        g = geology[l]
        p = jnp.abs(pressure[l])
        n = pick(t_n, g)
        m = pick(t_m, g)
        t = jnp.exp(n * (pick(t_la, g) + jnp.log(p)))
        one_t = 1.0 + t
        e = jnp.exp(-m * jnp.log(one_t))
        k = pick(t_ks, g) * e
        d = 0.05 + 0.4 * m * n * t * e / (p * one_t) + sea
        cond[l] = k
        diag[l] = d
        for f, x in enumerate((rhs[l], k, d)):
            slab[f * LAYERS + l] = x[0 : E - X]
    out = pick(t_slope, slope_class[...]) * jnp.exp((5.0 / 3.0) * jnp.log(ponding[...]))
    eastward = jnp.where(flow[...] == 0, out, 0.0)
    east[...] = eastward
    south[...] = out - eastward
    copies[11].wait()


def pack_kernel(rhs, cond, diag, after, packed):
    for lo, rows in ((0, X), (X, E - X)):
        lane = iota((rows, Y), 1)
        total = jnp.zeros((rows, Y), F32)
        for f, ref in enumerate((rhs, cond, diag)):
            for l in range(LAYERS):
                q = f * LAYERS + l
                x = pltpu.roll(after[q] if lo else ref[l], (G * q) % Y, 1)
                total = jnp.where((lane >= G * q) & (lane < G * q + G), x, total)
        packed[lo : lo + rows, :] = total


def krylov_kernel(
    rhs, cond, diag, after, right, east, south, v1_out, v2_out, row_out, back_out,
    strip_out, fr, fc, fv, dd, v,
):
    lane, row_of = iota((E, Y), 1), iota((E, Y), 0)
    first, last = lane == 0, lane == Y - 1
    x, y = lax.axis_index("gx"), lax.axis_index("gy")
    x_end, y_end = x == lax.axis_size("gx") - 1, y == lax.axis_size("gy") - 1
    closed_rows = (row_of == 0) | (row_of == jnp.where(x_end, X, 0))
    closed_lanes = (
        lane == 0,
        lane == jnp.where(y_end, 0, -1),
    )

    def turn(m, h, by, edge):
        m, h = pltpu.roll(m, by, 1), pltpu.roll(h, by, 1)
        return jnp.where(edge, h, m), jnp.where(edge, m, h)

    w = right[...]

    def both(ref, f, l):
        q = f * LAYERS + l
        return (
            jnp.concatenate([ref[l], after[q]], axis=0),
            pltpu.roll(w, (-G * q) % Y, 1),
        )

    def harmonic(a, b):
        return 2.0 * a * b / jnp.maximum(a + b, 1e-30)

    above = None
    for l in range(LAYERS):
        v[0, l], v[1, l] = both(rhs, 0, l)
        k = both(cond, 1, l)
        dd[0, l], dd[1, l] = both(diag, 2, l)
        west = turn(*k, 1, first)
        for s in range(2):
            fr[s, l] = jnp.where(
                closed_rows, 0.0, harmonic(k[s], pltpu.roll(k[s], 1, 0))
            )
            fc[s, l] = harmonic(k[s], west[s])
            if l:
                fv[s, l - 1] = harmonic(k[s], above[s])
        above = k

    def product(l, flux_above):
        vm, vh = v[0, l], v[1, l]
        west = turn(vm, vh, 1, first)
        side = [
            jnp.where(closed_lanes[s], 0.0, fc[s, l] * (x - west[s]))
            for s, x in enumerate((vm, vh))
        ]
        gone = turn(*side, Y - 1, last)
        outs, flux = [], []
        for s, x in enumerate((vm, vh)):
            rows = fr[s, l] * (x - pltpu.roll(x, 1, 0))
            r = dd[s, l] * x + (rows - pltpu.roll(rows, E - 1, 0)) + (side[s] - gone[s])
            if l:
                r = r - flux_above[s]
            if l < LAYERS - 1:
                fl = fv[s, l] * (x - v[s, l + 1])
                r = r + fl
                flux.append(fl)
            outs.append(r)
        return outs, flux

    zero = jnp.zeros((8, Y), F32)
    sums = [(zero, zero)] * 6
    sub = iota((8, Y), 0)
    start, stop = jnp.where(x == 0, 0, W), jnp.where(x_end, 0, W)

    def add_to(j, a, b):
        p, e = two_prod(a, b)
        s, e2 = two_sum(sums[j][0], p)
        sums[j] = s, sums[j][1] + (e + e2)

    def count(step, old, new):
        for i in range(0, E, 8):
            a, b = old[i : i + 8], new[i : i + 8]
            if i == 0 or i == X:
                keep = sub >= start if i == 0 else sub < stop
                a, b = jnp.where(keep, a, 0.0), jnp.where(keep, b, 0.0)
            add_to(2 * step, a, a)
            add_to(2 * step + 1, a, b)

    def counted(m, h):
        return jnp.where(lane >= W, m, jnp.where(y_end, 0.0, h))

    strip = jnp.zeros((E, Y), F32)
    for step in range(3):
        results, flux = [], None
        head = [jnp.zeros((E, Y), F32)] * 2
        for l in range(LAYERS):
            outs, flux = product(l, flux)
            old, new = (v[0, l], v[1, l]), outs
            count(step, counted(*old), counted(*new))
            here = (lane >= W * l) & (lane < W * l + W) & (y == 0)
            head = [
                jnp.where(here, pltpu.roll(t[0], W * l, 1), h)
                for t, h in zip((old, new), head)
            ]
            results.append(outs)
        count(step, *head)
        if step < 2:
            for l in range(LAYERS):
                m, h = results[l]
                v[0, l], v[1, l] = m, h
                (v1_out, v2_out)[step][l] = m[0:X]
                q, n = (LAYERS + 2 * l, 2) if step else (l, 1)
                back_out[q : q + n, :] = m[X : X + n]
                strip = jnp.where(
                    (lane >= q) & (lane < q + n), pltpu.roll(h, q, 1), strip
                )
    back_out[3 * LAYERS : 3 * LAYERS + 1, :] = east[X - 1 : X, :]
    back_out[16:24, :] = strip[X:E]
    strip_out[...] = jnp.where(lane[0:X] == Y - 1, south[...], strip[0:X])

    ln = iota((8, Y), 1)
    total = zero, zero
    for j in range(6):
        s = fold(sums[j], (4, 2, 1), 0)
        total = tuple(jnp.where(sub == j, a, b) for a, b in zip(s, total))
    total = renorm(*fold(total, (64, 32, 16, 8, 4, 2, 1), 1))
    row = jnp.where(ln == sub, total[0], jnp.where(ln == sub + 8, total[1], 0.0))
    row = jnp.sum(row, axis=0, keepdims=True)
    row_out[...] = jnp.broadcast_to(row, row_out.shape)


def fold(s, steps, dim):
    for by in steps:
        hi, e = two_sum(s[0], pltpu.roll(s[0], by, dim))
        s = hi, s[1] + pltpu.roll(s[1], by, dim) + e
    return s


def rows_total(ref):
    parts = [
        (ref[i : i + 8, :], pltpu.roll(ref[i : i + 8, :], Y - 8, 1))
        for i in range(0, ref.shape[0], 8)
    ]
    while len(parts) > 1:
        parts = [pair_add(a, b) for a, b in zip(parts[::2], parts[1::2])]
    return renorm(*fold(parts[0], (4, 2, 1), 0))


def mend_kernel(edge, strip, west_out):
    row, lane = iota((X, Y), 0), iota((X, Y), 1)
    given = jnp.where(lax.axis_index("gx") == 0, 0, 3 * LAYERS)
    west = jnp.where((row == 0) & (lane < given), edge[16:17, :], strip[...])
    west_out[...] = jnp.where(
        (row == 1) & (lane >= LAYERS) & (lane < given), edge[17:18, :], west
    )


def relay_kernel(rows, row_out):
    hi, lo = rows_total(rows)
    ln = iota((8, Y), 1)
    both = jnp.where(ln < 8, hi, pltpu.roll(lo, 8, 1))
    for i in range(0, row_out.shape[0], 8):
        row_out[i : i + 8, :] = both


def soil_kernel(state, soil_class, land, inverse, base, w):
    w[...] = jnp.zeros(w.shape, F32)
    for e in range(CLASSES):
        x = inverse[e]
        w[0:STATE, 16 * e : 16 * e + 16] = x[:, 0:16]
        w[0:STATE, 192 + 4 * e : 196 + 4 * e] = x[:, 16:STATE]
    w_all = w[...]
    half = (iota((8, Y), 0) >= 4).astype(jnp.int32)
    for x0 in range(0, X, 4):
        fields, spread, kinds = [], [], []
        for x in range(x0, x0 + 4):
            f = state[pl.ds(x, STATE, stride=X), :]
            kind = jnp.where(land[x : x + 1, :] == 1, soil_class[x : x + 1, :], -1)
            twice = jnp.concatenate([f[16:STATE], f[16:STATE]], axis=0)
            parts = [jnp.where(kind == e, f[0:16], 0.0) for e in range(CLASSES)]
            for e in range(0, CLASSES, 2):
                parts.append(jnp.where(kind == e + half, twice, 0.0))
            spread.append(jnp.concatenate(parts, axis=0))
            fields.append(f)
            kinds.append(kind)
        solved = jnp.dot(
            w_all,
            jnp.concatenate(spread, axis=1),
            precision=lax.Precision.HIGHEST,
            preferred_element_type=F32,
        )
        for n in range(4):
            base[pl.ds(x0 + n, STATE, stride=X), :] = jnp.where(
                kinds[n] >= 0, solved[0:STATE, n * Y : n * Y + Y], fields[n]
            )


def unit_kernel(soil_class, land, inverse, water, head, table):
    for e in range(CLASSES):
        x = inverse[e]
        table[0:STATE, e : e + 1] = x[:, 0:1]
        table[PAD : PAD + STATE, e : e + 1] = x[:, 1:2]
    index = soil_class[...]
    half = 0.5 * land[...].astype(F32)
    for i in range(STATE):
        here = slice(i * X, i * X + X)
        water[here, :] = half * pick(table[i : i + 1, :], index)
        head[here, :] = half * pick(table[PAD + i : PAD + i + 1, :], index)


def final_kernel(
    rows, rhs, v1, v2, back, base, water, head, strip, east, south, ponding, land,
    corr_out, pond_out, soil_out,
):
    hi, lo = rows_total(rows)
    mu = [
        tuple(jnp.broadcast_to(t[:, j : j + 1], (8, Y)) for t in (hi, lo))
        for j in range(6)
    ]
    l21 = pair_div(mu[2], mu[1])
    l31 = pair_div(mu[3], mu[1])
    d2 = pair_sub(mu[3], pair_mul(l21, mu[2]))
    u = pair_sub(mu[4], pair_mul(l31, mu[2]))
    l32 = pair_div(u, d2)
    d3 = pair_sub(pair_sub(mu[5], pair_mul(l31, mu[3])), pair_mul(l32, u))
    y2 = pair_sub(mu[1], pair_mul(l21, mu[0]))
    y3 = pair_sub(pair_sub(mu[2], pair_mul(l31, mu[0])), pair_mul(l32, y2))
    c3 = pair_div(y3, d3)
    c2 = pair_sub(pair_div(y2, d2), pair_mul(l32, c3))
    c1 = pair_sub(
        pair_sub(pair_div(mu[0], mu[1]), pair_mul(l21, c2)), pair_mul(l31, c3)
    )
    c1, c2, c3 = (jnp.concatenate([c[0]] * (X // 8), axis=0) for c in (c1, c2, c3))

    row, lane = iota((X, Y), 0), iota((X, Y), 1)
    es, so = east[...], south[...]
    side = strip[...]
    given = jnp.where(lax.axis_index("gx") == 0, 0, 1)
    west = jnp.where(given == 0, 0.0, back[3 * LAYERS : 3 * LAYERS + 1, :])
    north = jnp.where(lax.axis_index("gy") == 0, 0.0, pltpu.roll(side, 1, 1))
    inflow = jnp.where(row == 0, west, pltpu.roll(es, 1, 0)) + jnp.where(
        lane == 0, north, pltpu.roll(so, 1, 1)
    )
    pond = land[...].astype(F32) * (ponding[...] + 0.2 * (inflow - (es + so)))
    pond_out[...] = pond

    lanes = jnp.where(lax.axis_index("gy") == 0, 0, 1)
    top = None
    for l in range(LAYERS):
        q = LAYERS + 2 * l
        a1 = jnp.where(row < given, back[l : l + 1, :], v1[l])
        a2 = jnp.where(row < given, back[q : q + 1, :], v2[l])
        a2 = jnp.where((row == 1) & (given > 0), back[q + 1 : q + 2, :], a2)
        a1 = jnp.where(lane < lanes, pltpu.roll(side, (-l) % Y, 1), a1)
        a2 = jnp.where(lane < 2 * lanes, pltpu.roll(side, (-q) % Y, 1), a2)
        x = c1 * rhs[l] + c2 * a1 + c3 * a2
        corr_out[l] = x
        top = x if top is None else top
    for i in range(STATE):
        here = slice(i * X, i * X + X)
        soil_out[i] = base[here, :] + water[here, :] * pond + head[here, :] * top


def ahead(x, axis):
    n = lax.axis_size(axis)
    return lax.ppermute(x, axis, [(i, (i + 1) % n) for i in range(n)])


def back(x, axis):
    n = lax.axis_size(axis)
    return lax.ppermute(x, axis, [((i + 1) % n, i) for i in range(n)])


def everyones(rows, axis):
    count = lax.axis_size(axis)
    return lax.all_to_all(rows.reshape(count, 1, Y), axis, 0, 0).reshape(count, Y)


def on_device(
    pressure, newton_rhs, geology, saturated_conductivity, genuchten_alpha,
    genuchten_exponent, land_mask, ponding, slope_class, slope_table,
    flow_direction, soil_class, soil_inverse, soil_state,
):
    block, plane, tall = (LAYERS, X, Y), (X, Y), (STATE * X, Y)
    local = (
        pressure, newton_rhs, geology, saturated_conductivity, genuchten_alpha,
        genuchten_exponent, land_mask, ponding, slope_class, slope_table,
        flow_direction, soil_state.reshape(tall),
    )
    cond, diag, slab, east, south, state = call(
        local_kernel,
        [block, block, (FIELDS, E - X, Y), plane, plane, tall],
        [
            (pltpu.SMEM if a.ndim == 1 else pltpu.VMEM)(a.shape, a.dtype)
            for a in local[:-1]
        ]
        + [pltpu.SemaphoreType.DMA((len(local),))],
        [pl.BlockSpec(memory_space=pltpu.HBM)] * len(local),
    )(*(pltpu.with_memory_space_constraint(a, pltpu.HBM) for a in local))
    after = back(slab, "gx")
    (packed,) = call(pack_kernel, [(E, Y)])(newton_rhs, cond, diag, after)
    right = back(packed, "gy")
    water, head = call(unit_kernel, [tall] * 2, [pltpu.VMEM((2 * PAD, Y), F32)])(
        soil_class, land_mask, soil_inverse
    )
    right, water, head = lax.optimization_barrier((right, water, head))
    v1, v2, rows, edge, strip = call(
        krylov_kernel,
        [block, block, (lax.axis_size("gy"), Y), (24, Y), plane],
        [pltpu.VMEM((2, n, E, Y), F32) for n in (5, 5, 4, 5, 5)],
    )(newton_rhs, cond, diag, after, right, east, south)
    edge = ahead(edge, "gx")
    rows = everyones(rows, "gy")
    (rows,) = call(relay_kernel, [(lax.axis_size("gx"), Y)])(rows)
    (strip,) = call(mend_kernel, [plane])(edge, strip)
    strip = ahead(strip, "gy")
    rows, kinds = lax.optimization_barrier((rows, soil_class))
    (base,) = call(
        soil_kernel, [tall], [pltpu.VMEM((PAD, 240), F32)], flops=20_000_000
    )(state, kinds, land_mask, soil_inverse)
    rows = everyones(rows, "gx")
    return call(final_kernel, [block, plane, (STATE, X, Y)])(
        rows, newton_rhs, v1, v2, edge, base, water, head, strip, east, south,
        ponding, land_mask,
    )


def solution(mesh):
    cells, plane, rest = P(None, "gx", "gy"), P("gx", "gy"), P()
    return jax.shard_map(
        on_device,
        mesh=mesh,
        in_specs=(
            cells, cells, cells, rest, rest, rest, plane, plane, plane, rest, plane,
            plane, rest, cells,
        ),
        out_specs=(cells, plane, cells),
        check_vma=False,
    )
```
